32 devices in a mesh: wide: 16 (over z, y, x), narrow: 2 (over core).
Axes of the slice: x: 2, y: 2, z: 4, core: 2. Of those that a mesh axis runs over, the one named last changes fastest.
Arguments:
- tokens: bfloat16 [32768, 512], P('wide', 'narrow'), may hold values from -6 to 6
- encoded: bfloat16 [32768, 512], P('wide', 'narrow'), may hold values from -6 to 6
- cotangent: bfloat16 [32768, 512], P('wide', 'narrow'), may hold values from -6 to 6
- target_lengths: int32 [256, 2], replicated, may hold values from 32 to 96, as said below
- source_segments: int32 [256, 128], replicated, may hold values from 0 to 1, as said below
- send_rows: int32 [16, 16], replicated, may hold values from 0 to 16, as said below
- proj_in: float32 [6, 512, 512], P(None, 'wide', 'narrow'), may hold values from -0.375 to 0.375
- proj_out: float32 [2, 512, 512], P(None, 'narrow', 'wide'), may hold values from -0.75 to 0.75
- ffn_in: float32 [512, 2048], P('wide', 'narrow'), may hold values from -0.25 to 0.25
- ffn_out: float32 [2048, 512], P('narrow', 'wide'), may hold values from -0.125 to 0.125
- norm_par: float32 [6, 512], P(None, 'wide')
- proj_in_moment: float32 [6, 512, 512], P(None, 'wide', 'narrow'), may hold values from -64 to 64
- proj_in_square: float32 [6, 512, 512], P(None, 'wide', 'narrow'), may hold values from 167.1168 to 668.4672
- proj_out_moment: float32 [2, 512, 512], P(None, 'narrow', 'wide'), may hold values from -64 to 64
- proj_out_square: float32 [2, 512, 512], P(None, 'narrow', 'wide'), may hold values from 167.1168 to 668.4672
- ffn_in_moment: float32 [512, 2048], P('wide', 'narrow'), may hold values from -64 to 64
- ffn_in_square: float32 [512, 2048], P('wide', 'narrow'), may hold values from 167.1168 to 668.4672
- ffn_out_moment: float32 [2048, 512], P('narrow', 'wide'), may hold values from -64 to 64
- ffn_out_square: float32 [2048, 512], P('narrow', 'wide'), may hold values from 167.1168 to 668.4672
- norm_moment: float32 [6, 512], P(None, 'wide'), may hold values from -80 to 80
- norm_square: float32 [6, 512], P(None, 'wide'), may hold values from 327.68 to 1310.72
Outputs:
- layer_out: bfloat16 [32768, 512], P('wide', 'narrow')
- tokens_grad: bfloat16 [32768, 512], P('wide', 'narrow')
- encoded_grad: bfloat16 [32768, 512], P('wide', 'narrow')
- proj_in_first: float32 [6, 512, 512], P(None, 'wide', 'narrow')
- proj_in_second: float32 [6, 512, 512], P(None, 'wide', 'narrow')
- proj_in_new: float32 [6, 512, 512], P(None, 'wide', 'narrow')
- proj_out_first: float32 [2, 512, 512], P(None, 'narrow', 'wide')
- proj_out_second: float32 [2, 512, 512], P(None, 'narrow', 'wide')
- proj_out_new: float32 [2, 512, 512], P(None, 'narrow', 'wide')
- ffn_in_first: float32 [512, 2048], P('wide', 'narrow')
- ffn_in_second: float32 [512, 2048], P('wide', 'narrow')
- ffn_in_new: float32 [512, 2048], P('wide', 'narrow')
- ffn_out_first: float32 [2048, 512], P('narrow', 'wide')
- ffn_out_second: float32 [2048, 512], P('narrow', 'wide')
- ffn_out_new: float32 [2048, 512], P('narrow', 'wide')
- norm_first: float32 [6, 512], P(None, 'wide')
- norm_second: float32 [6, 512], P(None, 'wide')
- norm_new: float32 [6, 512], P(None, 'wide')
The draws below stay inside these ranges and needn't reach their ends.
Inputs may be any that keep to these rules, and one draw needn't show every extreme that they name: send_rows[s, d] is the row of sender s (of its 16) that goes to receiver d, or 16 where s sends d nothing. Sender s sends one row to each receiver (s + k) mod 16, for k = 0 .. 15, naming each of its rows once, so that each receiver gets exactly 16 rows. `target_lengths`: each row holds two pairs whose lengths sum to 128; some row has a pair of exactly 96 tokens. `source_segments`: pair 0 takes the first positions of a row and pair 1 the rest; each covers 128 - 96 to 96 positions, and some row has a pair of exactly 96.
All inputs are finite; a program needn't handle non-finite values.
Results may differ from the reference program's by a relative error of at most 0.02.
The reference program's roundings to bfloat16 on the way count: a program that leaves them out, or rounds other values in their place, can miss the bound.
Values may be sent and summed in bfloat16 or wider, within the bound.
No kernel may reach another device: no remote copies, remote signals or barrier semaphores. Data moves between devices by JAX's collectives and lax.ppermute only.
A program may use at most 192 MiB of HBM per device.

```python
import math
import jax
import jax.numpy as jnp
from jax import lax

D = 512
H = 8
FF = 2048
PACK = 128
TGT_MOST = 96
SRC_MOST = 96
STEP = 5
ROWS_DEV = 16
ROWS = 256
TOKENS = 32768


def first_lengths(key, longest):
    key_len, key_row, key_side = jax.random.split(key, 3)
    first = jax.random.randint(key_len, (ROWS,), PACK - longest, longest + 1)
    chosen = jax.random.randint(key_row, (), 0, ROWS)
    side = jax.random.randint(key_side, (), 0, 2)
    forced = jnp.where(side == 0, longest, PACK - longest)
    return jnp.where(jnp.arange(ROWS) == chosen, forced, first).astype(jnp.int32)


def draw_target_lengths(key, part):
    key = jax.random.fold_in(key, 5)
    first = first_lengths(key, TGT_MOST)
    return jnp.stack([first, PACK - first], 1).astype(jnp.int32)


def draw_source_segments(key, part):
    key = jax.random.fold_in(key, 9)
    first = first_lengths(key, SRC_MOST)
    positions = jnp.arange(PACK, dtype=jnp.int32)
    return (positions[None, :] >= first[:, None]).astype(jnp.int32)


def draw_send_rows(key, part):
    key = jax.random.fold_in(key, 11)
    peers = ROWS // ROWS_DEV
    stride = peers // ROWS_DEV
    row_keys = jax.random.split(key, peers)
    local_rows = jax.vmap(lambda single: jax.random.permutation(single, ROWS_DEV))(row_keys)
    senders = jnp.arange(peers, dtype=jnp.int32)[:, None]
    receivers = (senders + jnp.arange(ROWS_DEV, dtype=jnp.int32)[None, :] * stride) % peers
    table = jnp.full((peers, peers), ROWS_DEV, jnp.int32)
    table = table.at[senders, receivers].set(local_rows.astype(jnp.int32))
    return table.astype(jnp.int32)


def draw_norm_par(key, part):
    key = jax.random.fold_in(key, 7)
    key_gain, key_bias = jax.random.split(key)
    gains = jax.random.uniform(key_gain, (3, D), jnp.float32, 0.5, 1.5)
    biases = 0.3 * jnp.clip(jax.random.normal(key_bias, (3, D), jnp.float32), -3.0, 3.0)
    return jnp.concatenate([gains, biases], 0).astype(jnp.float32)


def block_levels(rng, dims, cuts, smallest, high):
    level, own = 1.0, jax.random.fold_in(rng, 6)
    for axis_at, parts in cuts:
        heights = jnp.exp(jax.random.uniform(jax.random.fold_in(own, axis_at), (parts,), jnp.float32, smallest / len(cuts), high / len(cuts)))
        level = level * jnp.repeat(heights, dims[axis_at] // parts).reshape([-1 if axis == axis_at else 1 for axis in range(len(dims))])
    return level


def gaussian(stream_key, dims, scale, bound, cuts=(), kind=jnp.bfloat16):
    values = jax.random.normal(stream_key, dims, jnp.float32) * scale
    if len(cuts) > 0:
        values = block_levels(stream_key, dims, cuts, -0.22, 0.18) * values
    return jnp.clip(values, min=-bound, max=bound).astype(kind)


def setup_inputs(seed: int = 0) -> dict:
    arg_keys = jax.random.split(jax.random.key(seed), 22)
    return {
        "tokens": gaussian(arg_keys[0], (TOKENS, D), 1.0, 6.0, ((0, 16), (1, 2))),
        "encoded": gaussian(arg_keys[1], (TOKENS, D), 1.0, 6.0, ((0, 16), (1, 2))),
        "cotangent": gaussian(arg_keys[2], (TOKENS, D), 1.0, 6.0, ((0, 16), (1, 2))),
        "target_lengths": draw_target_lengths(jax.random.fold_in(arg_keys[21], 71), 0),
        "source_segments": draw_source_segments(jax.random.fold_in(arg_keys[21], 71), 0),
        "send_rows": draw_send_rows(jax.random.fold_in(arg_keys[21], 71), 0),
        "proj_in": gaussian(arg_keys[6], (6, D, D), (D // 2) ** -0.5, 0.375, ((1, 16), (2, 2)), jnp.float32),
        "proj_out": gaussian(arg_keys[7], (2, D, D), (D // 8) ** -0.5, 0.75, ((1, 2), (2, 16)), jnp.float32),
        "ffn_in": gaussian(arg_keys[8], (D, FF), D ** -0.5, 0.25, ((0, 16), (1, 2)), jnp.float32),
        "ffn_out": gaussian(arg_keys[9], (FF, D), FF ** -0.5, 0.125, ((0, 2), (1, 16)), jnp.float32),
        "norm_par": draw_norm_par(jax.random.fold_in(arg_keys[21], 71), 0),
        "proj_in_moment": gaussian(arg_keys[11], (6, D, D), (0.055 * (ROWS * PACK) ** 0.5), 64.0, ((1, 16), (2, 2)), jnp.float32),
        "proj_in_square": jnp.clip(jnp.exp(math.log(668.4672) - 1.3862944 * jax.random.uniform(arg_keys[12], (6, D, D), jnp.float32) ** block_levels(arg_keys[12], (6, D, D), ((1, 16), (2, 2)), -0.2, 0.2)), 167.1168, 668.4672),
        "proj_out_moment": gaussian(arg_keys[13], (2, D, D), (0.055 * (ROWS * PACK) ** 0.5), 64.0, ((1, 2), (2, 16)), jnp.float32),
        "proj_out_square": jnp.clip(jnp.exp(math.log(668.4672) - 1.3862944 * jax.random.uniform(arg_keys[14], (2, D, D), jnp.float32) ** block_levels(arg_keys[14], (2, D, D), ((1, 2), (2, 16)), -0.2, 0.2)), 167.1168, 668.4672),
        "ffn_in_moment": gaussian(arg_keys[15], (D, FF), (0.055 * (ROWS * PACK) ** 0.5), 64.0, ((0, 16), (1, 2)), jnp.float32),
        "ffn_in_square": jnp.clip(jnp.exp(math.log(668.4672) - 1.3862944 * jax.random.uniform(arg_keys[16], (D, FF), jnp.float32) ** block_levels(arg_keys[16], (D, FF), ((0, 16), (1, 2)), -0.2, 0.2)), 167.1168, 668.4672),
        "ffn_out_moment": gaussian(arg_keys[17], (FF, D), (0.055 * (ROWS * PACK) ** 0.5), 64.0, ((0, 2), (1, 16)), jnp.float32),
        "ffn_out_square": jnp.clip(jnp.exp(math.log(668.4672) - 1.3862944 * jax.random.uniform(arg_keys[18], (FF, D), jnp.float32) ** block_levels(arg_keys[18], (FF, D), ((0, 2), (1, 16)), -0.2, 0.2)), 167.1168, 668.4672),
        "norm_moment": gaussian(arg_keys[19], (6, D), (0.08 * (ROWS * PACK) ** 0.5), 80.0, ((1, 16),), jnp.float32),
        "norm_square": jnp.clip(jnp.exp(math.log(1310.72) - 1.3862944 * jax.random.uniform(arg_keys[20], (6, D), jnp.float32) ** block_levels(arg_keys[20], (6, D), ((1, 16),), -0.2, 0.2)), 327.68, 1310.72),
    }


@jax.custom_vjp
def low(v):
    return lax.optimization_barrier(v.astype(jnp.bfloat16)).astype(jnp.float32)

@jax.custom_vjp
def low_back(v):
    return v

def low_keep(v):
    return (low(v), None)

def low_pass(kept, grad):
    return (grad,)

def back_keep(v):
    return (v, None)

def back_low(kept, grad):
    return (low(grad),)
low.defvjp(low_keep, low_pass)
low_back.defvjp(back_keep, back_low)
norm_epsilon = 1e-05
beta_first = 0.9
beta_second = 0.98
adam_epsilon = 1e-08
rate_matrix = 0.1
rate_norm = 0.5
decay_matrix = 0.01
masked_score = -1e+30
highest = lax.Precision.HIGHEST

def round_both(value):
    return low(low_back(value))

def project(inputs, weight):
    return jnp.einsum('gpd,de->gpe', inputs, weight, precision=highest)

def layer_norm(resid, gain, shift):
    center = resid - lax.optimization_barrier(jnp.mean(resid, -1, keepdims=True))
    return center * lax.rsqrt(lax.optimization_barrier(jnp.mean(center * center, -1, keepdims=True)) + norm_epsilon) * gain + shift

def attention(queries_in, keys_in, w_query, w_key, w_value, w_output, allowed):
    head_size = D // H
    query = round_both(project(queries_in, w_query))
    keys = round_both(project(keys_in, w_key))
    values = round_both(project(keys_in, w_value))
    groups = query.shape[0]
    length = query.shape[1]
    q_heads = query.reshape(groups, length, H, head_size)
    k_heads = keys.reshape(groups, keys.shape[1], H, head_size)
    v_heads = values.reshape(groups, keys.shape[1], H, head_size)
    scores = jnp.einsum('gqhe,gkhe->ghqk', q_heads, k_heads, precision=highest) * head_size ** (-0.5)
    scores = low_back(jnp.where(allowed[:, None], scores, masked_score))
    peak = lax.optimization_barrier(jnp.max(scores, -1, keepdims=True))
    exponent = jnp.exp(scores - peak)
    probs = low(exponent / lax.optimization_barrier(jnp.sum(exponent, -1, keepdims=True)))
    mixed = jnp.einsum('ghqk,gkhe->gqhe', probs, v_heads, precision=highest).reshape(groups, length, D)
    return low_back(project(round_both(mixed), w_output))

def layer(params, x_rows, enc_rows, tgt_seg, src_seg):
    proj_in, proj_out, ffn_in, ffn_out, norm_par = params
    self_mask = tgt_seg[:, :, None] == tgt_seg[:, None, :]
    cross_mask = tgt_seg[:, :, None] == src_seg[:, None, :]
    resid_one = x_rows + attention(x_rows, x_rows, proj_in[0], proj_in[1], proj_in[2], proj_out[0], self_mask)
    hidden_one = layer_norm(resid_one, norm_par[0], norm_par[3])
    resid_two = hidden_one + attention(low(hidden_one), enc_rows, proj_in[3], proj_in[4], proj_in[5], proj_out[1], cross_mask)
    hidden_two = layer_norm(resid_two, norm_par[1], norm_par[4])
    pre_act = low_back(project(low(hidden_two), ffn_in))
    resid_three = hidden_two + low_back(project(low(jax.nn.gelu(pre_act)), ffn_out))
    return layer_norm(resid_three, norm_par[2], norm_par[5])

def adam(weight, first_old, second_old, grad, rate, decay):
    first_new = beta_first * first_old + (1.0 - beta_first) * grad
    second_new = beta_second * second_old + (1.0 - beta_second) * grad * grad
    first_hat = first_new / (1.0 - beta_first ** STEP)
    second_hat = second_new / (1.0 - beta_second ** STEP)
    updated = weight - rate * (first_hat / (jnp.sqrt(second_hat) + adam_epsilon) + decay * weight)
    return (first_new, second_new, updated)

def reference(tokens, encoded, cotangent, target_lengths, source_segments, send_rows, proj_in, proj_out, ffn_in, ffn_out, norm_par, proj_in_moment, proj_in_square, proj_out_moment, proj_out_square, ffn_in_moment, ffn_in_square, ffn_out_moment, ffn_out_square, norm_moment, norm_square):
    peers = ROWS // ROWS_DEV
    live = send_rows < ROWS_DEV
    rank = jnp.cumsum(live.astype(jnp.int32), axis=0) - 1
    senders = jnp.arange(peers, dtype=jnp.int32)[:, None]
    receivers = jnp.arange(peers, dtype=jnp.int32)[None, :]
    target = jnp.where(live, receivers * ROWS_DEV + rank, ROWS).astype(jnp.int32)
    anchor = (senders * ROWS_DEV + send_rows).astype(jnp.int32)
    order = jnp.zeros((ROWS,), jnp.int32).at[target.reshape(-1)].set(anchor.reshape(-1), mode='drop')
    positions = jnp.arange(PACK, dtype=jnp.int32)
    ends = jnp.cumsum(target_lengths, -1)
    tgt_all = lax.optimization_barrier(jnp.sum((ends[:, None, :] <= positions[None, :, None]).astype(jnp.int32), -1))
    tgt_seg = tgt_all[order]
    src_seg = source_segments[order]
    x_rows = tokens.astype(jnp.float32).reshape(ROWS, PACK, D)[order]
    enc_rows = encoded.astype(jnp.float32).reshape(ROWS, PACK, D)[order]
    cot_rows = cotangent.astype(jnp.float32).reshape(ROWS, PACK, D)
    group = min(ROWS, max(1, 4096 // PACK))
    count = ROWS // group

    def regroup(array):
        return array.reshape((count, group) + array.shape[1:])
    checked = jax.checkpoint(layer)
    params = (proj_in, proj_out, ffn_in, ffn_out, norm_par)

    def forward(weights, x_all, enc_all):
        lowered = jax.tree.map(low, weights)

        def advance(carry, pieces):
            return (carry, checked(lowered, pieces[0], pieces[1], pieces[2], pieces[3]))
        carry_out, outputs = lax.scan(advance, jnp.zeros((), jnp.float32), (regroup(x_all), regroup(enc_all), regroup(tgt_seg), regroup(src_seg)))
        return outputs.reshape(ROWS, PACK, D)
    result, pullback = jax.vjp(forward, params, x_rows, enc_rows)
    grads, d_rows, d_enc = pullback(cot_rows)
    tokens_grad = jnp.zeros_like(d_rows).at[order].set(d_rows).reshape(TOKENS, D).astype(jnp.bfloat16)
    encoded_grad = jnp.zeros_like(d_enc).at[order].set(d_enc).reshape(TOKENS, D).astype(jnp.bfloat16)
    layer_out = result.reshape(TOKENS, D).astype(jnp.bfloat16)
    pin = adam(proj_in, proj_in_moment, proj_in_square, grads[0], rate_matrix, decay_matrix)
    pout = adam(proj_out, proj_out_moment, proj_out_square, grads[1], rate_matrix, decay_matrix)
    fin = adam(ffn_in, ffn_in_moment, ffn_in_square, grads[2], rate_matrix, decay_matrix)
    fout = adam(ffn_out, ffn_out_moment, ffn_out_square, grads[3], rate_matrix, decay_matrix)
    norms = adam(norm_par, norm_moment, norm_square, grads[4], rate_norm, 0.0)
    return (layer_out, tokens_grad, encoded_grad, pin[0], pin[1], pin[2], pout[0], pout[1], pout[2], fin[0], fin[1], fin[2], fout[0], fout[1], fout[2], norms[0], norms[1], norms[2])
```

```python
import functools
import math

import jax
import jax.numpy as jnp
from jax import lax
from jax.experimental import pallas as pl
from jax.experimental.pallas import tpu as pltpu
from jax.sharding import PartitionSpec as P

D = 512
H = 8
HD = D // H
PACK = 128
STEP = 5
CH = 32
HALF = D // 2
PIECES = D // CH
SLOTS = 8
TOK = SLOTS * PACK
BLK = 256
GRID = TOK // BLK
PER = BLK // PACK

norm_epsilon = 1e-05
beta_first = 0.9
beta_second = 0.98
adam_epsilon = 1e-08
rate_matrix = 0.1
rate_norm = 0.5
decay_matrix = 0.01
masked_score = -1e30

CORE = 0
PIECE = 1
ROW = PIECE + PIECES
FIRST = ROW + 2 * SLOTS
SECOND = FIRST + SLOTS
GLOBAL = SECOND + SLOTS

BF = jnp.bfloat16
F32 = jnp.float32


def dot(a, b):
    return jnp.dot(a, b, preferred_element_type=F32)


def dot_nt(a, b):
    return lax.dot_general(a, b, (((1,), (1,)), ((), ())), preferred_element_type=F32)


def dot_tn(a, b):
    return lax.dot_general(a, b, (((0,), (0,)), ((), ())), preferred_element_type=F32)


def sds(shape, dtype=BF):
    return jax.ShapeDtypeStruct(shape, dtype)


def call(body, grid, in_specs, out_specs, out_shape, scratch=(), flops=0, nbytes=0, prefetch=1):
    return pl.pallas_call(
        body,
        grid_spec=pltpu.PrefetchScalarGridSpec(
            num_scalar_prefetch=prefetch,
            grid=grid,
            in_specs=in_specs,
            out_specs=out_specs,
            scratch_shapes=list(scratch),
        ),
        out_shape=out_shape,
        cost_estimate=pl.CostEstimate(flops=flops, bytes_accessed=nbytes, transcendentals=0),
        compiler_params=pltpu.CompilerParams(
            vmem_limit_bytes=56 * 1024 * 1024, dimension_semantics=("arbitrary",) * len(grid)
        ),
    )


ANY = pl.BlockSpec(memory_space=pl.ANY)


def rows_spec(width, rows=BLK):
    return pl.BlockSpec((rows, width), lambda i, meta: (i, 0))


def fixed_spec(shape):
    return pl.BlockSpec(shape, lambda i, meta: (0,) * len(shape))


def slot_spec(k):
    return pl.BlockSpec((PACK, HALF), lambda i, meta: (meta[ROW + PER * i + k], 0))


def pack_body(pin, pout, win, wout, norm, g0, g1, g2):
    eye = (
        lax.broadcasted_iota(jnp.int32, (CH, CH), 0) == lax.broadcasted_iota(jnp.int32, (CH, CH), 1)
    ).astype(BF)
    wide = (
        lax.broadcasted_iota(jnp.int32, (CH, HALF), 1) % CH
        == lax.broadcasted_iota(jnp.int32, (CH, HALF), 0)
    ).astype(BF)
    place = (
        lax.broadcasted_iota(jnp.int32, (CH, 6), 0) == lax.broadcasted_iota(jnp.int32, (CH, 6), 1)
    ).astype(BF)
    for m in range(3):
        g0[m] = pin[m].astype(BF)
        g1[1 + m] = pin[3 + m].astype(BF)
    g1[0] = dot_nt(eye, pout[0].astype(BF)).astype(BF)
    g1[4] = dot(dot(place, norm[...].astype(BF)).astype(BF), wide).astype(BF)
    g2[0] = dot_nt(eye, pout[1].astype(BF)).astype(BF)
    blocks = win.shape[1] // HALF
    for b in range(blocks):
        g2[1 + b] = win[:, b * HALF : (b + 1) * HALF].astype(BF)
        g2[1 + blocks + b] = dot_nt(eye, wout[b * HALF : (b + 1) * HALF, :].astype(BF)).astype(BF)


def pack(pin, pout, win, wout, norm):
    blocks = win.shape[1] // HALF
    counts = (3, 5, 1 + 2 * blocks)
    return pl.pallas_call(
        pack_body,
        out_shape=tuple(sds((c, CH, HALF)) for c in counts),
        compiler_params=pltpu.CompilerParams(vmem_limit_bytes=56 * 1024 * 1024),
        cost_estimate=pl.CostEstimate(flops=10**6, bytes_accessed=6 * 10**6, transcendentals=0),
    )(pin, pout, win, wout, norm)


def load_weights(meta, pieces, w_ref, sems):
    copies = []
    for a, piece in enumerate(pieces):
        half, group = divmod(a, len(pieces) // 2)
        per = piece.shape[0]
        for j in range(per):
            row = pl.multiple_of(meta[PIECE + group * per + j] * CH, CH)
            copies.append(
                pltpu.make_async_copy(
                    piece.at[j],
                    w_ref.at[:, pl.ds(row, CH), pl.ds(half * HALF, HALF)],
                    sems.at[a],
                )
            )
    for c in copies:
        c.start()
    return copies


def lane_masks():
    low = lax.broadcasted_iota(jnp.int32, (1, PACK), 1) < HD
    return low.astype(F32).astype(BF), (1.0 - low.astype(F32)).astype(BF)


def low_lanes():
    return lax.broadcasted_iota(jnp.int32, (PACK, PACK), 1) < HD


def pair_forward(q, k, v, mask2, low, high, pick):
    scale = HD**-0.5
    qs = jnp.concatenate([q * (low * scale), q * (high * scale)], 0)
    s = jnp.where(mask2, dot_nt(qs, k), masked_score)
    e = jnp.exp(s - jnp.max(s, -1, keepdims=True))
    p = (e * (1.0 / jnp.sum(e, -1, keepdims=True))).astype(BF)
    r = dot(p, v)
    return p, jnp.where(pick, r[:PACK], r[PACK:]).astype(BF)


def pair_backward(q, k, v, p, dm, low, high, pick):
    scale = HD**-0.5
    qs = jnp.concatenate([q * (low * scale), q * (high * scale)], 0)
    dms = jnp.concatenate([dm * low, dm * high], 0)
    dp = dot_nt(dms, v)
    pf = p.astype(F32)
    ds = (pf * (dp - jnp.sum(pf * dp, -1, keepdims=True))).astype(BF)
    r = dot(ds, k)
    dq = (jnp.where(pick, r[:PACK], r[PACK:]) * scale).astype(BF)
    return dq, dot_tn(ds, qs).astype(BF), dot_tn(p, dms).astype(BF)


def norm_forward(r):
    center = r - jnp.mean(r, -1, keepdims=True)
    rstd = lax.rsqrt(jnp.mean(center * center, -1, keepdims=True) + norm_epsilon)
    return center * rstd, rstd


def norm_backward(dy, n, rstd, gain):
    dn = dy * gain
    dr = rstd * (dn - jnp.mean(dn, -1, keepdims=True) - n * jnp.mean(dn * n, -1, keepdims=True))
    return dr, jnp.sum(dy * n, 0, keepdims=True), jnp.sum(dy, 0, keepdims=True)


def segments(meta, slot, dim):
    at = lax.broadcasted_iota(jnp.int32, (PACK, PACK), dim)
    one = (at >= meta[FIRST + slot]).astype(jnp.int32)
    return one + (at >= meta[SECOND + slot]).astype(jnp.int32)


def natural(meta, own, other):
    first = meta[CORE] == 0
    return jnp.concatenate([jnp.where(first, own, other), jnp.where(first, other, own)], 1)


def halves(meta, full):
    first = meta[CORE] == 0
    lo, hi = full[:, :HALF], full[:, HALF:]
    return jnp.where(first, lo, hi), jnp.where(first, hi, lo)


def self_forward_body(*refs):
    meta, own0, oth0, own1, oth1 = refs[:5]
    pieces = refs[5:13]
    x_ref, q_ref, k_ref, v_ref, m_ref, p_ref, w_ref, sems = refs[13:]
    i = pl.program_id(0)

    @pl.when(i == 0)
    def _():
        for c in load_weights(meta, pieces, w_ref, sems):
            c.wait()

    x = jnp.concatenate(
        [natural(meta, own0[...], oth0[...]), natural(meta, own1[...], oth1[...])], 0
    )
    x_ref[...] = x
    q_ref[...] = dot(x, w_ref[0]).astype(BF)
    k_ref[...] = dot(x, w_ref[1]).astype(BF)
    v_ref[...] = dot(x, w_ref[2]).astype(BF)
    low, high = lane_masks()
    pick = low_lanes()
    for s in range(PER):
        slot = PER * i + s
        mask = segments(meta, slot, 0) == segments(meta, slot, 1)
        mask2 = jnp.concatenate([mask, mask], 0)
        rows = slice(s * PACK, (s + 1) * PACK)
        for h in range(H // 2):
            cols = slice(h * PACK, (h + 1) * PACK)
            p, m = pair_forward(
                q_ref[rows, cols], k_ref[rows, cols], v_ref[rows, cols], mask2, low, high, pick
            )
            p_ref[s * (H // 2) + h] = p
            m_ref[rows, cols] = m


def self_forward(meta, tok_own, tok_oth, pieces):
    full = rows_spec(D)
    p_spec = pl.BlockSpec((PER * H // 2, 2 * PACK, PACK), lambda i, meta: (i, 0, 0))
    return call(
        self_forward_body,
        (GRID,),
        [slot_spec(0), slot_spec(0), slot_spec(1), slot_spec(1)] + [ANY] * 8,
        (full, full, full, full, full, p_spec, fixed_spec((3, D, D))),
        (
            (sds((TOK, D)),) * 5
            + (sds((SLOTS * H // 2, 2 * PACK, PACK)), sds((3, D, D)))
        ),
        [pltpu.SemaphoreType.DMA((8,))],
        flops=2 * TOK * D * D * 4,
        nbytes=10 * 2**20,
    )(meta, tok_own, tok_oth, tok_own, tok_oth, *pieces)


def cross_forward_body(*refs):
    meta, x_ref, m_in, own0, oth0, own1, oth1, seg0, seg1 = refs[:9]
    pieces = refs[9:17]
    (n_ref, r_ref, h_ref, e_ref, q_ref, k_ref, v_ref, m_ref, p_ref, w_ref, norm_ref, sems) = refs[17:]
    i = pl.program_id(0)

    @pl.when(i == 0)
    def _():
        for c in load_weights(meta, pieces, w_ref, sems):
            c.wait()
        lane = lax.broadcasted_iota(jnp.int32, (8, HALF), 1) // CH
        for half in range(2):
            total = jnp.zeros((8, HALF), F32)
            for j in range(PIECES // 2):
                at = (half * (PIECES // 2) + j) * CH
                part = w_ref[4, at : at + 16, :HALF][:8].astype(F32)
                total = total + jnp.where(lane == j, part, 0.0)
            norm_ref[:, half * HALF : (half + 1) * HALF] = total

    n, rstd = norm_forward(x_ref[...].astype(F32) + dot_nt(m_in[...], w_ref[0]))
    n_ref[...] = n
    r_ref[...] = jnp.broadcast_to(rstd, (BLK, PACK))
    h = (n * norm_ref[0:1, :] + norm_ref[3:4, :]).astype(BF)
    h_ref[...] = h
    enc = jnp.concatenate(
        [natural(meta, own0[...], oth0[...]), natural(meta, own1[...], oth1[...])], 0
    )
    e_ref[...] = enc
    q_ref[...] = dot(h, w_ref[1]).astype(BF)
    k_ref[...] = dot(enc, w_ref[2]).astype(BF)
    v_ref[...] = dot(enc, w_ref[3]).astype(BF)
    low, high = lane_masks()
    pick = low_lanes()
    for s, seg in enumerate((seg0, seg1)):
        mask = segments(meta, PER * i + s, 0) == seg[0]
        mask2 = jnp.concatenate([mask, mask], 0)
        rows = slice(s * PACK, (s + 1) * PACK)
        for h_at in range(H // 2):
            cols = slice(h_at * PACK, (h_at + 1) * PACK)
            p, m = pair_forward(
                q_ref[rows, cols], k_ref[rows, cols], v_ref[rows, cols], mask2, low, high, pick
            )
            p_ref[s * (H // 2) + h_at] = p
            m_ref[rows, cols] = m


def cross_forward(meta, x, m, enc_own, enc_oth, segs, pieces):
    full = rows_spec(D)
    p_spec = pl.BlockSpec((PER * H // 2, 2 * PACK, PACK), lambda i, meta: (i, 0, 0))

    def seg_spec(k):
        return pl.BlockSpec((1, 1, PACK), lambda i, meta: (meta[GLOBAL + PER * i + k], 0, 0))

    return call(
        cross_forward_body,
        (GRID,),
        [full, full, slot_spec(0), slot_spec(0), slot_spec(1), slot_spec(1), seg_spec(0), seg_spec(1)]
        + [ANY] * 8,
        (full, rows_spec(PACK), full, full, full, full, full, full, p_spec)
        + (fixed_spec((5, D, D)), fixed_spec((8, D))),
        (sds((TOK, D), F32), sds((TOK, PACK), F32))
        + (sds((TOK, D)),) * 6
        + (sds((SLOTS * H // 2, 2 * PACK, PACK)), sds((5, D, D)), sds((8, D), F32)),
        [pltpu.SemaphoreType.DMA((8,))],
        flops=2 * TOK * D * D * 5,
        nbytes=16 * 2**20,
    )(meta, x, m, enc_own, enc_oth, enc_own, enc_oth, segs, segs, *pieces)


def gelu_both(v):
    c = math.sqrt(2.0 / math.pi)
    v2 = v * v
    t = jnp.tanh(c * (v + 0.044715 * (v * v2)))
    cdf = 0.5 + 0.5 * t
    return v * cdf, cdf + (0.5 * v) * (1.0 - t * t) * (c + (3.0 * 0.044715 * c) * v2)


def ffn_body(*refs):
    meta, n_in, m_in, norm, cot_own, cot_oth = refs[:6]
    pieces = refs[6:14]
    out_own, out_oth, dr_ref, po_ref, g_own, g_oth, ng_ref = refs[14:21]
    w_ref, act_ref, pre_ref, slope_ref, df_t, h_t, sems = refs[21:]
    i = pl.program_id(0)
    blocks = (w_ref.shape[0] - 1) // 2

    @pl.when(i == 0)
    def _():
        for c in load_weights(meta, pieces, w_ref, sems):
            c.wait()
        po_ref[...] = w_ref[0]
        ng_ref[...] = jnp.zeros_like(ng_ref)

    at = pl.multiple_of(i * BLK, BLK)
    here = pl.ds(at, BLK)
    h1 = n_in[...] * norm[0:1, :] + norm[3:4, :]
    n2, rstd2 = norm_forward(h1 + dot_nt(m_in[...], w_ref[0]))
    h2 = n2 * norm[1:2, :] + norm[4:5, :]
    h2b = h2.astype(BF)
    h_t[:, here] = h2b.T
    r3 = h2
    for b in range(blocks):
        act, slope = gelu_both(dot(h2b, w_ref[1 + b]))
        act = act.astype(BF)
        act_ref[b, here, :] = act
        slope_ref[b] = slope
        r3 = r3 + dot_nt(act, w_ref[1 + blocks + b])
    n3, rstd3 = norm_forward(r3)
    result = n3 * norm[2:3, :] + norm[5:6, :]
    own, oth = halves(meta, result.astype(BF))
    out_own[...] = own
    out_oth[...] = oth
    dy = natural(meta, cot_own[...], cot_oth[...]).astype(F32)
    dr3, gain3, bias3 = norm_backward(dy, n3, rstd3, norm[2:3, :])
    df = dr3.astype(BF)
    df_t[:, here] = df.T
    dh2 = dr3
    for b in range(blocks):
        dpre = (dot(df, w_ref[1 + blocks + b]) * slope_ref[b]).astype(BF)
        pre_ref[b, here, :] = dpre
        dh2 = dh2 + dot_nt(dpre, w_ref[1 + b])
    dr2, gain2, bias2 = norm_backward(dh2, n2, rstd2, norm[1:2, :])
    dr_ref[...] = dr2
    ng_ref[1:2, :] += gain2
    ng_ref[2:3, :] += gain3
    ng_ref[4:5, :] += bias2
    ng_ref[5:6, :] += bias3

    @pl.when(i == GRID - 1)
    def _():
        for b in range(blocks):
            put_grad(g_own, g_oth, b, dot(h_t[...], pre_ref[b]))
            put_grad(g_own, g_oth, blocks + b, dot(df_t[...], act_ref[b]))


def put_grad(g_own, g_oth, m, value):
    value = value.astype(BF)
    g_own[:, m] = value[:, :HALF].reshape(PIECES, CH, HALF)
    g_oth[:, m] = value[:, HALF:].reshape(PIECES, CH, HALF)


def ffn(meta, n1, m2, norm, cot_own, cot_oth, pieces):
    mats = pieces[0].shape[1]
    blocks = (mats - 1) // 2
    full = rows_spec(D)
    half = rows_spec(HALF)
    cot = pl.BlockSpec((BLK, HALF), lambda i, meta: (meta[CORE] * GRID + i, 0))
    grad = (PIECES, 2 * blocks, CH, HALF)
    return call(
        ffn_body,
        (GRID,),
        [full, full, fixed_spec((8, D)), cot, cot] + [ANY] * 8,
        (half, half, full, fixed_spec((D, D)), fixed_spec(grad), fixed_spec(grad), fixed_spec((8, D))),
        (sds((TOK, HALF)),) * 2
        + (sds((TOK, D), F32), sds((D, D)), sds(grad), sds(grad), sds((8, D), F32)),
        [
            pltpu.VMEM((mats, D, D), BF),
            pltpu.VMEM((blocks, TOK, D), BF),
            pltpu.VMEM((blocks, TOK, D), BF),
            pltpu.VMEM((blocks, BLK, D), F32),
            pltpu.VMEM((D, TOK), BF),
            pltpu.VMEM((D, TOK), BF),
            pltpu.SemaphoreType.DMA((8,)),
        ],
        flops=2 * TOK * D * D * (1 + 6 * blocks),
        nbytes=20 * 2**20,
    )(meta, n1, m2, norm, cot_own, cot_oth, *pieces)


def cross_backward_body(*refs):
    (meta, dr_in, m_in, p_in, q_in, k_in, v_in, e_in, h_in, n_in, r_in, norm, ng_in, w_ref, po_ref) = refs[:15]
    dr_ref, dk_ref, dv_ref, g_own, g_oth, ng_ref = refs[15:21]
    da_t, h_t, e_t, m_all, dq_all, dk_all, dv_all, dm_ref = refs[21:]
    i = pl.program_id(0)

    @pl.when(i == 0)
    def _():
        ng_ref[...] = ng_in[...]

    here = pl.ds(pl.multiple_of(i * BLK, BLK), BLK)
    dr2 = dr_in[...]
    da = dr2.astype(BF)
    da_t[:, here] = da.T
    h_t[:, here] = h_in[...].T
    e_t[:, here] = e_in[...].T
    m_all[here, :] = m_in[...]
    dm_ref[...] = dot(da, po_ref[...]).astype(BF)
    low, high = lane_masks()
    pick = low_lanes()
    for s in range(PER):
        rows = slice(s * PACK, (s + 1) * PACK)
        there = pl.ds(pl.multiple_of(i * BLK + s * PACK, PACK), PACK)
        for h in range(H // 2):
            cols = slice(h * PACK, (h + 1) * PACK)
            dq, dk, dv = pair_backward(
                q_in[rows, cols], k_in[rows, cols], v_in[rows, cols],
                p_in[s * (H // 2) + h], dm_ref[rows, cols], low, high, pick,
            )
            dq_all[there, cols] = dq
            dk_all[there, cols] = dk
            dv_all[there, cols] = dv
    dk_ref[...] = dk_all[here, :]
    dv_ref[...] = dv_all[here, :]
    dh1 = dr2 + dot_nt(dq_all[here, :], w_ref[1])
    dr1, gain1, bias1 = norm_backward(dh1, n_in[...], r_in[:, 0:1], norm[0:1, :])
    dr_ref[...] = dr1
    ng_ref[0:1, :] += gain1
    ng_ref[3:4, :] += bias1

    @pl.when(i == GRID - 1)
    def _():
        put_grad(g_own, g_oth, 0, dot(da_t[...], m_all[...]))
        put_grad(g_own, g_oth, 1, dot(h_t[...], dq_all[...]))
        put_grad(g_own, g_oth, 2, dot(e_t[...], dk_all[...]))
        put_grad(g_own, g_oth, 3, dot(e_t[...], dv_all[...]))
        total = jnp.concatenate([ng_ref[...], jnp.zeros((CH - 8, D), F32)], 0).astype(BF)
        for c in range(PIECES):
            part = total[:, :HALF] if c < PIECES // 2 else total[:, HALF:]
            g_own[c, 4] = part
            g_oth[c, 4] = part


def cross_backward(meta, dr2, m2, p2, q2, k2, v2, enc, h1, n1, rstd1, norm, ng, w, po):
    full = rows_spec(D)
    p_spec = pl.BlockSpec((PER * H // 2, 2 * PACK, PACK), lambda i, meta: (i, 0, 0))
    grad = (PIECES, 5, CH, HALF)
    small = fixed_spec((8, D))
    return call(
        cross_backward_body,
        (GRID,),
        [full, full, p_spec, full, full, full, full, full, full, rows_spec(PACK), small, small]
        + [fixed_spec((5, D, D)), fixed_spec((D, D))],
        (full, full, full, fixed_spec(grad), fixed_spec(grad), small),
        (sds((TOK, D), F32), sds((TOK, D)), sds((TOK, D)), sds(grad), sds(grad), sds((8, D), F32)),
        [pltpu.VMEM((D, TOK), BF)] * 3
        + [pltpu.VMEM((TOK, D), BF)] * 4
        + [pltpu.VMEM((BLK, D), BF)],
        flops=2 * TOK * D * D * 8,
        nbytes=20 * 2**20,
    )(meta, dr2, m2, p2, q2, k2, v2, enc, h1, n1, rstd1, norm, ng, w, po)


def self_backward_body(*refs):
    (meta, dr_in, m_in, p_in, q_in, k_in, v_in, x_in, po_ref) = refs[:9]
    dq_ref, dk_ref, dv_ref, g_own, g_oth = refs[9:14]
    da_t, x_t, m_all, dq_all, dk_all, dv_all, dm_ref = refs[14:]
    i = pl.program_id(0)
    here = pl.ds(pl.multiple_of(i * BLK, BLK), BLK)
    da = dr_in[...].astype(BF)
    da_t[:, here] = da.T
    x_t[:, here] = x_in[...].T
    m_all[here, :] = m_in[...]
    dm_ref[...] = dot(da, po_ref[0]).astype(BF)
    low, high = lane_masks()
    pick = low_lanes()
    for s in range(PER):
        rows = slice(s * PACK, (s + 1) * PACK)
        there = pl.ds(pl.multiple_of(i * BLK + s * PACK, PACK), PACK)
        for h in range(H // 2):
            cols = slice(h * PACK, (h + 1) * PACK)
            dq, dk, dv = pair_backward(
                q_in[rows, cols], k_in[rows, cols], v_in[rows, cols],
                p_in[s * (H // 2) + h], dm_ref[rows, cols], low, high, pick,
            )
            dq_all[there, cols] = dq
            dk_all[there, cols] = dk
            dv_all[there, cols] = dv
    dq_ref[...] = dq_all[here, :]
    dk_ref[...] = dk_all[here, :]
    dv_ref[...] = dv_all[here, :]

    @pl.when(i == GRID - 1)
    def _():
        put_grad(g_own, g_oth, 0, dot(da_t[...], m_all[...]))
        put_grad(g_own, g_oth, 1, dot(x_t[...], dq_all[...]))
        put_grad(g_own, g_oth, 2, dot(x_t[...], dk_all[...]))
        put_grad(g_own, g_oth, 3, dot(x_t[...], dv_all[...]))


def self_backward(meta, dr1, m, p, q, k, v, x, w_cross):
    full = rows_spec(D)
    p_spec = pl.BlockSpec((PER * H // 2, 2 * PACK, PACK), lambda i, meta: (i, 0, 0))
    grad = (PIECES, 4, CH, HALF)
    return call(
        self_backward_body,
        (GRID,),
        [full, full, p_spec, full, full, full, full, fixed_spec((1, D, D))],
        (full, full, full, fixed_spec(grad), fixed_spec(grad)),
        (sds((TOK, D)),) * 3 + (sds(grad), sds(grad)),
        [pltpu.VMEM((D, TOK), BF)] * 2
        + [pltpu.VMEM((TOK, D), BF)] * 4
        + [pltpu.VMEM((BLK, D), BF)],
        flops=2 * TOK * D * D * 6,
        nbytes=12 * 2**20,
    )(meta, dr1, m, p, q, k, v, x, w_cross)


def inputs_backward_body(meta, dr, dq, dk, dv, dk2, dv2, w_self, w_cross, x_own, x_oth, e_own, e_oth):
    dx = dr[...] + dot_nt(dq[...], w_self[0]) + dot_nt(dk[...], w_self[1]) + dot_nt(dv[...], w_self[2])
    x_own[...], x_oth[...] = halves(meta, dx.astype(BF))
    de = dot_nt(dk2[...], w_cross[2]) + dot_nt(dv2[...], w_cross[3])
    e_own[...], e_oth[...] = halves(meta, de.astype(BF))


def inputs_backward(meta, dr1, dq, dk, dv, dk2, dv2, w_self, w_cross):
    full = rows_spec(D)
    return call(
        inputs_backward_body,
        (GRID,),
        [full] * 6 + [fixed_spec((3, D, D)), fixed_spec((5, D, D))],
        (rows_spec(HALF),) * 4,
        (sds((TOK, HALF)),) * 4,
        flops=2 * TOK * D * D * 5,
        nbytes=14 * 2**20,
    )(meta, dr1, dq, dk, dv, dk2, dv2, w_self, w_cross)


def place_body(meta, own, oth, out, sems):
    me = meta[CORE]
    copies = []
    for side, src in enumerate((own, oth)):
        first = ROW + SLOTS * side
        for j in range(SLOTS):
            at = pl.multiple_of(meta[first + j] * PACK, PACK)
            copies.append(
                pltpu.make_async_copy(
                    src.at[pl.ds(j * PACK, PACK)], out.at[pl.ds(at, PACK)], sems.at[side * SLOTS + j]
                )
            )
    for c in copies:
        c.start()
    for c in copies:
        c.wait()


def place(meta, own, oth):
    return call(
        place_body,
        (1,),
        [ANY, ANY],
        ANY,
        sds((2 * TOK, HALF)),
        [pltpu.SemaphoreType.DMA((2 * SLOTS,))],
        nbytes=4 * 2**20,
    )(meta, own, oth)


def pair_sum_body(meta, *refs):
    for k in range(4):
        refs[8 + k][...] = (refs[k][...].astype(F32) + refs[4 + k][...].astype(F32)).astype(BF)


def pair_sum(meta, own, rec):
    _, mats, _, _ = own.shape
    block = (1, mats, CH, HALF)

    def pick(k):
        return pl.BlockSpec(block, lambda i, meta: (meta[PIECE + 4 * k + i], 0, 0, 0))

    out = pl.BlockSpec(block, lambda i, meta: (i, 0, 0, 0))
    return call(
        pair_sum_body,
        (4,),
        [pick(k) for k in range(4)] * 2,
        (out,) * 4,
        (sds((4, mats, CH, HALF)),) * 4,
        flops=10**6,
        nbytes=own.size * 6,
    )(meta, own, own, own, own, rec, rec, rec, rec)


def four_sum_body(a, b, c, d, *outs):
    for j in range(4):
        total = a[j].astype(F32) + b[j].astype(F32) + (c[j].astype(F32) + d[j].astype(F32))
        outs[j][...] = total.astype(BF)


def four_sum(a, b, c, d):
    return pl.pallas_call(
        four_sum_body,
        out_shape=(sds(a.shape[1:]),) * 4,
        cost_estimate=pl.CostEstimate(flops=10**6, bytes_accessed=a.size * 10, transcendentals=0),
        compiler_params=pltpu.CompilerParams(vmem_limit_bytes=56 * 1024 * 1024),
    )(a, b, c, d)


def adam(weight, first_old, second_old, grad, rate, decay):
    first_new = beta_first * first_old + (1.0 - beta_first) * grad
    second_new = beta_second * second_old + (1.0 - beta_second) * grad * grad
    first_hat = first_new / (1.0 - beta_first**STEP)
    second_hat = second_new / (1.0 - beta_second**STEP)
    updated = weight - rate * (first_hat / (jnp.sqrt(second_hat) + adam_epsilon) + decay * weight)
    return (first_new, second_new, updated)


def swap(value):
    return lax.ppermute(value, "narrow", [(0, 1), (1, 0)])


def peer(value, mask):
    return lax.ppermute(value, "wide", [(i, i ^ mask) for i in range(lax.axis_size("wide"))])


def gather_pieces(g):
    z = jnp.stack([g] + [peer(g, 4 * k) for k in (1, 2, 3)])
    own = [z] + [peer(z, k) for k in (1, 2, 3)]
    return own + [swap(a) for a in own]


def sum_pieces(meta, own, oth):
    s = pair_sum(meta, own, swap(oth))
    z = four_sum(s[0], *[peer(s[k], k) for k in (1, 2, 3)])
    rest = [peer(z[k], 4 * k) for k in (1, 2, 3)]
    return z[0].astype(F32) + rest[0].astype(F32) + (rest[1].astype(F32) + rest[2].astype(F32))


def local(
    tokens,
    encoded,
    cotangent,
    target_lengths,
    source_segments,
    send_rows,
    proj_in,
    proj_out,
    ffn_in,
    ffn_out,
    norm_par,
    proj_in_moment,
    proj_in_square,
    proj_out_moment,
    proj_out_square,
    ffn_in_moment,
    ffn_in_square,
    ffn_out_moment,
    ffn_out_square,
    norm_moment,
    norm_square,
):
    wide_count = lax.axis_size("wide")
    w = lax.axis_index("wide")
    n = lax.axis_index("narrow")
    rows_dev = tokens.shape[0] // PACK
    stride = wide_count // rows_dev
    share = proj_in.shape[1]
    blocks = ffn_in.shape[1] // HALF
    direct = share == CH

    places = jnp.arange(rows_dev, dtype=jnp.int32)
    slot_rows = lax.dynamic_index_in_dim(send_rows, w, 0, keepdims=False)[places * stride + w % stride]
    mine = lax.dynamic_slice_in_dim(slot_rows, n * SLOTS, SLOTS)
    theirs = lax.dynamic_slice_in_dim(slot_rows, (1 - n) * SLOTS, SLOTS)
    mine_global = w * rows_dev + mine
    lengths = target_lengths[mine_global]
    if direct:
        piece_ids = w ^ jnp.array([a | (b << 2) for a in range(4) for b in range(4)], jnp.int32)
    else:
        piece_ids = jnp.arange(PIECES, dtype=jnp.int32)
    meta = jnp.concatenate(
        [n[None], piece_ids, mine, theirs, lengths[:, 0], lengths[:, 0] + lengths[:, 1], mine_global]
    ).astype(jnp.int32)

    if direct:
        g0, g1, g2 = pack(proj_in, proj_out, ffn_in, ffn_out, norm_par)
        pieces = [gather_pieces(g) for g in (g0, g1, g2)]
    else:
        low_in = lax.all_gather(proj_in.astype(BF), "wide", axis=1, tiled=True)
        low_out = lax.all_gather(proj_out.astype(BF), "wide", axis=2, tiled=True).transpose(0, 2, 1)
        low_win = lax.all_gather(ffn_in.astype(BF), "wide", axis=0, tiled=True)
        low_wout = lax.all_gather(ffn_out.astype(BF), "wide", axis=1, tiled=True).T
        low_norm = lax.all_gather(norm_par.astype(BF), "wide", axis=1, tiled=True)

        def column_blocks(a):
            return a.reshape(D, blocks, HALF).transpose(1, 0, 2)

        tiled = jnp.tile(low_norm.reshape(6, PIECES, CH).transpose(1, 0, 2), (1, 1, HALF // CH))
        norm_mat = jnp.pad(tiled, ((0, 0), (0, CH - 6), (0, 0))).reshape(1, D, HALF)
        groups = (
            low_in[:3],
            jnp.concatenate([low_out[:1], low_in[3:], norm_mat]),
            jnp.concatenate([low_out[1:], column_blocks(low_win), column_blocks(low_wout)]),
        )
        pieces = []
        for group in groups:
            cut = group.reshape(-1, PIECES, CH, HALF).transpose(1, 0, 2, 3)
            own = [cut[4 * k : 4 * k + 4] for k in range(4)]
            pieces.append(own + [swap(a) for a in own])

    tok_oth = swap(tokens)
    enc_oth = swap(encoded)
    everyone = [[r + stride * j for j in range(rows_dev)] for r in range(stride)]

    def exchange(rows):
        return lax.all_to_all(
            rows.reshape(rows_dev, PACK, HALF), "wide", 0, 0, axis_index_groups=everyone
        ).reshape(rows_dev * PACK, HALF)

    cot_own = exchange(cotangent)
    cot_oth = swap(cot_own)
    segs = source_segments.reshape(-1, 1, PACK)

    x, q1, k1, v1, m1, p1, w_self = self_forward(meta, tokens, tok_oth, pieces[0])
    n1, rstd1, h1, enc, q2, k2, v2, m2, p2, w_cross, norm = cross_forward(
        meta, x, m1, encoded, enc_oth, segs, pieces[1]
    )
    out_own, out_oth, dr2, po2, gf_own, gf_oth, ng = ffn(
        meta, n1, m2, norm, cot_own, cot_oth, pieces[2]
    )
    dr1, dk2, dv2, gc_own, gc_oth, ng = cross_backward(
        meta, dr2, m2, p2, q2, k2, v2, enc, h1, n1, rstd1, norm, ng, w_cross, po2
    )
    dq1, dk1, dv1, gs_own, gs_oth = self_backward(meta, dr1, m1, p1, q1, k1, v1, x, w_cross)
    dx_own, dx_oth, de_own, de_oth = inputs_backward(
        meta, dr1, dq1, dk1, dv1, dk2, dv2, w_self, w_cross
    )
    tokens_grad = place(meta, dx_own, swap(dx_oth))
    encoded_grad = place(meta, de_own, swap(de_oth))

    out_rec = swap(out_oth)
    out_lo = jnp.where(n == 0, out_own, out_rec)
    out_hi = jnp.where(n == 0, out_rec, out_own)
    layer_out = exchange(jnp.concatenate([out_lo, out_hi], 0))

    if direct:
        gf = sum_pieces(meta, gf_own, gf_oth)
        gc = sum_pieces(meta, gc_own, gc_oth)
        gs = sum_pieces(meta, gs_own, gs_oth)
        norm_half = gc[4, :6]
        norm_grad = lax.dynamic_slice_in_dim(norm_half, (w % (HALF // CH)) * CH, CH, 1)
    else:

        def summed(own, oth):
            total = (own.astype(F32) + swap(oth).astype(F32)).astype(BF)
            total = total.transpose(1, 0, 2, 3).reshape(-1, D, HALF)
            return lax.psum_scatter(total, "wide", scatter_dimension=1, tiled=True).astype(F32)

        gf, gc, gs = summed(gf_own, gf_oth), summed(gc_own[:, :4], gc_oth[:, :4]), summed(gs_own, gs_oth)
        norm_all = lax.psum(ng, ("wide", "narrow"))[:6]
        norm_grad = lax.dynamic_slice_in_dim(norm_all, w * share, share, 1)

    grad_in = jnp.concatenate([gs[1:4], gc[1:4]])
    grad_out = jnp.stack([gs[0], gc[0]]).transpose(0, 2, 1)
    grad_expand = gf[:blocks].transpose(1, 0, 2).reshape(share, blocks * HALF)
    grad_reduce = gf[blocks:].transpose(1, 0, 2).reshape(share, blocks * HALF).T
    upd_in = adam(proj_in, proj_in_moment, proj_in_square, grad_in, rate_matrix, decay_matrix)
    upd_out = adam(proj_out, proj_out_moment, proj_out_square, grad_out, rate_matrix, decay_matrix)
    upd_expand = adam(ffn_in, ffn_in_moment, ffn_in_square, grad_expand, rate_matrix, decay_matrix)
    upd_reduce = adam(ffn_out, ffn_out_moment, ffn_out_square, grad_reduce, rate_matrix, decay_matrix)
    upd_norm = adam(norm_par, norm_moment, norm_square, norm_grad, rate_norm, 0.0)
    return (layer_out, tokens_grad, encoded_grad) + upd_in + upd_out + upd_expand + upd_reduce + upd_norm


def solution(mesh):
    rows = P("wide", "narrow")
    p_in = P(None, "wide", "narrow")
    p_out = P(None, "narrow", "wide")
    p_expand = P("wide", "narrow")
    p_reduce = P("narrow", "wide")
    p_norm = P(None, "wide")
    weights = (p_in, p_out, p_expand, p_reduce, p_norm)
    in_specs = (rows,) * 3 + (P(),) * 3 + weights + tuple(s for s in weights for _ in range(2))
    out_specs = (rows,) * 3 + tuple(s for s in weights for _ in range(3))
    return jax.shard_map(local, mesh=mesh, in_specs=in_specs, out_specs=out_specs, check_vma=False)
```

```python
import functools
import math

import jax
import jax.numpy as jnp
from jax import lax
from jax.experimental import pallas as pl
from jax.experimental.pallas import tpu as pltpu
from jax.sharding import PartitionSpec as P

D = 512
H = 8
HD = D // H
PACK = 128
STEP = 5
CH = 32
HALF = D // 2
PIECES = D // CH
SLOTS = 8
TOK = SLOTS * PACK
BLK = 1024

norm_epsilon = 1e-05
beta_first = 0.9
beta_second = 0.98
adam_epsilon = 1e-08
rate_matrix = 0.1
rate_norm = 0.5
decay_matrix = 0.01
masked_score = -1e30

CORE = 0
PIECE = 1
ROW = PIECE + 2 * PIECES
FIRST = ROW + 2 * SLOTS
SECOND = FIRST + SLOTS
CUT = SECOND + SLOTS

BF = jnp.bfloat16
F32 = jnp.float32


def dot(a, b):
    return jnp.dot(a, b, preferred_element_type=F32)


def dot_nt(a, b):
    return lax.dot_general(a, b, (((1,), (1,)), ((), ())), preferred_element_type=F32)


def dot_tn(a, b):
    return lax.dot_general(a, b, (((0,), (0,)), ((), ())), preferred_element_type=F32)


def sds(shape, dtype=BF):
    return jax.ShapeDtypeStruct(shape, dtype)


def cost(us):
    return pl.CostEstimate(flops=us * 10**9, bytes_accessed=us * 3 * 10**6, transcendentals=0)


def call(body, outs, operands, far=(), far_outs=(), deps=(), scratch=(), us=1, mb=16):
    count = len(operands) + len(far)

    def run(*refs):
        body(*refs[:count], *refs[count + len(deps) :])

    vmem = pl.BlockSpec(memory_space=pltpu.VMEM)
    hbm = pl.BlockSpec(memory_space=pltpu.HBM)
    smem = pl.BlockSpec(memory_space=pltpu.SMEM)
    specs = [smem if o.dtype == jnp.int32 and o.ndim == 1 else vmem for o in operands]
    return pl.pallas_call(
        run,
        in_specs=specs + [ANY] * (len(far) + len(deps)),
        out_specs=(vmem,) * len(outs) + (hbm,) * len(far_outs),
        out_shape=tuple(outs) + tuple(far_outs),
        scratch_shapes=list(scratch),
        cost_estimate=cost(us),
        compiler_params=pltpu.CompilerParams(vmem_limit_bytes=mb * 2**20),
    )(*operands, *far, *deps)


def sems(count):
    return pltpu.SemaphoreType.DMA((count,))


class Copies:
    def __init__(self, sem):
        self.sem, self.count = sem, 0

    def start(self, src, dst):
        c = pltpu.make_async_copy(src, dst, self.sem.at[self.count])
        self.count += 1
        c.start()
        return c


def wait(copies):
    for c in copies:
        c.wait()


ANY = pl.BlockSpec(memory_space=pl.ANY)


def block(i, size):
    return pl.ds(pl.multiple_of(i * size, size), size)


def loop(count, body, unroll=1):
    def step(i, carry):
        body(i)
        return carry

    lax.fori_loop(0, count, step, 0, unroll=unroll)


def eye_of(rows, columns):
    at = [lax.broadcasted_iota(jnp.int32, (rows, columns), d) for d in range(2)]
    return (at[0] == at[1] % CH).astype(BF)


def pack_attention_body(pin, pout, norm, g):
    g[0:3] = pin[0:3].astype(BF)
    g[3] = pout[0].astype(BF)
    g[4:7] = pin[3:6].astype(BF)
    rows = dot(eye_of(CH, 6), norm[...].astype(BF)).astype(BF)
    g[7] = dot(rows, eye_of(CH, HALF)).astype(BF)


def pack_ffn_body(pout, win, wout, g):
    g[0] = pout[1].astype(BF)
    blocks = win.shape[1] // HALF
    for b in range(blocks):
        g[1 + b] = win[:, b * HALF : (b + 1) * HALF].astype(BF)
        g[1 + blocks + b] = wout[:, b * HALF : (b + 1) * HALF].astype(BF)


def stack_body(a, b, c, d, out):
    for k, ref in enumerate((a, b, c, d)):
        out[k] = ref[...]


def load_weights(meta, pieces, w_ref, sem, first=0, count=None):
    count = w_ref.shape[0] if count is None else count
    copies = []
    for a, piece in enumerate(pieces):
        half, group = divmod(a, len(pieces) // 2)
        per = piece.shape[0]
        for j in range(per):
            row = pl.multiple_of(meta[PIECE + half * PIECES + group * per + j] * CH, CH)
            copies.append(
                pltpu.make_async_copy(
                    piece.at[j, pl.ds(first, count)],
                    w_ref.at[:, pl.ds(row, CH), pl.ds(half * HALF, HALF)],
                    sem.at[a],
                )
            )
    for c in copies:
        c.start()
    return copies


def load_rows(meta, own, oth, dst, sem):
    copies = []
    for side, src in enumerate((own, oth)):
        at = meta[CORE] if side == 0 else 1 - meta[CORE]
        for j in range(SLOTS):
            copies.append(
                pltpu.make_async_copy(
                    src.at[block(meta[ROW + j], PACK)],
                    dst.at[pl.ds(j * PACK, PACK), block(at, HALF)],
                    sem.at[side],
                )
            )
    for c in copies:
        c.start()
    return copies


def lane_masks():
    low = (lax.broadcasted_iota(jnp.int32, (1, PACK), 1) < HD).astype(F32)
    return low.astype(BF), (1.0 - low).astype(BF)


def low_lanes(rows=PACK):
    return lax.broadcasted_iota(jnp.int32, (rows, PACK), 1) < HD


def two_heads(rows, low, high):
    return jnp.concatenate([rows * low, rows * high], 0)


def norm_forward(r):
    center = r - jnp.mean(r, -1, keepdims=True)
    rstd = lax.rsqrt(jnp.mean(center * center, -1, keepdims=True) + norm_epsilon)
    return center * rstd, rstd


def norm_backward(dy, n, rstd, gain):
    dn = dy * gain
    dr = rstd * (dn - jnp.mean(dn, -1, keepdims=True) - n * jnp.mean(dn * n, -1, keepdims=True))
    return dr, jnp.sum(dy * n, 0, keepdims=True), jnp.sum(dy, 0, keepdims=True)


def target_segments(meta, slot, dim):
    at = lax.broadcasted_iota(jnp.int32, (PACK, PACK), dim)
    one = (at >= meta[FIRST + slot]).astype(jnp.int32)
    return one + (at >= meta[SECOND + slot]).astype(jnp.int32)


def source_segments_of(meta, slot, dim):
    return (lax.broadcasted_iota(jnp.int32, (PACK, PACK), dim) >= meta[CUT + slot]).astype(jnp.int32)


def halves(meta, full):
    first = meta[CORE] == 0
    lo, hi = full[:, :HALF], full[:, HALF:]
    return jnp.where(first, lo, hi), jnp.where(first, hi, lo)


def mask_of(meta, slot, key_segments):
    mask = key_segments(meta, slot, 0) == target_segments(meta, slot, 1)
    return jnp.concatenate([mask, mask], 1)


def pairs_of(meta, first, count, key_segments):
    pairs = []
    for slot in [first + j for j in range(count)]:
        mask = mask_of(meta, slot, key_segments)
        rows = block(slot, PACK)
        for h in range(H // 2):
            pairs.append((rows, slice(h * PACK, (h + 1) * PACK), mask, (slot, slice(h, h + 1))))
    return pairs


def attention_forward(meta, q, k, v, lse, m, key_segments):
    low, high = lane_masks()
    scale = HD**-0.5
    slots = 2

    def step(i):
        pairs = pairs_of(meta, i * slots, slots, key_segments)
        s = [
            jnp.where(mask, dot_nt(k[r, c], two_heads(q[r, c], low * scale, high * scale)), masked_score)
            for r, c, mask, _ in pairs
        ]
        peak = [jnp.max(one, 0, keepdims=True) for one in s]
        e = [jnp.exp(one - top) for one, top in zip(s, peak)]
        total = [jnp.sum(one, 0, keepdims=True) for one in e]
        p = [(one * (1.0 / all_keys)).astype(BF) for one, all_keys in zip(e, total)]
        for (_, _, _, (slot, h)), top, all_keys in zip(pairs, peak, total):
            lse[slot, h, :] = top + jnp.log(all_keys)
        for (r, c, _, _), one in zip(pairs, p):
            mixed = dot_tn(v[r, c], one).astype(BF)
            m[r, c] = jnp.concatenate([mixed[:HD, :PACK], mixed[HD:, PACK:]], 0).T

    loop(SLOTS // slots, step, 4)


def attention_backward(meta, q, k, v, lse, dm, dq, dk, dv, key_segments):
    low, high = lane_masks()
    pick = low_lanes()
    scale = HD**-0.5

    def step(i):
        pairs = pairs_of(meta, i, 1, key_segments)
        qs = [two_heads(q[r, c], low * scale, high * scale) for r, c, _, _ in pairs]
        s = [dot_nt(k[r, c], one) for (r, c, _, _), one in zip(pairs, qs)]
        dms = [two_heads(dm[r, c], low, high) for r, c, _, _ in pairs]
        dp = [dot_nt(v[r, c], one) for (r, c, _, _), one in zip(pairs, dms)]
        p = [
            jnp.exp(jnp.where(mask, one, masked_score) - lse[slot, h, :])
            for (_, _, mask, (slot, h)), one in zip(pairs, s)
        ]
        for (r, c, _, _), one, grad in zip(pairs, p, dms):
            dv[r, c] = dot(one.astype(BF), grad).astype(BF)
        ds = [
            (one * (grad - jnp.sum(one * grad, 0, keepdims=True))).astype(BF) for one, grad in zip(p, dp)
        ]
        for (r, c, _, _), one, two in zip(pairs, ds, qs):
            dk[r, c] = dot(one, two).astype(BF)
        for (r, c, _, _), one in zip(pairs, ds):
            both = dot_tn(one, k[r, c])
            dq[r, c] = (jnp.where(pick, both[:PACK], both[PACK:]) * scale).astype(BF)

    loop(SLOTS, step, 4)


ROWS_BF = (TOK, D)
TOTALS = (SLOTS, 8, 2 * PACK)


def full(dtype=BF):
    return sds((TOK, D), dtype)


def attention_layers_body(*refs):
    meta, tok_own, tok_oth, enc_own, enc_oth = refs[:5]
    pieces = refs[5:13]
    n_ref, m2, lse1, lse2, norm = refs[13:18]
    q1_far, k1_far, v1_far, m1_far, n_far, r_far, q2_far, k2_far, v2_far = refs[18:27]
    w, x, enc, q1, k1, v1, m1, h, q2, k2, v2, r_ref, x_sem, enc_sem, w_sem, out_sem = refs[27:]
    loads = load_rows(meta, tok_own, tok_oth, x, x_sem)
    weights = load_weights(meta, pieces, w, w_sem)
    enc_loads = load_rows(meta, enc_own, enc_oth, enc, enc_sem)
    wait(loads)
    wait(weights)
    outs = Copies(out_sem)
    q1[...] = dot(x[...], w[0]).astype(BF)
    k1[...] = dot(x[...], w[1]).astype(BF)
    v1[...] = dot(x[...], w[2]).astype(BF)
    flying = [outs.start(q1, q1_far), outs.start(k1, k1_far), outs.start(v1, v1_far)]
    attention_forward(meta, q1, k1, v1, lse1, m1, target_segments)
    flying.append(outs.start(m1, m1_far))
    wait(enc_loads)
    lane = lax.broadcasted_iota(jnp.int32, (8, HALF), 1) // CH
    for half in range(2):
        total = jnp.zeros((8, HALF), F32)
        for j in range(PIECES // 2):
            at = (half * (PIECES // 2) + j) * CH
            part = w[7, at : at + 16, :HALF][:8].astype(F32)
            total = total + jnp.where(lane == j, part, 0.0)
        norm[:, half * HALF : (half + 1) * HALF] = total
    k2[...] = dot(enc[...], w[5]).astype(BF)
    v2[...] = dot(enc[...], w[6]).astype(BF)

    def step(i):
        rows = block(i, BLK)
        n, rstd = norm_forward(x[rows, :].astype(F32) + dot_nt(m1[rows, :], w[3]))
        n_ref[rows, :] = n
        r_ref[rows, :] = jnp.broadcast_to(rstd, (BLK, PACK))
        h[rows, :] = (n * norm[0:1, :] + norm[3:4, :]).astype(BF)

    loop(TOK // BLK, step)
    q2[...] = dot(h[...], w[4]).astype(BF)
    flying += [
        outs.start(src, dst)
        for src, dst in ((k2, k2_far), (v2, v2_far), (q2, q2_far), (n_ref, n_far), (r_ref, r_far))
    ]
    attention_forward(meta, q2, k2, v2, lse2, m2, source_segments_of)
    wait(flying)


def attention_layers(meta, rows, pieces):
    one = pltpu.VMEM(ROWS_BF, BF)
    return call(
        attention_layers_body,
        (full(F32), full(), sds(TOTALS, F32), sds(TOTALS, F32), sds((8, D), F32)),
        (meta,),
        rows + tuple(pieces),
        (full(),) * 4 + (full(F32), sds((TOK, PACK), F32)) + (full(),) * 3,
        scratch=[pltpu.VMEM((pieces[0].shape[1], D, D), BF)]
        + [one] * 10
        + [pltpu.VMEM((TOK, PACK), F32), sems(2), sems(2), sems(8), sems(9)],
        us=15,
        mb=48,
    )


def gelu_both(v):
    c = math.sqrt(2.0 / math.pi)
    v2 = v * v
    t = jnp.tanh(c * (v + 0.044715 * (v * v2)))
    cdf = 0.5 + 0.5 * t
    return v * cdf, cdf + (0.5 * v) * (1.0 - t * t) * (c + (3.0 * 0.044715 * c) * v2)


def put_grad(g_own, g_oth, m, value):
    value = value.astype(BF)
    g_own[:, m] = value[:, :HALF].reshape(PIECES, CH, HALF)
    g_oth[:, m] = value[:, HALF:].reshape(PIECES, CH, HALF)


def ffn_forward_body(*refs):
    meta, n1, m2, norm = refs[:4]
    pieces = refs[4:12]
    out_own, out_oth, w, act_ref, slope_ref, n2_ref, n3_ref, r_ref, m_far, po_far, sem, out_sem = refs[12:]
    blocks = (w.shape[0] - 1) // 2
    outs = Copies(out_sem)
    flying = [outs.start(m2, m_far)]
    wait(load_weights(meta, pieces, w, sem))
    flying.append(outs.start(w.at[0], po_far))

    def step(i):
        rows = block(i, BLK)
        h1 = n1[rows, :] * norm[0:1, :] + norm[3:4, :]
        n2, rstd2 = norm_forward(h1 + dot_nt(m2[rows, :], w[0]))
        n2_ref[rows, :] = n2
        h2 = n2 * norm[1:2, :] + norm[4:5, :]
        h2b = h2.astype(BF)
        r3 = h2
        pre = dot(h2b, w[1])
        for b in range(blocks):
            now = pre
            if b + 1 < blocks:
                pre = dot(h2b, w[2 + b])
            act, slope = gelu_both(now)
            act = act.astype(BF)
            act_ref[b, rows, :] = act
            slope_ref[b, rows, :] = slope.astype(BF)
            r3 = r3 + dot_nt(act, w[1 + blocks + b])
        n3, rstd3 = norm_forward(r3)
        n3_ref[rows, :] = n3
        r_ref[rows, :] = jnp.where(low_lanes(BLK), rstd2, rstd3)
        result = n3 * norm[2:3, :] + norm[5:6, :]
        out_own[rows, :], out_oth[rows, :] = halves(meta, result.astype(BF))

    loop(TOK // BLK, step)
    wait(flying)


def ffn_forward(meta, n1, m2, norm, pieces):
    mats = pieces[0].shape[1]
    hidden = sds(((mats - 1) // 2, TOK, D))
    return call(
        ffn_forward_body,
        (sds((TOK, HALF)), sds((TOK, HALF)), sds((mats, D, D)), hidden, hidden)
        + (full(F32), full(F32), sds((TOK, PACK), F32)),
        (meta, n1, m2, norm),
        tuple(pieces),
        (full(), sds((D, D))),
        scratch=[sems(8), sems(2)],
        us=9,
        mb=36,
    )


def ffn_backward_body(*refs):
    meta, norm, w, act_ref, slope_ref, n2_ref, n3_ref, r_ref, cot_own, cot_oth = refs[:10]
    dr_ref, g_own, g_oth, ng = refs[10:14]
    cot, pre_ref, df_ref, h_ref, sem = refs[14:]
    blocks = (w.shape[0] - 1) // 2
    mine = block(meta[CORE], TOK)
    loads = Copies(sem)
    wait(
        [
            loads.start(src.at[mine], cot.at[:, block(at, HALF)])
            for src, at in ((cot_own, meta[CORE]), (cot_oth, 1 - meta[CORE]))
        ]
    )
    ng[...] = jnp.zeros_like(ng)

    def step(i):
        rows = block(i, BLK)
        dy = cot[rows, :].astype(F32)
        dr3, gain3, bias3 = norm_backward(dy, n3_ref[rows, :], r_ref[rows, HD : HD + 1], norm[2:3, :])
        df = dr3.astype(BF)
        df_ref[rows, :] = df
        dh2 = dr3
        for b in range(blocks):
            dpre = (dot(df, w[1 + blocks + b]) * slope_ref[b, rows, :].astype(F32)).astype(BF)
            pre_ref[b, rows, :] = dpre
            dh2 = dh2 + dot_nt(dpre, w[1 + b])
        n2 = n2_ref[rows, :]
        h_ref[rows, :] = (n2 * norm[1:2, :] + norm[4:5, :]).astype(BF)
        dr2, gain2, bias2 = norm_backward(dh2, n2, r_ref[rows, 0:1], norm[1:2, :])
        dr_ref[rows, :] = dr2
        ng[1:2, :] += gain2
        ng[2:3, :] += gain3
        ng[4:5, :] += bias2
        ng[5:6, :] += bias3

    loop(TOK // BLK, step)
    h_t = h_ref[...].T
    for b in range(blocks):
        put_grad(g_own, g_oth, b, dot(h_t, pre_ref[b]))
    df_t = df_ref[...].T
    for b in range(blocks):
        put_grad(g_own, g_oth, blocks + b, dot(df_t, act_ref[b]))


def ffn_backward(meta, norm, w, act, slope, n2, n3, rstd, cot_own, cot_oth):
    blocks = act.shape[0]
    grad = sds((PIECES, 2 * blocks, CH, HALF))
    return call(
        ffn_backward_body,
        (full(F32), grad, grad, sds((8, D), F32)),
        (meta, norm, w, act, slope, n2, n3, rstd),
        (cot_own, cot_oth),
        scratch=[
            pltpu.VMEM(ROWS_BF, BF),
            pltpu.VMEM((blocks, TOK, D), BF),
            pltpu.VMEM(ROWS_BF, BF),
            pltpu.VMEM(ROWS_BF, BF),
            sems(2),
        ],
        us=14,
        mb=34,
    )


def fetch(sem, pairs):
    copies = Copies(sem)
    started = [copies.start(src, dst) for src, dst in pairs]
    return lambda *at: wait([started[k] for k in at])


def cross_backward_body(*refs):
    meta, dr_in, norm, ng_in, lse = refs[:5]
    q_far, k_far, v_far, m_far, n_far, r_far, po_far, enc_own, enc_oth = refs[5:14]
    pieces = refs[14:22]
    dr_ref, g_own, g_oth, ng, dr_far, dk_far, dv_far = refs[22:29]
    q, k, v, m, enc, n, r, w, po, da, dm, dq, dk, dv, h, in_sem, out_sem, w_sem, enc_sem = refs[29:]
    ready = fetch(
        in_sem,
        ((po_far, po), (q_far, q), (k_far, k), (v_far, v), (n_far, n), (r_far, r), (m_far, m)),
    )
    weights = load_weights(meta, pieces, w, w_sem, 4)
    rows_in = load_rows(meta, enc_own, enc_oth, enc, enc_sem)
    outs = Copies(out_sem)
    da[...] = dr_in[...].astype(BF)
    ready(0)
    dm[...] = dot(da[...], po[...]).astype(BF)
    ready(1, 2, 3)
    attention_backward(meta, q, k, v, lse, dm, dq, dk, dv, source_segments_of)
    flying = [outs.start(dk, dk_far), outs.start(dv, dv_far)]
    ng[...] = ng_in[...]
    ready(4, 5)
    wait(weights)

    def step(i):
        rows = block(i, BLK)
        normed = n[rows, :]
        h[rows, :] = (normed * norm[0:1, :] + norm[3:4, :]).astype(BF)
        dh1 = dr_in[rows, :] + dot_nt(dq[rows, :], w[0])
        dr1, gain1, bias1 = norm_backward(dh1, normed, r[rows, 0:1], norm[0:1, :])
        dr_ref[rows, :] = dr1
        ng[0:1, :] += gain1
        ng[3:4, :] += bias1

    loop(TOK // BLK, step)
    flying.append(outs.start(dr_ref, dr_far))
    ready(6)
    wait(rows_in)
    put_grad(g_own, g_oth, 0, dot_tn(da[...], m[...]))
    put_grad(g_own, g_oth, 1, dot_tn(h[...], dq[...]))
    put_grad(g_own, g_oth, 2, dot_tn(enc[...], dk[...]))
    put_grad(g_own, g_oth, 3, dot_tn(enc[...], dv[...]))
    total = jnp.concatenate([ng[...], jnp.zeros((CH - 8, D), F32)], 0).astype(BF)
    for c in range(PIECES):
        part = total[:, :HALF] if c < PIECES // 2 else total[:, HALF:]
        g_own[c, 4] = part
        g_oth[c, 4] = part
    wait(flying)


def cross_backward(meta, dr2, norm, ng, lse, saved, pieces, deps=()):
    grad = sds((PIECES, 5, CH, HALF))
    rows = pltpu.VMEM(ROWS_BF, BF)
    return call(
        cross_backward_body,
        (full(F32), grad, grad, sds((8, D), F32)),
        (meta, dr2, norm, ng, lse),
        saved + tuple(pieces),
        (full(F32), full(), full()),
        deps,
        [rows] * 5
        + [pltpu.VMEM((TOK, D), F32), pltpu.VMEM((TOK, PACK), F32), pltpu.VMEM((1, D, D), BF), pltpu.VMEM((D, D), BF)]
        + [rows] * 6
        + [sems(7), sems(3), sems(8), sems(2)],
        us=12,
        mb=46,
    )


def self_backward_body(*refs):
    meta, dr_in, lse = refs[:3]
    q_far, k_far, v_far, m_far, tok_own, tok_oth = refs[3:9]
    pieces = refs[9:17]
    dq, dk, dv, g_own, g_oth, q, k, v, m, x, w, da, dm, in_sem, w_sem, x_sem = refs[17:]
    weights = load_weights(meta, pieces, w, w_sem, 3)
    ready = fetch(in_sem, ((q_far, q), (k_far, k), (v_far, v), (m_far, m)))
    rows_in = load_rows(meta, tok_own, tok_oth, x, x_sem)
    da[...] = dr_in[...].astype(BF)
    wait(weights)
    dm[...] = dot(da[...], w[0]).astype(BF)
    ready(0, 1, 2)
    attention_backward(meta, q, k, v, lse, dm, dq, dk, dv, target_segments)
    ready(3)
    wait(rows_in)
    put_grad(g_own, g_oth, 0, dot_tn(da[...], m[...]))
    put_grad(g_own, g_oth, 1, dot_tn(x[...], dq[...]))
    put_grad(g_own, g_oth, 2, dot_tn(x[...], dk[...]))
    put_grad(g_own, g_oth, 3, dot_tn(x[...], dv[...]))


def self_backward(meta, dr1, lse, saved, pieces, deps=()):
    grad = sds((PIECES, 4, CH, HALF))
    rows = pltpu.VMEM(ROWS_BF, BF)
    return call(
        self_backward_body,
        (full(), full(), full(), grad, grad),
        (meta, dr1, lse),
        saved + tuple(pieces),
        (),
        deps,
        [rows] * 5 + [pltpu.VMEM((1, D, D), BF), rows, rows] + [sems(4), sems(8), sems(2)],
        us=10,
        mb=46,
    )


def inputs_backward_body(*refs):
    meta, dq, dk, dv, dr_far, dk2_far, dv2_far = refs[:7]
    pieces = refs[7:15]
    x_own, x_oth, e_own, e_oth, dr, dk2, dv2, w, w2, in_sem, w_sem, w2_sem = refs[15:]
    ready = fetch(in_sem, ((dr_far, dr), (dk2_far, dk2), (dv2_far, dv2)))
    weights = load_weights(meta, pieces, w, w_sem, 0) + load_weights(meta, pieces, w2, w2_sem, 5)
    wait(weights)
    ready(0, 1, 2)

    def step(i):
        rows = block(i, BLK)
        dx = dr[rows, :] + dot_nt(dq[rows, :], w[0]) + dot_nt(dk[rows, :], w[1]) + dot_nt(dv[rows, :], w[2])
        x_own[rows, :], x_oth[rows, :] = halves(meta, dx.astype(BF))
        de = dot_nt(dk2[rows, :], w2[0]) + dot_nt(dv2[rows, :], w2[1])
        e_own[rows, :], e_oth[rows, :] = halves(meta, de.astype(BF))

    loop(TOK // BLK, step)


def inputs_backward(meta, dq, dk, dv, saved, pieces, deps=()):
    rows = pltpu.VMEM(ROWS_BF, BF)
    return call(
        inputs_backward_body,
        (sds((TOK, HALF)),) * 4,
        (meta, dq, dk, dv),
        saved + tuple(pieces),
        (),
        deps,
        [pltpu.VMEM((TOK, D), F32), rows, rows, pltpu.VMEM((3, D, D), BF), pltpu.VMEM((2, D, D), BF)]
        + [sems(3), sems(8), sems(8)],
        us=5,
        mb=46,
    )


def place_body(meta, own, oth, out):
    for side, src in enumerate((own, oth)):
        for j in range(SLOTS):
            out[block(meta[ROW + SLOTS * side + j], PACK), :] = src[j * PACK : (j + 1) * PACK, :]


def join_body(meta, own, oth, out):
    out[block(meta[CORE], TOK), :] = own[...]
    out[block(1 - meta[CORE], TOK), :] = oth[...]


def copy_body(src, out):
    out[...] = src[...]


BOTH = (2 * TOK, HALF)


def add(a, b):
    return (a.astype(F32) + b.astype(F32)).astype(BF)


def pair_sum_body(meta, own, rec, *outs):
    for k in range(4):
        for j in range(4):
            c = meta[PIECE + 4 * k + j]
            total = add(own[c], rec[c])
            if len(outs) == 4:
                outs[k][j] = total
            elif k < 2:
                outs[k][j] = total
            else:
                outs[2][k - 2, j] = total


def pair_sum(meta, own, rec, joined, deps=()):
    shape = (4,) + own.shape[1:]
    outs = (sds(shape), sds(shape), sds((2,) + shape)) if joined else (sds(shape),) * 4
    return call(pair_sum_body, outs, (meta, own, rec), deps=deps)


def stage_sum_body(a0, a1, b, keep, send):
    keep[...] = add(a0[...], b[0])
    send[...] = add(a1[...], b[1])


def last_sum_body(a, b, *outs):
    for j in range(4):
        outs[j][...] = add(a[j], b[j])


def four_sum_body(a, b, c, d, *outs):
    for j in range(4):
        total = a[j].astype(F32) + b[j].astype(F32) + (c[j].astype(F32) + d[j].astype(F32))
        outs[j][...] = total.astype(BF)


def adam(weight, first_old, second_old, grad, rate, decay):
    first_new = beta_first * first_old + (1.0 - beta_first) * grad
    second_new = beta_second * second_old + (1.0 - beta_second) * grad * grad
    first_hat = first_new / (1.0 - beta_first**STEP)
    second_hat = second_new / (1.0 - beta_second**STEP)
    updated = weight - rate * (first_hat / (jnp.sqrt(second_hat) + adam_epsilon) + decay * weight)
    return (first_new, second_new, updated)


def swap(value):
    return lax.ppermute(value, "narrow", [(0, 1), (1, 0)])


def peer(value, mask, mask_one=None):
    masks = (mask, mask if mask_one is None else mask_one)
    chips = lax.axis_size("wide")
    route = [(2 * i + c, 2 * (i ^ masks[c]) + c) for i in range(chips) for c in range(2)]
    return lax.ppermute(value, ("wide", "narrow"), route)


def along_z(g, deps=()):
    parts = [g] + [peer(g, 4 * k) for k in (1, 2, 3)]
    return call(stack_body, (sds((4,) + g.shape),), parts, deps=deps)[0]


def sum_z(z):
    rest = [peer(z[k], 4 * k) for k in (1, 2, 3)]
    return z[0].astype(F32) + rest[0].astype(F32) + (rest[1].astype(F32) + rest[2].astype(F32))


def local(
    tokens,
    encoded,
    cotangent,
    target_lengths,
    source_segments,
    send_rows,
    proj_in,
    proj_out,
    ffn_in,
    ffn_out,
    norm_par,
    proj_in_moment,
    proj_in_square,
    proj_out_moment,
    proj_out_square,
    ffn_in_moment,
    ffn_in_square,
    ffn_out_moment,
    ffn_out_square,
    norm_moment,
    norm_square,
):
    wide_count = lax.axis_size("wide")
    w = lax.axis_index("wide")
    n = lax.axis_index("narrow")
    rows_dev = tokens.shape[0] // PACK
    stride = wide_count // rows_dev
    share = proj_in.shape[1]
    blocks = ffn_in.shape[1] // HALF
    direct = share == CH

    places = jnp.arange(rows_dev, dtype=jnp.int32)
    slot_rows = lax.dynamic_index_in_dim(send_rows, w, 0, keepdims=False)[places * stride + w % stride]
    mine = lax.dynamic_slice_in_dim(slot_rows, n * SLOTS, SLOTS)
    theirs = lax.dynamic_slice_in_dim(slot_rows, (1 - n) * SLOTS, SLOTS)
    mine_global = w * rows_dev + mine
    lengths = target_lengths[mine_global]
    if direct:
        orders = jnp.array([[a | (b << 2) for a in order for b in range(4)] for order in ((0, 1, 2, 3), (0, 2, 1, 3))])
        piece_ids = w ^ jnp.concatenate([orders[n], orders[1 - n]])
    else:
        piece_ids = jnp.tile(jnp.arange(PIECES, dtype=jnp.int32), 2)
    cut = jnp.sum((source_segments[mine_global] == 0).astype(jnp.int32), 1)
    meta = jnp.concatenate(
        [n[None], piece_ids, mine, theirs, lengths[:, 0], lengths[:, 0] + lengths[:, 1], cut]
    ).astype(jnp.int32)

    tok_rows = (tokens, swap(tokens))
    enc_rows = (encoded, swap(encoded))
    pout_t = proj_out.transpose(0, 2, 1)
    wout_t = ffn_out.T

    if direct:
        g0 = call(pack_attention_body, (sds((8, CH, HALF)),), (proj_in, pout_t, norm_par), us=2)[0]
        z0 = along_z(g0)
        first0 = peer(z0, 1, 2)
        second0 = peer(z0, 2, 1)
        third0 = peer(first0, 2, 1)
        pieces0 = [z0, first0, second0, third0]
        g1 = call(
            pack_ffn_body,
            (sds((1 + 2 * blocks, CH, HALF)),),
            (pout_t, ffn_in, wout_t),
            deps=(first0,),
            us=2,
        )[0]
        z1 = along_z(g1, (second0, third0))
        first1 = peer(z1, 1, 2)
        pieces1 = [z1, first1, peer(z1, 2, 1)]
        pieces = [own + [swap(a) for a in own] for own in (pieces0, pieces1)]
        cotangent = call(copy_body, (sds(cotangent.shape),), (cotangent,), deps=(first1,))[0]
    else:
        low_in = lax.all_gather(proj_in.astype(BF), "wide", axis=1, tiled=True)
        low_out = lax.all_gather(proj_out.astype(BF), "wide", axis=2, tiled=True).transpose(0, 2, 1)
        low_win = lax.all_gather(ffn_in.astype(BF), "wide", axis=0, tiled=True)
        low_wout = lax.all_gather(ffn_out.astype(BF), "wide", axis=1, tiled=True).T
        low_norm = lax.all_gather(norm_par.astype(BF), "wide", axis=1, tiled=True)

        def column_blocks(a):
            return a.reshape(D, blocks, HALF).transpose(1, 0, 2)

        tiled = jnp.tile(low_norm.reshape(6, PIECES, CH).transpose(1, 0, 2), (1, 1, HALF // CH))
        norm_mat = jnp.pad(tiled, ((0, 0), (0, CH - 6), (0, 0))).reshape(1, D, HALF)
        groups = (
            jnp.concatenate([low_in[:3], low_out[:1], low_in[3:], norm_mat]),
            jnp.concatenate([low_out[1:], column_blocks(low_win), column_blocks(low_wout)]),
        )
        pieces = []
        for group in groups:
            cut = group.reshape(-1, PIECES, CH, HALF).transpose(1, 0, 2, 3)
            own = [cut[4 * k : 4 * k + 4] for k in range(4)]
            pieces.append(own + [swap(a) for a in own])

    everyone = [[r + stride * j for j in range(rows_dev)] for r in range(stride)]

    def exchange(rows):
        return lax.all_to_all(
            rows.reshape(rows_dev, PACK, HALF), "wide", 0, 0, axis_index_groups=everyone
        ).reshape(rows_dev * PACK, HALF)

    cot_own = exchange(cotangent)
    cot_oth = swap(cot_own)
    n1, m2, lse1, lse2, norm, q1, k1, v1, m1, n1_far, rstd1, q2, k2, v2 = attention_layers(
        meta, tok_rows + enc_rows, pieces[0]
    )
    if direct:
        passed = call(copy_body, (sds(first1.shape),), (first1,), deps=(lse2,))[0]
        third1 = peer(passed, 2, 1)
        pieces[1] = pieces[1][:3] + [third1] + pieces[1][3:] + [swap(third1)]
    out_own, out_oth, w_ffn, act, slope, n2, n3, rstd, m2_far, po2 = ffn_forward(meta, n1, m2, norm, pieces[1])
    dr2, gf_own, gf_oth, ng = ffn_backward(
        meta, norm, w_ffn, act, slope, n2, n3, rstd, cot_own, cot_oth
    )
    layer_out = exchange(call(join_body, (sds(BOTH),), (meta, out_own, swap(out_oth)))[0])
    early = ()
    if direct:
        sf = pair_sum(meta, gf_own, swap(gf_oth), True)
        early = (sf[2],)
    dr1, gc_own, gc_oth, ng, dr1_far, dk2, dv2 = cross_backward(
        meta, dr2, norm, ng, lse2, (q2, k2, v2, m2_far, n1_far, rstd1, po2) + enc_rows, pieces[0], early
    )
    if direct:
        kf, send_f = call(stage_sum_body, (sds(sf[0].shape),) * 2, (sf[0], sf[1], peer(sf[2], 2, 1)))
        sc = pair_sum(meta, gc_own, swap(gc_oth), True)
        early = (send_f,)
    dq1, dk1, dv1, gs_own, gs_oth = self_backward(
        meta, dr1, lse1, (q1, k1, v1, m1) + tok_rows, pieces[0], early
    )
    if direct:
        zf = call(last_sum_body, (sds(kf.shape[1:]),) * 4, (kf, peer(send_f, 1, 2)), deps=(dq1,))
        ss = pair_sum(meta, gs_own, swap(gs_oth), False)
        kc, send_c = call(
            stage_sum_body, (sds(sc[0].shape),) * 2, (sc[0], sc[1], peer(sc[2], 2, 1)), deps=(ss[1],)
        )
        early = (ss[1], layer_out)
    dx_own, dx_oth, de_own, de_oth = inputs_backward(
        meta, dq1, dk1, dv1, (dr1_far, dk2, dv2), pieces[0], early
    )
    tokens_grad = call(place_body, (sds(BOTH),), (meta, dx_own, swap(dx_oth)))[0]
    encoded_grad = call(place_body, (sds(BOTH),), (meta, de_own, swap(de_oth)))[0]

    if direct:
        zs = call(
            four_sum_body,
            (sds(ss[0].shape[1:]),) * 4,
            (ss[0], peer(ss[1], 1, 2), peer(ss[2], 2, 1), peer(ss[3], 3)),
        )
        zc = call(last_sum_body, (sds(kc.shape[1:]),) * 4, (kc, peer(send_c, 1, 2)))
        gf, gc, gs = sum_z(zf), sum_z(zc), sum_z(zs)
        norm_half = gc[4, :6]
        norm_half = jnp.where(n == 0, norm_half, swap(norm_half))
        norm_grad = lax.dynamic_slice_in_dim(norm_half, (w % (HALF // CH)) * CH, CH, 1)
    else:

        def summed(own, oth):
            total = (own.astype(F32) + swap(oth).astype(F32)).astype(BF)
            total = total.transpose(1, 0, 2, 3).reshape(-1, D, HALF)
            return lax.psum_scatter(total, "wide", scatter_dimension=1, tiled=True).astype(F32)

        gf, gc, gs = summed(gf_own, gf_oth), summed(gc_own[:, :4], gc_oth[:, :4]), summed(gs_own, gs_oth)
        norm_all = lax.psum(ng, ("wide", "narrow"))[:6]
        norm_grad = lax.dynamic_slice_in_dim(norm_all, w * share, share, 1)

    grad_in = jnp.concatenate([gs[1:4], gc[1:4]])
    grad_out = jnp.stack([gs[0], gc[0]])
    grad_expand = gf[:blocks].transpose(1, 0, 2).reshape(share, blocks * HALF)
    grad_reduce = gf[blocks:].transpose(1, 0, 2).reshape(share, blocks * HALF)
    upd_in = adam(proj_in, proj_in_moment, proj_in_square, grad_in, rate_matrix, decay_matrix)
    upd_out = adam(
        pout_t,
        proj_out_moment.transpose(0, 2, 1),
        proj_out_square.transpose(0, 2, 1),
        grad_out,
        rate_matrix,
        decay_matrix,
    )
    upd_out = tuple(u.transpose(0, 2, 1) for u in upd_out)
    upd_expand = adam(ffn_in, ffn_in_moment, ffn_in_square, grad_expand, rate_matrix, decay_matrix)
    upd_reduce = adam(
        wout_t, ffn_out_moment.T, ffn_out_square.T, grad_reduce, rate_matrix, decay_matrix
    )
    upd_reduce = tuple(u.T for u in upd_reduce)
    upd_norm = adam(norm_par, norm_moment, norm_square, norm_grad, rate_norm, 0.0)
    return (layer_out, tokens_grad, encoded_grad) + upd_in + upd_out + upd_expand + upd_reduce + upd_norm


def solution(mesh):
    rows = P("wide", "narrow")
    p_in = P(None, "wide", "narrow")
    p_out = P(None, "narrow", "wide")
    p_expand = P("wide", "narrow")
    p_reduce = P("narrow", "wide")
    p_norm = P(None, "wide")
    weights = (p_in, p_out, p_expand, p_reduce, p_norm)
    in_specs = (rows,) * 3 + (P(),) * 3 + weights + tuple(s for s in weights for _ in range(2))
    out_specs = (rows,) * 3 + tuple(s for s in weights for _ in range(3))
    return jax.shard_map(local, mesh=mesh, in_specs=in_specs, out_specs=out_specs, check_vma=False)
```

```python
import functools
import math

import jax
import jax.numpy as jnp
from jax import lax
from jax.experimental import pallas as pl
from jax.experimental.pallas import tpu as pltpu
from jax.sharding import PartitionSpec as P

D = 512
H = 8
HD = D // H
PACK = 128
STEP = 5
CH = 32
HALF = D // 2
PIECES = D // CH
SLOTS = 8
TOK = SLOTS * PACK
BLK = 1024

norm_epsilon = 1e-05
beta_first = 0.9
beta_second = 0.98
adam_epsilon = 1e-08
rate_matrix = 0.1
rate_norm = 0.5
decay_matrix = 0.01
masked_score = -1e30

CORE = 0
PIECE = 1
ROW = PIECE + 2 * PIECES
FIRST = ROW + 2 * SLOTS
SECOND = FIRST + SLOTS
CUT = SECOND + SLOTS

BF = jnp.bfloat16
F32 = jnp.float32


def dot(a, b):
    return jnp.dot(a, b, preferred_element_type=F32)


def dot_nt(a, b):
    return lax.dot_general(a, b, (((1,), (1,)), ((), ())), preferred_element_type=F32)


def dot_tn(a, b):
    return lax.dot_general(a, b, (((0,), (0,)), ((), ())), preferred_element_type=F32)


def sds(shape, dtype=BF):
    return jax.ShapeDtypeStruct(shape, dtype)


def cost(us):
    return pl.CostEstimate(flops=us * 10**9, bytes_accessed=us * 3 * 10**6, transcendentals=0)


def call(body, outs, operands, far=(), far_outs=(), deps=(), scratch=(), us=1, mb=16):
    count = len(operands) + len(far)

    def run(*refs):
        body(*refs[:count], *refs[count + len(deps) :])

    vmem = pl.BlockSpec(memory_space=pltpu.VMEM)
    hbm = pl.BlockSpec(memory_space=pltpu.HBM)
    smem = pl.BlockSpec(memory_space=pltpu.SMEM)
    specs = [smem if o.dtype == jnp.int32 and o.ndim == 1 else vmem for o in operands]
    return pl.pallas_call(
        run,
        in_specs=specs + [hbm] * len(far) + [ANY] * len(deps),
        out_specs=(vmem,) * len(outs) + (hbm,) * len(far_outs),
        out_shape=tuple(outs) + tuple(far_outs),
        scratch_shapes=list(scratch),
        cost_estimate=cost(us),
        compiler_params=pltpu.CompilerParams(vmem_limit_bytes=mb * 2**20),
    )(*operands, *far, *deps)


def sems(count):
    return pltpu.SemaphoreType.DMA((count,))


class Copies:
    def __init__(self, sem):
        self.sem, self.count = sem, 0

    def start(self, src, dst):
        c = pltpu.make_async_copy(src, dst, self.sem.at[self.count])
        self.count += 1
        c.start()
        return c


def wait(copies):
    for c in copies:
        c.wait()


ANY = pl.BlockSpec(memory_space=pl.ANY)


def block(i, size):
    return pl.ds(pl.multiple_of(i * size, size), size)


def loop(count, body, unroll=1):
    def step(i, carry):
        body(i)
        return carry

    lax.fori_loop(0, count, step, 0, unroll=unroll)


def eye_of(rows, columns):
    at = [lax.broadcasted_iota(jnp.int32, (rows, columns), d) for d in range(2)]
    return (at[0] == at[1] % CH).astype(BF)


def pack_attention_body(pin_far, pout_far, norm_far, g, pin, pout, norm, sem):
    loads = Copies(sem)
    wait([loads.start(pin_far, pin), loads.start(pout_far.at[0], pout), loads.start(norm_far, norm)])
    rows = dot(eye_of(CH, 6), norm[...].astype(BF)).astype(BF)
    rows = dot(rows, eye_of(CH, HALF)).astype(BF)
    g[0:3] = pin[0:3].astype(BF)
    g[3] = pout[...].astype(BF)
    g[4:7] = pin[3:6].astype(BF)
    g[7] = rows


def pack_ffn_body(pout, win, wout, g):
    blocks = win.shape[1] // HALF
    for to in range(4):
        g[to, 0] = pout[1].astype(BF)
        for b in range(blocks):
            g[to, 1 + b] = win[:, b * HALF : (b + 1) * HALF].astype(BF)
            g[to, 1 + blocks + b] = wout[:, b * HALF : (b + 1) * HALF].astype(BF)


def stack_body(at, *refs):
    for j in range(4):
        refs[4][at[0] ^ j] = refs[j][...]


def load_weights(meta, pieces, w_ref, sem, first=0, count=None, at=None):
    at = first if at is None else at
    count = w_ref.shape[0] - at if count is None else count
    copies = []
    for a, piece in enumerate(pieces):
        half, group = divmod(a, len(pieces) // 2)
        per = piece.shape[0]
        for j in range(per):
            row = pl.multiple_of(meta[PIECE + half * PIECES + group * per + j] * CH, CH)
            copies.append(
                pltpu.make_async_copy(
                    piece.at[j, pl.ds(first, count)],
                    w_ref.at[pl.ds(at, count), pl.ds(row, CH), pl.ds(half * HALF, HALF)],
                    sem.at[a],
                )
            )
    for c in copies:
        c.start()
    return copies


def load_rows(meta, own, oth, dst, sem):
    copies = []
    for side, src in enumerate((own, oth)):
        at = meta[CORE] if side == 0 else 1 - meta[CORE]
        for j in range(SLOTS):
            copies.append(
                pltpu.make_async_copy(
                    src.at[block(meta[ROW + j], PACK)],
                    dst.at[pl.ds(j * PACK, PACK), block(at, HALF)],
                    sem.at[side],
                )
            )
    for c in copies:
        c.start()
    return copies


def lane_masks():
    low = (lax.broadcasted_iota(jnp.int32, (1, PACK), 1) < HD).astype(F32)
    return low.astype(BF), (1.0 - low).astype(BF)


def low_lanes(rows=PACK):
    return lax.broadcasted_iota(jnp.int32, (rows, PACK), 1) < HD


def two_heads(rows, low, high):
    return jnp.concatenate([rows * low, rows * high], 0)


def norm_forward(r):
    center = r - jnp.mean(r, -1, keepdims=True)
    rstd = lax.rsqrt(jnp.mean(center * center, -1, keepdims=True) + norm_epsilon)
    return center * rstd, rstd


def norm_backward(dy, n, rstd, gain):
    dn = dy * gain
    dr = rstd * (dn - jnp.mean(dn, -1, keepdims=True) - n * jnp.mean(dn * n, -1, keepdims=True))
    return dr, jnp.sum(dy * n, 0, keepdims=True), jnp.sum(dy, 0, keepdims=True)


def target_segments(meta, slot, dim):
    at = lax.broadcasted_iota(jnp.int32, (PACK, PACK), dim)
    one = (at >= meta[FIRST + slot]).astype(jnp.int32)
    return one + (at >= meta[SECOND + slot]).astype(jnp.int32)


def source_segments_of(meta, slot, dim):
    return (lax.broadcasted_iota(jnp.int32, (PACK, PACK), dim) >= meta[CUT + slot]).astype(jnp.int32)


def halves(meta, full):
    first = meta[CORE] == 0
    lo, hi = full[:, :HALF], full[:, HALF:]
    return jnp.where(first, lo, hi), jnp.where(first, hi, lo)


def mask_of(meta, slot, key_segments):
    mask = key_segments(meta, slot, 0) == target_segments(meta, slot, 1)
    return jnp.concatenate([mask, mask], 1)


def pairs_of(meta, first, count, key_segments):
    pairs = []
    for slot in [first + j for j in range(count)]:
        mask = mask_of(meta, slot, key_segments)
        rows = block(slot, PACK)
        for h in range(H // 2):
            pairs.append((rows, slice(h * PACK, (h + 1) * PACK), mask, (slot, slice(h, h + 1))))
    return pairs


def attention_forward(meta, q, k, v, lse, m, key_segments):
    low, high = lane_masks()
    scale = HD**-0.5
    slots = 2

    def step(i):
        pairs = pairs_of(meta, i * slots, slots, key_segments)
        s = [
            jnp.where(mask, dot_nt(k[r, c], two_heads(q[r, c], low * scale, high * scale)), masked_score)
            for r, c, mask, _ in pairs
        ]
        peak = [jnp.max(one, 0, keepdims=True) for one in s]
        e = [jnp.exp(one - top) for one, top in zip(s, peak)]
        total = [jnp.sum(one, 0, keepdims=True) for one in e]
        p = [(one * (1.0 / all_keys)).astype(BF) for one, all_keys in zip(e, total)]
        for (_, _, _, (slot, h)), top, all_keys in zip(pairs, peak, total):
            lse[slot, h, :] = top + jnp.log(all_keys)
        for (r, c, _, _), one in zip(pairs, p):
            mixed = dot_tn(v[r, c], one).astype(BF)
            m[r, c] = jnp.concatenate([mixed[:HD, :PACK], mixed[HD:, PACK:]], 0).T

    loop(SLOTS // slots, step, 4)


def attention_backward(meta, q, k, v, lse, dm, dq, dk, dv, key_segments):
    low, high = lane_masks()
    pick = low_lanes()
    scale = HD**-0.5

    def step(i):
        pairs = pairs_of(meta, i, 1, key_segments)
        qs = [two_heads(q[r, c], low * scale, high * scale) for r, c, _, _ in pairs]
        s = [dot_nt(k[r, c], one) for (r, c, _, _), one in zip(pairs, qs)]
        dms = [two_heads(dm[r, c], low, high) for r, c, _, _ in pairs]
        dp = [dot_nt(v[r, c], one) for (r, c, _, _), one in zip(pairs, dms)]
        p = [
            jnp.exp(jnp.where(mask, one, masked_score) - lse[slot, h, :])
            for (_, _, mask, (slot, h)), one in zip(pairs, s)
        ]
        for (r, c, _, _), one, grad in zip(pairs, p, dms):
            dv[r, c] = dot(one.astype(BF), grad).astype(BF)
        ds = [
            (one * (grad - jnp.sum(one * grad, 0, keepdims=True))).astype(BF) for one, grad in zip(p, dp)
        ]
        for (r, c, _, _), one, two in zip(pairs, ds, qs):
            dk[r, c] = dot(one, two).astype(BF)
        for (r, c, _, _), one in zip(pairs, ds):
            both = dot_tn(one, k[r, c])
            dq[r, c] = (jnp.where(pick, both[:PACK], both[PACK:]) * scale).astype(BF)

    loop(SLOTS, step, 4)


ROWS_BF = (TOK, D)
TOTALS = (SLOTS, 8, 2 * PACK)


def full(dtype=BF):
    return sds((TOK, D), dtype)


def attention_layers_body(*refs):
    meta, tok_own, tok_oth, enc_own, enc_oth = refs[:5]
    pieces = refs[5:13]
    m2, lse1, lse2, norm = refs[13:17]
    q1_far, k1_far, v1_far, m1_far, n_far, r_far, q2_far, k2_far, v2_far = refs[17:26]
    w, x, enc, q1, k1, v1, m1, h, q2, k2, v2, n_ref, r_ref, x_sem, enc_sem, w_sem, out_sem = refs[26:]
    loads = load_rows(meta, tok_own, tok_oth, x, x_sem)
    loads += load_weights(meta, pieces, w, w_sem.at[0], 0, 3)
    rest = load_weights(meta, pieces, w, w_sem.at[1], 3)
    rest += load_rows(meta, enc_own, enc_oth, enc, enc_sem)
    wait(loads)
    outs = Copies(out_sem)
    q1[...] = dot(x[...], w[0]).astype(BF)
    k1[...] = dot(x[...], w[1]).astype(BF)
    v1[...] = dot(x[...], w[2]).astype(BF)
    flying = [outs.start(q1, q1_far), outs.start(k1, k1_far), outs.start(v1, v1_far)]
    attention_forward(meta, q1, k1, v1, lse1, m1, target_segments)
    flying.append(outs.start(m1, m1_far))
    wait(rest)
    lane = lax.broadcasted_iota(jnp.int32, (8, HALF), 1) // CH
    for half in range(2):
        total = jnp.zeros((8, HALF), F32)
        for j in range(PIECES // 2):
            at = (half * (PIECES // 2) + j) * CH
            part = w[7, at : at + 16, :HALF][:8].astype(F32)
            total = total + jnp.where(lane == j, part, 0.0)
        norm[:, half * HALF : (half + 1) * HALF] = total
    k2[...] = dot(enc[...], w[5]).astype(BF)
    v2[...] = dot(enc[...], w[6]).astype(BF)

    def step(i):
        rows = block(i, BLK)
        n, rstd = norm_forward(x[rows, :].astype(F32) + dot_nt(m1[rows, :], w[3]))
        n_ref[rows, :] = n
        r_ref[rows, :] = jnp.broadcast_to(rstd, (BLK, PACK))
        h[rows, :] = (n * norm[0:1, :] + norm[3:4, :]).astype(BF)

    loop(TOK // BLK, step)
    q2[...] = dot(h[...], w[4]).astype(BF)
    flying += [
        outs.start(src, dst)
        for src, dst in ((k2, k2_far), (v2, v2_far), (q2, q2_far), (n_ref, n_far), (r_ref, r_far))
    ]
    attention_forward(meta, q2, k2, v2, lse2, m2, source_segments_of)
    wait(flying)


def attention_layers(meta, rows, pieces, deps=()):
    one = pltpu.VMEM(ROWS_BF, BF)
    return call(
        attention_layers_body,
        (full(), sds(TOTALS, F32), sds(TOTALS, F32), sds((8, D), F32)),
        (meta,),
        rows + tuple(pieces),
        (full(),) * 4 + (full(F32), sds((TOK, PACK), F32)) + (full(),) * 3,
        deps=deps,
        scratch=[pltpu.VMEM((pieces[0].shape[1], D, D), BF)]
        + [one] * 10
        + [pltpu.VMEM((TOK, D), F32), pltpu.VMEM((TOK, PACK), F32), sems(2), sems(2), pltpu.SemaphoreType.DMA((2, 8)), sems(9)],
        us=15,
        mb=48,
    )


def gelu_both(v):
    c = math.sqrt(2.0 / math.pi)
    v2 = v * v
    t = jnp.tanh(c * (v + 0.044715 * (v * v2)))
    cdf = 0.5 + 0.5 * t
    return v * cdf, cdf + (0.5 * v) * (1.0 - t * t) * (c + (3.0 * 0.044715 * c) * v2)


def put_grad(g_own, g_oth, m, value):
    value = value.astype(BF)
    g_own[:, m] = value[:, :HALF].reshape(PIECES, CH, HALF)
    g_oth[:, m] = value[:, HALF:].reshape(PIECES, CH, HALF)


def ffn_forward_body(*refs):
    meta, m2, norm, n_far = refs[:4]
    pieces = refs[4:12]
    out_own, out_oth, w, act_ref, slope_ref, n2_ref, n3_ref, r_ref, m_far, po_far, n1, sem, out_sem, in_sem = refs[12:]
    blocks = (w.shape[0] - 1) // 2
    outs = Copies(out_sem)
    flying = [outs.start(m2, m_far)]
    loading = Copies(in_sem).start(n_far, n1)
    wait(load_weights(meta, pieces, w, sem))
    loading.wait()
    flying.append(outs.start(w.at[0], po_far))

    def step(i):
        rows = block(i, BLK)
        h1 = n1[rows, :] * norm[0:1, :] + norm[3:4, :]
        n2, rstd2 = norm_forward(h1 + dot_nt(m2[rows, :], w[0]))
        n2_ref[rows, :] = n2
        h2 = n2 * norm[1:2, :] + norm[4:5, :]
        h2b = h2.astype(BF)
        r3 = h2
        pre = dot(h2b, w[1])
        for b in range(blocks):
            now = pre
            if b + 1 < blocks:
                pre = dot(h2b, w[2 + b])
            act, slope = gelu_both(now)
            act = act.astype(BF)
            act_ref[b, rows, :] = act
            slope_ref[b, rows, :] = slope.astype(BF)
            r3 = r3 + dot_nt(act, w[1 + blocks + b])
        n3, rstd3 = norm_forward(r3)
        n3_ref[rows, :] = n3
        r_ref[rows, :] = jnp.where(low_lanes(BLK), rstd2, rstd3)
        result = n3 * norm[2:3, :] + norm[5:6, :]
        out_own[rows, :], out_oth[rows, :] = halves(meta, result.astype(BF))

    loop(TOK // BLK, step)
    wait(flying)


def ffn_forward(meta, n1_far, m2, norm, pieces):
    mats = pieces[0].shape[1]
    hidden = sds(((mats - 1) // 2, TOK, D))
    return call(
        ffn_forward_body,
        (sds((TOK, HALF)), sds((TOK, HALF)), sds((mats, D, D)), hidden, hidden)
        + (full(F32), full(F32), sds((TOK, PACK), F32)),
        (meta, m2, norm),
        (n1_far,) + tuple(pieces),
        (full(), sds((D, D))),
        scratch=[pltpu.VMEM((TOK, D), F32), sems(8), sems(2), sems(1)],
        us=9,
        mb=24,
    )


def ffn_backward_body(*refs):
    meta, norm, w, act_ref, slope_ref, n2_ref, n3_ref, r_ref, cot_own, cot_oth = refs[:10]
    g_own, g_oth, ng, dr_far = refs[10:14]
    cot, pre_ref, df_ref, h_ref, dr_ref, sem, out_sem = refs[14:]
    blocks = (w.shape[0] - 1) // 2
    mine = block(meta[CORE], TOK)
    loads = Copies(sem)
    wait(
        [
            loads.start(src.at[mine], cot.at[:, block(at, HALF)])
            for src, at in ((cot_own, meta[CORE]), (cot_oth, 1 - meta[CORE]))
        ]
    )
    ng[...] = jnp.zeros_like(ng)

    def step(i):
        rows = block(i, BLK)
        dy = cot[rows, :].astype(F32)
        dr3, gain3, bias3 = norm_backward(dy, n3_ref[rows, :], r_ref[rows, HD : HD + 1], norm[2:3, :])
        df = dr3.astype(BF)
        df_ref[rows, :] = df
        dh2 = dr3
        for b in range(blocks):
            dpre = (dot(df, w[1 + blocks + b]) * slope_ref[b, rows, :].astype(F32)).astype(BF)
            pre_ref[b, rows, :] = dpre
            dh2 = dh2 + dot_nt(dpre, w[1 + b])
        n2 = n2_ref[rows, :]
        h_ref[rows, :] = (n2 * norm[1:2, :] + norm[4:5, :]).astype(BF)
        dr2, gain2, bias2 = norm_backward(dh2, n2, r_ref[rows, 0:1], norm[1:2, :])
        dr_ref[rows, :] = dr2
        ng[1:2, :] += gain2
        ng[2:3, :] += gain3
        ng[4:5, :] += bias2
        ng[5:6, :] += bias3

    loop(TOK // BLK, step)
    flying = Copies(out_sem).start(dr_ref, dr_far)
    h_t = h_ref[...].T
    for b in range(blocks):
        put_grad(g_own, g_oth, b, dot(h_t, pre_ref[b]))
    df_t = df_ref[...].T
    for b in range(blocks):
        put_grad(g_own, g_oth, blocks + b, dot(df_t, act_ref[b]))
    flying.wait()


def ffn_backward(meta, norm, w, act, slope, n2, n3, rstd, cot_own, cot_oth, deps=()):
    blocks = act.shape[0]
    grad = sds((PIECES, 2 * blocks, CH, HALF))
    return call(
        ffn_backward_body,
        (grad, grad, sds((8, D), F32)),
        (meta, norm, w, act, slope, n2, n3, rstd),
        (cot_own, cot_oth),
        (full(F32),),
        deps=deps,
        scratch=[
            pltpu.VMEM(ROWS_BF, BF),
            pltpu.VMEM((blocks, TOK, D), BF),
            pltpu.VMEM(ROWS_BF, BF),
            pltpu.VMEM(ROWS_BF, BF),
            pltpu.VMEM((TOK, D), F32),
            sems(2),
            sems(1),
        ],
        us=14,
        mb=28,
    )


def fetch(sem, pairs):
    copies = Copies(sem)
    started = [copies.start(src, dst) for src, dst in pairs]
    return lambda *at: wait([started[k] for k in at])


def cross_backward_body(*refs):
    meta, norm, ng_in, lse = refs[:4]
    dr_in_far, q_far, k_far, v_far, m_far, n_far, r_far, po_far, enc_own, enc_oth = refs[4:14]
    pieces = refs[14:22]
    dr_ref, g_own, g_oth, ng, dr_far, dk_far, dv_far = refs[22:29]
    q, k, v, m, enc, n, r, w, po, da, dm, dq, dk, dv, h, dr_in, in_sem, out_sem, w_sem, enc_sem = refs[29:]
    ready = fetch(
        in_sem,
        ((po_far, po), (q_far, q), (k_far, k), (v_far, v), (n_far, n), (r_far, r), (m_far, m), (dr_in_far, dr_in)),
    )
    weights = load_weights(meta, pieces, w, w_sem, 4, 1, 0)
    rows_in = load_rows(meta, enc_own, enc_oth, enc, enc_sem)
    outs = Copies(out_sem)
    ready(7)
    da[...] = dr_in[...].astype(BF)
    ready(0)
    dm[...] = dot(da[...], po[...]).astype(BF)
    ready(1, 2, 3)
    attention_backward(meta, q, k, v, lse, dm, dq, dk, dv, source_segments_of)
    flying = [outs.start(dk, dk_far), outs.start(dv, dv_far)]
    ng[...] = ng_in[...]
    ready(4, 5)
    wait(weights)

    def step(i):
        rows = block(i, BLK)
        normed = n[rows, :]
        h[rows, :] = (normed * norm[0:1, :] + norm[3:4, :]).astype(BF)
        dh1 = dr_in[rows, :] + dot_nt(dq[rows, :], w[0])
        dr1, gain1, bias1 = norm_backward(dh1, normed, r[rows, 0:1], norm[0:1, :])
        dr_ref[rows, :] = dr1
        ng[0:1, :] += gain1
        ng[3:4, :] += bias1

    loop(TOK // BLK, step)
    flying.append(outs.start(dr_ref, dr_far))
    ready(6)
    wait(rows_in)
    put_grad(g_own, g_oth, 0, dot_tn(da[...], m[...]))
    put_grad(g_own, g_oth, 1, dot_tn(h[...], dq[...]))
    put_grad(g_own, g_oth, 2, dot_tn(enc[...], dk[...]))
    put_grad(g_own, g_oth, 3, dot_tn(enc[...], dv[...]))
    total = jnp.concatenate([ng[...], jnp.zeros((CH - 8, D), F32)], 0).astype(BF)
    for c in range(PIECES):
        part = total[:, :HALF] if c < PIECES // 2 else total[:, HALF:]
        g_own[c, 4] = part
        g_oth[c, 4] = part
    wait(flying)


def cross_backward(meta, dr2, norm, ng, lse, saved, pieces, deps=()):
    grad = sds((PIECES, 5, CH, HALF))
    rows = pltpu.VMEM(ROWS_BF, BF)
    return call(
        cross_backward_body,
        (full(F32), grad, grad, sds((8, D), F32)),
        (meta, norm, ng, lse),
        (dr2,) + saved + tuple(pieces),
        (full(F32), full(), full()),
        deps,
        [rows] * 5
        + [pltpu.VMEM((TOK, D), F32), pltpu.VMEM((TOK, PACK), F32), pltpu.VMEM((1, D, D), BF), pltpu.VMEM((D, D), BF)]
        + [rows] * 6
        + [pltpu.VMEM((TOK, D), F32), sems(8), sems(3), sems(8), sems(2)],
        us=12,
        mb=46,
    )


def self_backward_body(*refs):
    meta, dr_in, lse = refs[:3]
    q_far, k_far, v_far, m_far, tok_own, tok_oth = refs[3:9]
    pieces = refs[9:17]
    g_own, g_oth, dq_far, dk_far, dv_far, q, k, v, m, x, w, da, dm, dq, dk, dv, in_sem, w_sem, x_sem, out_sem = refs[17:]
    weights = load_weights(meta, pieces, w, w_sem, 3, 1, 0)
    ready = fetch(in_sem, ((q_far, q), (k_far, k), (v_far, v), (m_far, m)))
    rows_in = load_rows(meta, tok_own, tok_oth, x, x_sem)
    da[...] = dr_in[...].astype(BF)
    wait(weights)
    dm[...] = dot(da[...], w[0]).astype(BF)
    ready(0, 1, 2)
    attention_backward(meta, q, k, v, lse, dm, dq, dk, dv, target_segments)
    outs = Copies(out_sem)
    flying = [outs.start(dq, dq_far), outs.start(dk, dk_far), outs.start(dv, dv_far)]
    ready(3)
    wait(rows_in)
    put_grad(g_own, g_oth, 0, dot_tn(da[...], m[...]))
    put_grad(g_own, g_oth, 1, dot_tn(x[...], dq[...]))
    put_grad(g_own, g_oth, 2, dot_tn(x[...], dk[...]))
    put_grad(g_own, g_oth, 3, dot_tn(x[...], dv[...]))
    wait(flying)


def self_backward(meta, dr1, lse, saved, pieces, deps=()):
    grad = sds((PIECES, 4, CH, HALF))
    rows = pltpu.VMEM(ROWS_BF, BF)
    return call(
        self_backward_body,
        (grad, grad),
        (meta, dr1, lse),
        saved + tuple(pieces),
        (full(), full(), full()),
        deps,
        [rows] * 5 + [pltpu.VMEM((1, D, D), BF)] + [rows] * 5 + [sems(4), sems(8), sems(2), sems(3)],
        us=10,
        mb=46,
    )


def inputs_backward_body(*refs):
    meta = refs[0]
    pieces = refs[7:15]
    x_own, x_oth, e_own, e_oth, dr, dq, dk, dv, dk2, dv2, w, w2, in_sem, w_sem, w2_sem = refs[15:]
    ready = fetch(in_sem, tuple(zip(refs[1:7], (dr, dq, dk, dv, dk2, dv2))))
    weights = load_weights(meta, pieces, w, w_sem, 0, 3) + load_weights(meta, pieces, w2, w2_sem, 5, 2, 0)
    wait(weights)
    ready(*range(6))

    def step(i):
        rows = block(i, BLK)
        dx = dr[rows, :] + dot_nt(dq[rows, :], w[0]) + dot_nt(dk[rows, :], w[1]) + dot_nt(dv[rows, :], w[2])
        x_own[rows, :], x_oth[rows, :] = halves(meta, dx.astype(BF))
        de = dot_nt(dk2[rows, :], w2[0]) + dot_nt(dv2[rows, :], w2[1])
        e_own[rows, :], e_oth[rows, :] = halves(meta, de.astype(BF))

    loop(TOK // BLK, step)


def inputs_backward(meta, saved, pieces, deps=()):
    rows = pltpu.VMEM(ROWS_BF, BF)
    return call(
        inputs_backward_body,
        (sds((TOK, HALF)),) * 4,
        (meta,),
        saved + tuple(pieces),
        (),
        deps,
        [pltpu.VMEM((TOK, D), F32)] + [rows] * 5 + [pltpu.VMEM((3, D, D), BF), pltpu.VMEM((2, D, D), BF)]
        + [sems(6), sems(8), sems(8)],
        us=5,
        mb=46,
    )


def place_body(meta, own, oth, out):
    for side, src in enumerate((own, oth)):
        for j in range(SLOTS):
            out[block(meta[ROW + SLOTS * side + j], PACK), :] = src[j * PACK : (j + 1) * PACK, :]


def join_body(meta, own, oth, out):
    out[block(meta[CORE], TOK), :] = own[...]
    out[block(1 - meta[CORE], TOK), :] = oth[...]


def copy_body(src, out):
    out[...] = src[...]


def copy_after(value, deps):
    return call(copy_body, (sds(value.shape),), (value,), deps=deps)[0]


BOTH = (2 * TOK, HALF)


def add(a, b):
    return (a.astype(F32) + b.astype(F32)).astype(BF)


def pair_sum_body(meta, own, rec, *outs):
    for k in range(4):
        for j in range(4):
            c = meta[PIECE + 4 * k + j]
            total = add(own[c], rec[c])
            if len(outs) == 4:
                outs[k][j] = total
            elif k < 2:
                outs[k][j] = total
            else:
                outs[2][k - 2, j] = total


def pair_sum(meta, own, rec, joined, deps=()):
    shape = (4,) + own.shape[1:]
    outs = (sds(shape), sds(shape), sds((2,) + shape)) if joined else (sds(shape),) * 4
    return call(pair_sum_body, outs, (meta, own, rec), deps=deps)


def stage_sum_body(a0, a1, b, keep, send):
    keep[...] = add(a0[...], b[0])
    send[...] = add(a1[...], b[1])


def last_line_body(at, a, b, *outs):
    for j in range(4):
        k = at[0] ^ j
        outs[j][...] = add(a[k], b[k])


def tail_sum_body(at, kc, rc, s0, s1, s2, s3, *outs):
    mats = kc.shape[1]
    for j in range(4):
        k = at[0] ^ j
        outs[j][:mats] = add(kc[k], rc[k])
        total = s0[k].astype(F32) + s1[k].astype(F32) + (s2[k].astype(F32) + s3[k].astype(F32))
        outs[j][mats:] = total.astype(BF)


def adam_attention_body(*refs):
    parts, state, outs = refs[:4], refs[4:10], refs[10:]
    total = [ref[...].astype(F32) for ref in parts]
    g = (total[0] + total[1]) + (total[2] + total[3])
    grads = (jnp.concatenate([g[6:9], g[1:4]], 0), jnp.concatenate([g[5:6], g[0:1]], 0))
    for k, grad in enumerate(grads):
        weight, first, second = (ref[...] for ref in state[3 * k : 3 * k + 3])
        outs[3 * k][...], outs[3 * k + 1][...], outs[3 * k + 2][...] = adam(
            weight, first, second, grad, rate_matrix, decay_matrix
        )
    outs[6][...] = g[4, :8]


def adam_ffn_body(z, *refs):
    state, outs = refs[:6], refs[6:]
    g = (z[0].astype(F32) + z[1].astype(F32)) + (z[2].astype(F32) + z[3].astype(F32))
    blocks = g.shape[0] // 2
    for k in range(2):
        for b in range(blocks):
            cols = slice(b * HALF, (b + 1) * HALF)
            weight, first, second = (ref[:, cols] for ref in state[3 * k : 3 * k + 3])
            outs[3 * k][:, cols], outs[3 * k + 1][:, cols], outs[3 * k + 2][:, cols] = adam(
                weight, first, second, g[k * blocks + b], rate_matrix, decay_matrix
            )


def adam(weight, first_old, second_old, grad, rate, decay):
    first_new = beta_first * first_old + (1.0 - beta_first) * grad
    second_new = beta_second * second_old + (1.0 - beta_second) * grad * grad
    first_hat = first_new / (1.0 - beta_first**STEP)
    second_hat = second_new / (1.0 - beta_second**STEP)
    updated = weight - rate * (first_hat / (jnp.sqrt(second_hat) + adam_epsilon) + decay * weight)
    return (first_new, second_new, updated)


def swap(value):
    return lax.ppermute(value, "narrow", [(0, 1), (1, 0)])


def peer(value, mask, mask_one=None):
    masks = (mask, mask if mask_one is None else mask_one)
    chips = lax.axis_size("wide")
    route = [(2 * i + c, 2 * (i ^ masks[c]) + c) for i in range(chips) for c in range(2)]
    return lax.ppermute(value, ("wide", "narrow"), route)


def along_z(parts):
    plane = lax.axis_size("wide") // 4
    lines = [[at + plane * j for j in range(4)] for at in range(plane)]
    return lax.all_to_all(parts, "wide", 0, 0, axis_index_groups=lines)


def local(
    tokens,
    encoded,
    cotangent,
    target_lengths,
    source_segments,
    send_rows,
    proj_in,
    proj_out,
    ffn_in,
    ffn_out,
    norm_par,
    proj_in_moment,
    proj_in_square,
    proj_out_moment,
    proj_out_square,
    ffn_in_moment,
    ffn_in_square,
    ffn_out_moment,
    ffn_out_square,
    norm_moment,
    norm_square,
):
    wide_count = lax.axis_size("wide")
    w = lax.axis_index("wide")
    n = lax.axis_index("narrow")
    rows_dev = tokens.shape[0] // PACK
    stride = wide_count // rows_dev
    share = proj_in.shape[1]
    blocks = ffn_in.shape[1] // HALF
    direct = share == CH

    places = jnp.arange(rows_dev, dtype=jnp.int32)
    slot_rows = lax.dynamic_index_in_dim(send_rows, w, 0, keepdims=False)[places * stride + w % stride]
    mine = lax.dynamic_slice_in_dim(slot_rows, n * SLOTS, SLOTS)
    theirs = lax.dynamic_slice_in_dim(slot_rows, (1 - n) * SLOTS, SLOTS)
    mine_global = w * rows_dev + mine
    lengths = target_lengths[mine_global]
    if direct:
        orders = jnp.array([[a for a in order for _ in range(4)] for order in ((0, 1, 2, 3), (0, 2, 1, 3))])
        in_plane = jnp.concatenate([orders[n], orders[1 - n]]) ^ (w % 4)
        piece_ids = in_plane + 4 * (jnp.arange(2 * PIECES, dtype=jnp.int32) % 4)
    else:
        piece_ids = jnp.tile(jnp.arange(PIECES, dtype=jnp.int32), 2)
    cut = jnp.sum((source_segments[mine_global] == 0).astype(jnp.int32), 1)
    meta = jnp.concatenate(
        [n[None], piece_ids, mine, theirs, lengths[:, 0], lengths[:, 0] + lengths[:, 1], cut]
    ).astype(jnp.int32)

    tok_rows = (tokens, swap(tokens))
    enc_rows = (encoded, swap(encoded))
    pout_t = proj_out.transpose(0, 2, 1)
    wout_t = ffn_out.T
    out_moment, out_square = proj_out_moment.transpose(0, 2, 1), proj_out_square.transpose(0, 2, 1)

    if direct:
        g0 = call(
            pack_attention_body,
            (sds((8, CH, HALF)),),
            (),
            (proj_in, pout_t, norm_par),
            scratch=[pltpu.VMEM(a, F32) for a in (proj_in.shape, (CH, HALF), norm_par.shape)] + [sems(3)],
            us=2,
        )[0]
        line = [peer(g0, 4 * k) for k in (1, 2, 3)]
        z0 = call(
            stack_body,
            (sds((4, 8, CH, HALF)),),
            ((w // 4)[None], g0, *line),
            deps=(meta, tok_rows[1], enc_rows[1]),
        )[0]
        first0 = peer(z0, 1, 2)
        second0 = peer(z0, 2, 1)
        g1 = call(
            pack_ffn_body,
            (sds((4, 1 + 2 * blocks, CH, HALF)),),
            (pout_t, ffn_in, wout_t),
            deps=(z0,),
            us=2,
        )[0]
        z1 = along_z(g1)
        third0 = peer(copy_after(first0, (z1, second0)), 2, 1)
        pieces0 = [z0, first0, second0, third0]
        first1 = peer(z1, 1, 2)
        second1 = peer(z1, 2, 1)
        pieces1 = [z1, first1, second1]
        pieces = [own + [swap(a) for a in own] for own in (pieces0, pieces1)]
        cotangent = copy_after(cotangent, (third0,))
    else:
        low_in = lax.all_gather(proj_in.astype(BF), "wide", axis=1, tiled=True)
        low_out = lax.all_gather(proj_out.astype(BF), "wide", axis=2, tiled=True).transpose(0, 2, 1)
        low_win = lax.all_gather(ffn_in.astype(BF), "wide", axis=0, tiled=True)
        low_wout = lax.all_gather(ffn_out.astype(BF), "wide", axis=1, tiled=True).T
        low_norm = lax.all_gather(norm_par.astype(BF), "wide", axis=1, tiled=True)

        def column_blocks(a):
            return a.reshape(D, blocks, HALF).transpose(1, 0, 2)

        tiled = jnp.tile(low_norm.reshape(6, PIECES, CH).transpose(1, 0, 2), (1, 1, HALF // CH))
        norm_mat = jnp.pad(tiled, ((0, 0), (0, CH - 6), (0, 0))).reshape(1, D, HALF)
        groups = (
            jnp.concatenate([low_in[:3], low_out[:1], low_in[3:], norm_mat]),
            jnp.concatenate([low_out[1:], column_blocks(low_win), column_blocks(low_wout)]),
        )
        pieces = []
        for group in groups:
            cut = group.reshape(-1, PIECES, CH, HALF).transpose(1, 0, 2, 3)
            own = [cut[4 * k : 4 * k + 4] for k in range(4)]
            pieces.append(own + [swap(a) for a in own])

    everyone = [[r + stride * j for j in range(rows_dev)] for r in range(stride)]

    def exchange(rows):
        return lax.all_to_all(
            rows.reshape(rows_dev, PACK, HALF), "wide", 0, 0, axis_index_groups=everyone
        ).reshape(rows_dev * PACK, HALF)

    cot_own = exchange(cotangent)
    cot_oth = swap(cot_own)
    m2, lse1, lse2, norm, q1, k1, v1, m1, n1, rstd1, q2, k2, v2 = attention_layers(
        meta, tok_rows + enc_rows, pieces[0]
    )
    if direct:
        third1 = peer(copy_after(first1, (lse2, second1)), 2, 1)
        pieces[1] = pieces[1][:3] + [third1] + pieces[1][3:] + [swap(third1)]
    out_own, out_oth, w_ffn, act, slope, n2, n3, rstd, m2_far, po2 = ffn_forward(meta, n1, m2, norm, pieces[1])
    joined = call(join_body, (sds(BOTH),), (meta, out_own, swap(out_oth)))[0]
    gf_own, gf_oth, ng, dr2 = ffn_backward(
        meta, norm, w_ffn, act, slope, n2, n3, rstd, cot_own, cot_oth, (joined,)
    )
    layer_out = copy_after(exchange(joined), ())
    early = ()
    if direct:
        sf = pair_sum(meta, gf_own, swap(gf_oth), True)
        early = (sf[2],)
    dr1, gc_own, gc_oth, ng, dr1_far, dk2, dv2 = cross_backward(
        meta, dr2, norm, ng, lse2, (q2, k2, v2, m2_far, n1, rstd1, po2) + enc_rows, pieces[0], early
    )
    if direct:
        kf, send_f = call(stage_sum_body, (sds(sf[0].shape),) * 2, (sf[0], sf[1], peer(sf[2], 2, 1)))
        sc = pair_sum(meta, gc_own, swap(gc_oth), True)
    gs_own, gs_oth, dq1, dk1, dv1 = self_backward(
        meta, dr1, lse1, (q1, k1, v1, m1) + tok_rows, pieces[0]
    )
    early = ()
    if direct:
        at_z = (w // 4)[None]
        ss = pair_sum(meta, gs_own, swap(gs_oth), False, (sc[2],))
        zf = call(last_line_body, (sds(kf.shape[1:]),) * 4, (at_z, kf, peer(send_f, 1, 2)), deps=(ss[1],))
        zf = jnp.stack([zf[0]] + [peer(zf[k], 4 * k) for k in (1, 2, 3)])
        early = (ss[1], layer_out)
    dx_own, dx_oth, de_own, de_oth = inputs_backward(
        meta, (dr1_far, dq1, dk1, dv1, dk2, dv2), pieces[0], early
    )
    tokens_grad = call(place_body, (sds(BOTH),), (meta, dx_own, swap(dx_oth)))[0]
    encoded_grad = call(place_body, (sds(BOTH),), (meta, de_own, swap(de_oth)))[0]

    if direct:
        kc, send_c = call(
            stage_sum_body, (sds(sc[0].shape),) * 2, (sc[0], sc[1], peer(sc[2], 2, 1)), deps=(dx_own,)
        )
        line = call(
            tail_sum_body,
            (sds((kc.shape[1] + ss[0].shape[1], CH, HALF)),) * 4,
            (at_z, kc, peer(send_c, 1, 2), ss[0], peer(ss[1], 1, 2), peer(ss[2], 2, 1), peer(ss[3], 3)),
        )
        line = [line[0]] + [peer(line[k], 4 * k) for k in (1, 2, 3)]
        pairs = ((proj_in, proj_in_moment, proj_in_square), (pout_t, out_moment, out_square))
        wide_pairs = ((ffn_in, ffn_in_moment, ffn_in_square), (wout_t, ffn_out_moment.T, ffn_out_square.T))

        def news(group):
            return tuple(sds(a.shape, F32) for triple in group for a in triple)

        upd = call(adam_ffn_body, news(wide_pairs), (zf,) + wide_pairs[0] + wide_pairs[1], us=2)
        upd_expand, upd_reduce = upd[:3], tuple(u.T for u in upd[3:])
        upd = call(
            adam_attention_body,
            news(pairs) + (sds((8, HALF), F32),),
            tuple(line) + pairs[0] + pairs[1],
            deps=(tokens_grad, encoded_grad, upd[0]),
            us=2,
        )
        upd_in, upd_out = upd[:3], tuple(u.transpose(0, 2, 1) for u in upd[3:6])
        norm_half = upd[6][:6]
        norm_half = jnp.where(n == 0, norm_half, swap(norm_half))
        norm_grad = lax.dynamic_slice_in_dim(norm_half, (w % (HALF // CH)) * CH, CH, 1)
    else:

        def summed(own, oth):
            total = (own.astype(F32) + swap(oth).astype(F32)).astype(BF)
            total = total.transpose(1, 0, 2, 3).reshape(-1, D, HALF)
            return lax.psum_scatter(total, "wide", scatter_dimension=1, tiled=True).astype(F32)

        gf, gc, gs = summed(gf_own, gf_oth), summed(gc_own[:, :4], gc_oth[:, :4]), summed(gs_own, gs_oth)
        norm_all = lax.psum(ng, ("wide", "narrow"))[:6]
        norm_grad = lax.dynamic_slice_in_dim(norm_all, w * share, share, 1)

        grad_in = jnp.concatenate([gs[1:4], gc[1:4]])
        grad_out = jnp.stack([gs[0], gc[0]])
        grad_expand = gf[:blocks].transpose(1, 0, 2).reshape(share, blocks * HALF)
        grad_reduce = gf[blocks:].transpose(1, 0, 2).reshape(share, blocks * HALF)
        upd_in = adam(proj_in, proj_in_moment, proj_in_square, grad_in, rate_matrix, decay_matrix)
        upd_out = adam(pout_t, out_moment, out_square, grad_out, rate_matrix, decay_matrix)
        upd_out = tuple(u.transpose(0, 2, 1) for u in upd_out)
        upd_expand = adam(ffn_in, ffn_in_moment, ffn_in_square, grad_expand, rate_matrix, decay_matrix)
        upd_reduce = adam(
            wout_t, ffn_out_moment.T, ffn_out_square.T, grad_reduce, rate_matrix, decay_matrix
        )
        upd_reduce = tuple(u.T for u in upd_reduce)
    upd_norm = adam(norm_par, norm_moment, norm_square, norm_grad, rate_norm, 0.0)
    return (layer_out, tokens_grad, encoded_grad) + upd_in + upd_out + upd_expand + upd_reduce + upd_norm


def solution(mesh):
    rows = P("wide", "narrow")
    p_in = P(None, "wide", "narrow")
    p_out = P(None, "narrow", "wide")
    p_expand = P("wide", "narrow")
    p_reduce = P("narrow", "wide")
    p_norm = P(None, "wide")
    weights = (p_in, p_out, p_expand, p_reduce, p_norm)
    in_specs = (rows,) * 3 + (P(),) * 3 + weights + tuple(s for s in weights for _ in range(2))
    out_specs = (rows,) * 3 + tuple(s for s in weights for _ in range(3))
    return jax.shard_map(local, mesh=mesh, in_specs=in_specs, out_specs=out_specs, check_vma=False)
```

```python
import functools
import math

import jax
import jax.numpy as jnp
from jax import lax
from jax.experimental import pallas as pl
from jax.experimental.pallas import tpu as pltpu
from jax.sharding import PartitionSpec as P

D = 512
H = 8
HD = D // H
PACK = 128
STEP = 5
CH = 32
HALF = D // 2
PIECES = D // CH
SLOTS = 8
TOK = SLOTS * PACK
BLK = 1024

norm_epsilon = 1e-05
beta_first = 0.9
beta_second = 0.98
adam_epsilon = 1e-08
rate_matrix = 0.1
rate_norm = 0.5
decay_matrix = 0.01
masked_score = -1e30

CORE = 0
PIECE = 1
ROW = PIECE + 2 * PIECES
FIRST = ROW + 2 * SLOTS
SECOND = FIRST + SLOTS
CUT = SECOND + SLOTS

BF = jnp.bfloat16
F32 = jnp.float32


def dot(a, b):
    return jnp.dot(a, b, preferred_element_type=F32)


def dot_nt(a, b):
    return lax.dot_general(a, b, (((1,), (1,)), ((), ())), preferred_element_type=F32)


def dot_tn(a, b):
    return lax.dot_general(a, b, (((0,), (0,)), ((), ())), preferred_element_type=F32)


def sds(shape, dtype=BF):
    return jax.ShapeDtypeStruct(shape, dtype)


def cost(us):
    return pl.CostEstimate(flops=us * 10**9, bytes_accessed=us * 3 * 10**6, transcendentals=0)


def call(body, outs, operands, far=(), far_outs=(), deps=(), scratch=(), us=1, mb=16):
    count = len(operands) + len(far)

    def run(*refs):
        body(*refs[:count], *refs[count + len(deps) :])

    vmem = pl.BlockSpec(memory_space=pltpu.VMEM)
    hbm = pl.BlockSpec(memory_space=pltpu.HBM)
    smem = pl.BlockSpec(memory_space=pltpu.SMEM)
    specs = [smem if o.dtype == jnp.int32 and o.ndim == 1 else vmem for o in operands]
    return pl.pallas_call(
        run,
        in_specs=specs + [hbm] * len(far) + [ANY] * len(deps),
        out_specs=(vmem,) * len(outs) + (hbm,) * len(far_outs),
        out_shape=tuple(outs) + tuple(far_outs),
        scratch_shapes=list(scratch),
        cost_estimate=cost(us),
        compiler_params=pltpu.CompilerParams(vmem_limit_bytes=mb * 2**20),
    )(*operands, *far, *deps)


def sems(count):
    return pltpu.SemaphoreType.DMA((count,))


class Copies:
    def __init__(self, sem):
        self.sem, self.count = sem, 0

    def start(self, src, dst):
        c = pltpu.make_async_copy(src, dst, self.sem.at[self.count])
        self.count += 1
        c.start()
        return c


def wait(copies):
    for c in copies:
        c.wait()


ANY = pl.BlockSpec(memory_space=pl.ANY)


def block(i, size):
    return pl.ds(pl.multiple_of(i * size, size), size)


def loop(count, body, unroll=1):
    def step(i, carry):
        body(i)
        return carry

    lax.fori_loop(0, count, step, 0, unroll=unroll)


def eye_of(rows, columns):
    at = [lax.broadcasted_iota(jnp.int32, (rows, columns), d) for d in range(2)]
    return (at[0] == at[1] % CH).astype(BF)


def pack_attention_body(pin_far, pout_far, norm_far, g, pin, pout, norm, sem):
    loads = Copies(sem)
    wait([loads.start(pin_far, pin), loads.start(pout_far.at[0], pout), loads.start(norm_far, norm)])
    rows = dot(eye_of(CH, 6), norm[...].astype(BF)).astype(BF)
    rows = dot(rows, eye_of(CH, HALF)).astype(BF)
    g[0:3] = pin[0:3].astype(BF)
    g[3] = pout[...].astype(BF)
    g[4:7] = pin[3:6].astype(BF)
    g[7] = rows


def pack_ffn_body(pout, win, wout, g):
    blocks = win.shape[1] // HALF
    for to in range(4):
        g[to, 0] = pout[1].astype(BF)
        for b in range(blocks):
            g[to, 1 + b] = win[:, b * HALF : (b + 1) * HALF].astype(BF)
            g[to, 1 + blocks + b] = wout[:, b * HALF : (b + 1) * HALF].astype(BF)


def stack_body(at, *refs):
    for j in range(4):
        refs[4][at[0] ^ j] = refs[j][...]


def load_weights(meta, pieces, w_ref, sem, first=0, count=None, at=None):
    at = first if at is None else at
    count = w_ref.shape[0] - at if count is None else count
    copies = []
    for a, piece in enumerate(pieces):
        half, group = divmod(a, len(pieces) // 2)
        per = piece.shape[0]
        for j in range(per):
            row = pl.multiple_of(meta[PIECE + half * PIECES + group * per + j] * CH, CH)
            copies.append(
                pltpu.make_async_copy(
                    piece.at[j, pl.ds(first, count)],
                    w_ref.at[pl.ds(at, count), pl.ds(row, CH), pl.ds(half * HALF, HALF)],
                    sem.at[a],
                )
            )
    for c in copies:
        c.start()
    return copies


def load_rows(meta, own, oth, dst, sem):
    copies = []
    for side, src in enumerate((own, oth)):
        at = meta[CORE] if side == 0 else 1 - meta[CORE]
        for j in range(SLOTS):
            copies.append(
                pltpu.make_async_copy(
                    src.at[block(meta[ROW + j], PACK)],
                    dst.at[pl.ds(j * PACK, PACK), block(at, HALF)],
                    sem.at[side],
                )
            )
    for c in copies:
        c.start()
    return copies


def lane_masks():
    low = (lax.broadcasted_iota(jnp.int32, (1, PACK), 1) < HD).astype(F32)
    return low.astype(BF), (1.0 - low).astype(BF)


def low_lanes(rows=PACK):
    return lax.broadcasted_iota(jnp.int32, (rows, PACK), 1) < HD


def two_heads(rows, low, high):
    return jnp.concatenate([rows * low, rows * high], 0)


def norm_forward(r):
    center = r - jnp.mean(r, -1, keepdims=True)
    rstd = lax.rsqrt(jnp.mean(center * center, -1, keepdims=True) + norm_epsilon)
    return center * rstd, rstd


def norm_backward(dy, n, rstd, gain):
    dn = dy * gain
    dr = rstd * (dn - jnp.mean(dn, -1, keepdims=True) - n * jnp.mean(dn * n, -1, keepdims=True))
    return dr, jnp.sum(dy * n, 0, keepdims=True), jnp.sum(dy, 0, keepdims=True)


def target_segments(meta, slot, dim):
    at = lax.broadcasted_iota(jnp.int32, (PACK, PACK), dim)
    one = (at >= meta[FIRST + slot]).astype(jnp.int32)
    return one + (at >= meta[SECOND + slot]).astype(jnp.int32)


def source_segments_of(meta, slot, dim):
    return (lax.broadcasted_iota(jnp.int32, (PACK, PACK), dim) >= meta[CUT + slot]).astype(jnp.int32)


def halves(meta, full):
    first = meta[CORE] == 0
    lo, hi = full[:, :HALF], full[:, HALF:]
    return jnp.where(first, lo, hi), jnp.where(first, hi, lo)


def mask_of(meta, slot, key_segments):
    mask = key_segments(meta, slot, 0) == target_segments(meta, slot, 1)
    return jnp.concatenate([mask, mask], 1)


def pairs_of(meta, first, count, key_segments):
    pairs = []
    for slot in [first + j for j in range(count)]:
        mask = mask_of(meta, slot, key_segments)
        rows = block(slot, PACK)
        for h in range(H // 2):
            pairs.append((rows, slice(h * PACK, (h + 1) * PACK), mask, (slot, slice(h, h + 1))))
    return pairs


def attention_forward(meta, q, k, v, lse, m, key_segments):
    low, high = lane_masks()
    scale = HD**-0.5
    slots = 2

    def step(i):
        pairs = pairs_of(meta, i * slots, slots, key_segments)
        s = [
            jnp.where(mask, dot_nt(k[r, c], two_heads(q[r, c], low * scale, high * scale)), masked_score)
            for r, c, mask, _ in pairs
        ]
        peak = [jnp.max(one, 0, keepdims=True) for one in s]
        e = [jnp.exp(one - top) for one, top in zip(s, peak)]
        total = [jnp.sum(one, 0, keepdims=True) for one in e]
        p = [(one * (1.0 / all_keys)).astype(BF) for one, all_keys in zip(e, total)]
        for (_, _, _, (slot, h)), top, all_keys in zip(pairs, peak, total):
            lse[slot, h, :] = top + jnp.log(all_keys)
        for (r, c, _, _), one in zip(pairs, p):
            mixed = dot_tn(v[r, c], one).astype(BF)
            m[r, c] = jnp.concatenate([mixed[:HD, :PACK], mixed[HD:, PACK:]], 0).T

    loop(SLOTS // slots, step, 4)


def attention_backward(meta, q, k, v, lse, dm, dq, dk, dv, key_segments):
    low, high = lane_masks()
    pick = low_lanes()
    scale = HD**-0.5

    def step(i):
        pairs = pairs_of(meta, i, 1, key_segments)
        qs = [two_heads(q[r, c], low * scale, high * scale) for r, c, _, _ in pairs]
        s = [dot_nt(k[r, c], one) for (r, c, _, _), one in zip(pairs, qs)]
        dms = [two_heads(dm[r, c], low, high) for r, c, _, _ in pairs]
        dp = [dot_nt(v[r, c], one) for (r, c, _, _), one in zip(pairs, dms)]
        p = [
            jnp.exp(jnp.where(mask, one, masked_score) - lse[slot, h, :])
            for (_, _, mask, (slot, h)), one in zip(pairs, s)
        ]
        for (r, c, _, _), one, grad in zip(pairs, p, dms):
            dv[r, c] = dot(one.astype(BF), grad).astype(BF)
        ds = [
            (one * (grad - jnp.sum(one * grad, 0, keepdims=True))).astype(BF) for one, grad in zip(p, dp)
        ]
        for (r, c, _, _), one, two in zip(pairs, ds, qs):
            dk[r, c] = dot(one, two).astype(BF)
        for (r, c, _, _), one in zip(pairs, ds):
            both = dot_tn(one, k[r, c])
            dq[r, c] = (jnp.where(pick, both[:PACK], both[PACK:]) * scale).astype(BF)

    loop(SLOTS, step, 4)


ROWS_BF = (TOK, D)
TOTALS = (SLOTS, 8, 2 * PACK)


def full(dtype=BF):
    return sds((TOK, D), dtype)


def attention_layers_body(*refs):
    meta, tok_own, tok_oth, enc_own, enc_oth = refs[:5]
    pieces = refs[5:13]
    m2, lse1, lse2, norm = refs[13:17]
    q1_far, k1_far, v1_far, m1_far, n_far, r_far, q2_far, k2_far, v2_far = refs[17:26]
    w, x, enc, q1, k1, v1, m1, h, q2, k2, v2, n_ref, r_ref, x_sem, enc_sem, w_sem, out_sem = refs[26:]
    loads = load_rows(meta, tok_own, tok_oth, x, x_sem)
    loads += load_weights(meta, pieces, w, w_sem.at[0], 0, 3)
    rest = load_weights(meta, pieces, w, w_sem.at[1], 3)
    rest += load_rows(meta, enc_own, enc_oth, enc, enc_sem)
    wait(loads)
    outs = Copies(out_sem)
    q1[...] = dot(x[...], w[0]).astype(BF)
    k1[...] = dot(x[...], w[1]).astype(BF)
    v1[...] = dot(x[...], w[2]).astype(BF)
    flying = [outs.start(q1, q1_far), outs.start(k1, k1_far), outs.start(v1, v1_far)]
    attention_forward(meta, q1, k1, v1, lse1, m1, target_segments)
    flying.append(outs.start(m1, m1_far))
    wait(rest)
    lane = lax.broadcasted_iota(jnp.int32, (8, HALF), 1) // CH
    for half in range(2):
        total = jnp.zeros((8, HALF), F32)
        for j in range(PIECES // 2):
            at = (half * (PIECES // 2) + j) * CH
            part = w[7, at : at + 16, :HALF][:8].astype(F32)
            total = total + jnp.where(lane == j, part, 0.0)
        norm[:, half * HALF : (half + 1) * HALF] = total
    k2[...] = dot(enc[...], w[5]).astype(BF)
    v2[...] = dot(enc[...], w[6]).astype(BF)

    def step(i):
        rows = block(i, BLK)
        n, rstd = norm_forward(x[rows, :].astype(F32) + dot_nt(m1[rows, :], w[3]))
        n_ref[rows, :] = n
        r_ref[rows, :] = jnp.broadcast_to(rstd, (BLK, PACK))
        h[rows, :] = (n * norm[0:1, :] + norm[3:4, :]).astype(BF)

    loop(TOK // BLK, step)
    q2[...] = dot(h[...], w[4]).astype(BF)
    flying += [
        outs.start(src, dst)
        for src, dst in ((k2, k2_far), (v2, v2_far), (q2, q2_far), (n_ref, n_far), (r_ref, r_far))
    ]
    attention_forward(meta, q2, k2, v2, lse2, m2, source_segments_of)
    wait(flying)


def attention_layers(meta, rows, pieces, deps=()):
    one = pltpu.VMEM(ROWS_BF, BF)
    return call(
        attention_layers_body,
        (full(), sds(TOTALS, F32), sds(TOTALS, F32), sds((8, D), F32)),
        (meta,),
        rows + tuple(pieces),
        (full(),) * 4 + (full(F32), sds((TOK, PACK), F32)) + (full(),) * 3,
        deps=deps,
        scratch=[pltpu.VMEM((pieces[0].shape[1], D, D), BF)]
        + [one] * 10
        + [pltpu.VMEM((TOK, D), F32), pltpu.VMEM((TOK, PACK), F32), sems(2), sems(2), pltpu.SemaphoreType.DMA((2, 8)), sems(9)],
        us=15,
        mb=48,
    )


def gelu_both(v):
    c = math.sqrt(2.0 / math.pi)
    v2 = v * v
    t = jnp.tanh(c * (v + 0.044715 * (v * v2)))
    cdf = 0.5 + 0.5 * t
    return v * cdf, cdf + (0.5 * v) * (1.0 - t * t) * (c + (3.0 * 0.044715 * c) * v2)


def put_grad(g_own, g_oth, m, value):
    value = value.astype(BF)
    g_own[:, m] = value[:, :HALF].reshape(PIECES, CH, HALF)
    g_oth[:, m] = value[:, HALF:].reshape(PIECES, CH, HALF)


def ffn_forward_body(*refs):
    meta, m2, norm, n_far = refs[:4]
    pieces = refs[4:12]
    out_own, out_oth, w, act_ref, slope_ref, n2_ref, n3_ref, r_ref, m_far, po_far, n1, sem, out_sem, in_sem = refs[12:]
    blocks = (w.shape[0] - 1) // 2
    outs = Copies(out_sem)
    flying = [outs.start(m2, m_far)]
    loading = Copies(in_sem).start(n_far, n1)
    wait(load_weights(meta, pieces, w, sem))
    loading.wait()
    flying.append(outs.start(w.at[0], po_far))

    def step(i):
        rows = block(i, BLK)
        h1 = n1[rows, :] * norm[0:1, :] + norm[3:4, :]
        n2, rstd2 = norm_forward(h1 + dot_nt(m2[rows, :], w[0]))
        n2_ref[rows, :] = n2
        h2 = n2 * norm[1:2, :] + norm[4:5, :]
        h2b = h2.astype(BF)
        r3 = h2
        pre = dot(h2b, w[1])
        for b in range(blocks):
            now = pre
            if b + 1 < blocks:
                pre = dot(h2b, w[2 + b])
            act, slope = gelu_both(now)
            act = act.astype(BF)
            act_ref[b, rows, :] = act
            slope_ref[b, rows, :] = slope.astype(BF)
            r3 = r3 + dot_nt(act, w[1 + blocks + b])
        n3, rstd3 = norm_forward(r3)
        n3_ref[rows, :] = n3
        r_ref[rows, :] = jnp.where(low_lanes(BLK), rstd2, rstd3)
        result = n3 * norm[2:3, :] + norm[5:6, :]
        out_own[rows, :], out_oth[rows, :] = halves(meta, result.astype(BF))

    loop(TOK // BLK, step)
    wait(flying)


def ffn_forward(meta, n1_far, m2, norm, pieces):
    mats = pieces[0].shape[1]
    hidden = sds(((mats - 1) // 2, TOK, D))
    return call(
        ffn_forward_body,
        (sds((TOK, HALF)), sds((TOK, HALF)), sds((mats, D, D)), hidden, hidden)
        + (full(F32), full(F32), sds((TOK, PACK), F32)),
        (meta, m2, norm),
        (n1_far,) + tuple(pieces),
        (full(), sds((D, D))),
        scratch=[pltpu.VMEM((TOK, D), F32), sems(8), sems(2), sems(1)],
        us=9,
        mb=24,
    )


def ffn_backward_body(*refs):
    meta, norm, w, act_ref, slope_ref, n2_ref, n3_ref, r_ref, cot_own, cot_oth = refs[:10]
    g_own, g_oth, ng, dr_far = refs[10:14]
    cot, pre_ref, df_ref, h_ref, dr_ref, sem, out_sem = refs[14:]
    blocks = (w.shape[0] - 1) // 2
    mine = block(meta[CORE], TOK)
    loads = Copies(sem)
    wait(
        [
            loads.start(src.at[mine], cot.at[:, block(at, HALF)])
            for src, at in ((cot_own, meta[CORE]), (cot_oth, 1 - meta[CORE]))
        ]
    )
    ng[...] = jnp.zeros_like(ng)

    def step(i):
        rows = block(i, BLK)
        dy = cot[rows, :].astype(F32)
        dr3, gain3, bias3 = norm_backward(dy, n3_ref[rows, :], r_ref[rows, HD : HD + 1], norm[2:3, :])
        df = dr3.astype(BF)
        df_ref[rows, :] = df
        dh2 = dr3
        for b in range(blocks):
            dpre = (dot(df, w[1 + blocks + b]) * slope_ref[b, rows, :].astype(F32)).astype(BF)
            pre_ref[b, rows, :] = dpre
            dh2 = dh2 + dot_nt(dpre, w[1 + b])
        n2 = n2_ref[rows, :]
        h_ref[rows, :] = (n2 * norm[1:2, :] + norm[4:5, :]).astype(BF)
        dr2, gain2, bias2 = norm_backward(dh2, n2, r_ref[rows, 0:1], norm[1:2, :])
        dr_ref[rows, :] = dr2
        ng[1:2, :] += gain2
        ng[2:3, :] += gain3
        ng[4:5, :] += bias2
        ng[5:6, :] += bias3

    loop(TOK // BLK, step)
    flying = Copies(out_sem).start(dr_ref, dr_far)
    h_t = h_ref[...].T
    for b in range(blocks):
        put_grad(g_own, g_oth, b, dot(h_t, pre_ref[b]))
    df_t = df_ref[...].T
    for b in range(blocks):
        put_grad(g_own, g_oth, blocks + b, dot(df_t, act_ref[b]))
    flying.wait()


def ffn_backward(meta, norm, w, act, slope, n2, n3, rstd, cot_own, cot_oth, deps=()):
    blocks = act.shape[0]
    grad = sds((PIECES, 2 * blocks, CH, HALF))
    return call(
        ffn_backward_body,
        (grad, grad, sds((8, D), F32)),
        (meta, norm, w, act, slope, n2, n3, rstd),
        (cot_own, cot_oth),
        (full(F32),),
        deps=deps,
        scratch=[
            pltpu.VMEM(ROWS_BF, BF),
            pltpu.VMEM((blocks, TOK, D), BF),
            pltpu.VMEM(ROWS_BF, BF),
            pltpu.VMEM(ROWS_BF, BF),
            pltpu.VMEM((TOK, D), F32),
            sems(2),
            sems(1),
        ],
        us=14,
        mb=28,
    )


def fetch(sem, pairs):
    copies = Copies(sem)
    started = [copies.start(src, dst) for src, dst in pairs]
    return lambda *at: wait([started[k] for k in at])


def cross_backward_body(*refs):
    meta, norm, ng_in, lse = refs[:4]
    dr_in_far, q_far, k_far, v_far, m_far, n_far, r_far, po_far, enc_own, enc_oth = refs[4:14]
    pieces = refs[14:22]
    dr_ref, g_own, g_oth, ng, dr_far, dk_far, dv_far = refs[22:29]
    q, k, v, m, enc, n, r, w, po, da, dm, dq, dk, dv, h, dr_in, in_sem, out_sem, w_sem, enc_sem = refs[29:]
    ready = fetch(
        in_sem,
        ((po_far, po), (q_far, q), (k_far, k), (v_far, v), (n_far, n), (r_far, r), (m_far, m), (dr_in_far, dr_in)),
    )
    weights = load_weights(meta, pieces, w, w_sem, 4, 1, 0)
    rows_in = load_rows(meta, enc_own, enc_oth, enc, enc_sem)
    outs = Copies(out_sem)
    ready(7)
    da[...] = dr_in[...].astype(BF)
    ready(0)
    dm[...] = dot(da[...], po[...]).astype(BF)
    ready(1, 2, 3)
    attention_backward(meta, q, k, v, lse, dm, dq, dk, dv, source_segments_of)
    flying = [outs.start(dk, dk_far), outs.start(dv, dv_far)]
    ng[...] = ng_in[...]
    ready(4, 5)
    wait(weights)

    def step(i):
        rows = block(i, BLK)
        normed = n[rows, :]
        h[rows, :] = (normed * norm[0:1, :] + norm[3:4, :]).astype(BF)
        dh1 = dr_in[rows, :] + dot_nt(dq[rows, :], w[0])
        dr1, gain1, bias1 = norm_backward(dh1, normed, r[rows, 0:1], norm[0:1, :])
        dr_ref[rows, :] = dr1
        ng[0:1, :] += gain1
        ng[3:4, :] += bias1

    loop(TOK // BLK, step)
    flying.append(outs.start(dr_ref, dr_far))
    ready(6)
    wait(rows_in)
    put_grad(g_own, g_oth, 0, dot_tn(da[...], m[...]))
    put_grad(g_own, g_oth, 1, dot_tn(h[...], dq[...]))
    put_grad(g_own, g_oth, 2, dot_tn(enc[...], dk[...]))
    put_grad(g_own, g_oth, 3, dot_tn(enc[...], dv[...]))
    total = jnp.concatenate([ng[...], jnp.zeros((CH - 8, D), F32)], 0).astype(BF)
    for c in range(PIECES):
        part = total[:, :HALF] if c < PIECES // 2 else total[:, HALF:]
        g_own[c, 4] = part
        g_oth[c, 4] = part
    wait(flying)


def cross_backward(meta, dr2, norm, ng, lse, saved, pieces, deps=()):
    grad = sds((PIECES, 5, CH, HALF))
    rows = pltpu.VMEM(ROWS_BF, BF)
    return call(
        cross_backward_body,
        (full(F32), grad, grad, sds((8, D), F32)),
        (meta, norm, ng, lse),
        (dr2,) + saved + tuple(pieces),
        (full(F32), full(), full()),
        deps,
        [rows] * 5
        + [pltpu.VMEM((TOK, D), F32), pltpu.VMEM((TOK, PACK), F32), pltpu.VMEM((1, D, D), BF), pltpu.VMEM((D, D), BF)]
        + [rows] * 6
        + [pltpu.VMEM((TOK, D), F32), sems(8), sems(3), sems(8), sems(2)],
        us=12,
        mb=46,
    )


def self_backward_body(*refs):
    meta, dr_in, lse = refs[:3]
    q_far, k_far, v_far, m_far, tok_own, tok_oth = refs[3:9]
    pieces = refs[9:17]
    g_own, g_oth, dq_far, dk_far, dv_far, q, k, v, m, x, w, da, dm, dq, dk, dv, in_sem, w_sem, x_sem, out_sem = refs[17:]
    weights = load_weights(meta, pieces, w, w_sem, 3, 1, 0)
    ready = fetch(in_sem, ((q_far, q), (k_far, k), (v_far, v), (m_far, m)))
    rows_in = load_rows(meta, tok_own, tok_oth, x, x_sem)
    da[...] = dr_in[...].astype(BF)
    wait(weights)
    dm[...] = dot(da[...], w[0]).astype(BF)
    ready(0, 1, 2)
    attention_backward(meta, q, k, v, lse, dm, dq, dk, dv, target_segments)
    outs = Copies(out_sem)
    flying = [outs.start(dq, dq_far), outs.start(dk, dk_far), outs.start(dv, dv_far)]
    ready(3)
    wait(rows_in)
    put_grad(g_own, g_oth, 0, dot_tn(da[...], m[...]))
    put_grad(g_own, g_oth, 1, dot_tn(x[...], dq[...]))
    put_grad(g_own, g_oth, 2, dot_tn(x[...], dk[...]))
    put_grad(g_own, g_oth, 3, dot_tn(x[...], dv[...]))
    wait(flying)


def self_backward(meta, dr1, lse, saved, pieces, deps=()):
    grad = sds((PIECES, 4, CH, HALF))
    rows = pltpu.VMEM(ROWS_BF, BF)
    return call(
        self_backward_body,
        (grad, grad),
        (meta, dr1, lse),
        saved + tuple(pieces),
        (full(), full(), full()),
        deps,
        [rows] * 5 + [pltpu.VMEM((1, D, D), BF)] + [rows] * 5 + [sems(4), sems(8), sems(2), sems(3)],
        us=10,
        mb=46,
    )


def inputs_backward_body(*refs):
    meta = refs[0]
    pieces = refs[7:15]
    x_own, x_oth, e_own, e_oth, dr, dq, dk, dv, dk2, dv2, w, w2, in_sem, w_sem, w2_sem = refs[15:]
    ready = fetch(in_sem, tuple(zip(refs[1:7], (dr, dq, dk, dv, dk2, dv2))))
    weights = load_weights(meta, pieces, w, w_sem, 0, 3) + load_weights(meta, pieces, w2, w2_sem, 5, 2, 0)
    wait(weights)
    ready(*range(6))

    def step(i):
        rows = block(i, BLK)
        dx = dr[rows, :] + dot_nt(dq[rows, :], w[0]) + dot_nt(dk[rows, :], w[1]) + dot_nt(dv[rows, :], w[2])
        x_own[rows, :], x_oth[rows, :] = halves(meta, dx.astype(BF))
        de = dot_nt(dk2[rows, :], w2[0]) + dot_nt(dv2[rows, :], w2[1])
        e_own[rows, :], e_oth[rows, :] = halves(meta, de.astype(BF))

    loop(TOK // BLK, step)


def inputs_backward(meta, saved, pieces, deps=()):
    rows = pltpu.VMEM(ROWS_BF, BF)
    return call(
        inputs_backward_body,
        (sds((TOK, HALF)),) * 4,
        (meta,),
        saved + tuple(pieces),
        (),
        deps,
        [pltpu.VMEM((TOK, D), F32)] + [rows] * 5 + [pltpu.VMEM((3, D, D), BF), pltpu.VMEM((2, D, D), BF)]
        + [sems(6), sems(8), sems(8)],
        us=5,
        mb=46,
    )


def place_body(meta, own, oth, out):
    for side, src in enumerate((own, oth)):
        for j in range(SLOTS):
            out[block(meta[ROW + SLOTS * side + j], PACK), :] = src[j * PACK : (j + 1) * PACK, :]


def count_body(far, out, seg, sem):
    Copies(sem).start(far, seg).wait()
    first = jnp.where(seg[...] == 0, 1.0, 0.0).astype(BF)
    out[...] = dot_nt(jnp.ones((8, PACK), BF), first)


def join_body(meta, own, oth, out):
    out[block(meta[CORE], TOK), :] = own[...]
    out[block(1 - meta[CORE], TOK), :] = oth[...]


def copy_body(src, out):
    out[...] = src[...]


def copy_after(value, deps):
    return call(copy_body, (sds(value.shape),), (value,), deps=deps)[0]


BOTH = (2 * TOK, HALF)


def add(a, b):
    return (a.astype(F32) + b.astype(F32)).astype(BF)


def pair_sum_body(meta, own, rec, *outs):
    for k in range(4):
        for j in range(4):
            c = meta[PIECE + 4 * k + j]
            if k < 2:
                outs[k][j] = add(own[c], rec[c])
            else:
                outs[2][k - 2, j] = add(own[c], rec[c])


def pair_sum(meta, own, rec):
    shape = (4,) + own.shape[1:]
    return call(pair_sum_body, (sds(shape), sds(shape), sds((2,) + shape)), (meta, own, rec))


def stage_sum_body(a0, a1, b, keep, send):
    keep[...] = add(a0[...], b[0])
    send[...] = add(a1[...], b[1])


def last_line_body(at, a, b, *outs):
    for j in range(4):
        k = at[0] ^ j
        outs[j][...] = add(a[k], b[k])


def tail_sum_body(at, kc, rc, ks, rs, *outs):
    mats = kc.shape[1]
    for j in range(4):
        k = at[0] ^ j
        outs[j][:mats] = add(kc[k], rc[k])
        outs[j][mats:] = add(ks[k], rs[k])


def adam_attention_body(*refs):
    parts, state, outs = refs[:4], refs[4:10], refs[10:]
    total = [ref[...].astype(F32) for ref in parts]
    g = (total[0] + total[1]) + (total[2] + total[3])
    grads = (jnp.concatenate([g[6:9], g[1:4]], 0), jnp.concatenate([g[5:6], g[0:1]], 0))
    for k, grad in enumerate(grads):
        weight, first, second = (ref[...] for ref in state[3 * k : 3 * k + 3])
        outs[3 * k][...], outs[3 * k + 1][...], outs[3 * k + 2][...] = adam(
            weight, first, second, grad, rate_matrix, decay_matrix
        )
    outs[6][...] = g[4, :8]


def adam_ffn_body(z, *refs):
    state, outs = refs[:6], refs[6:]
    g = (z[0].astype(F32) + z[1].astype(F32)) + (z[2].astype(F32) + z[3].astype(F32))
    blocks = g.shape[0] // 2
    for k in range(2):
        for b in range(blocks):
            cols = slice(b * HALF, (b + 1) * HALF)
            weight, first, second = (ref[:, cols] for ref in state[3 * k : 3 * k + 3])
            outs[3 * k][:, cols], outs[3 * k + 1][:, cols], outs[3 * k + 2][:, cols] = adam(
                weight, first, second, g[k * blocks + b], rate_matrix, decay_matrix
            )


def adam(weight, first_old, second_old, grad, rate, decay):
    first_new = beta_first * first_old + (1.0 - beta_first) * grad
    second_new = beta_second * second_old + (1.0 - beta_second) * grad * grad
    first_hat = first_new / (1.0 - beta_first**STEP)
    second_hat = second_new / (1.0 - beta_second**STEP)
    updated = weight - rate * (first_hat / (jnp.sqrt(second_hat) + adam_epsilon) + decay * weight)
    return (first_new, second_new, updated)


def swap(value):
    return lax.ppermute(value, "narrow", [(0, 1), (1, 0)])


def peer(value, mask, mask_one=None):
    masks = (mask, mask if mask_one is None else mask_one)
    chips = lax.axis_size("wide")
    route = [(2 * i + c, 2 * (i ^ masks[c]) + c) for i in range(chips) for c in range(2)]
    return lax.ppermute(value, ("wide", "narrow"), route)


def along_z(parts):
    plane = lax.axis_size("wide") // 4
    lines = [[at + plane * j for j in range(4)] for at in range(plane)]
    return lax.all_to_all(parts, "wide", 0, 0, axis_index_groups=lines)


def local(
    tokens,
    encoded,
    cotangent,
    target_lengths,
    source_segments,
    send_rows,
    proj_in,
    proj_out,
    ffn_in,
    ffn_out,
    norm_par,
    proj_in_moment,
    proj_in_square,
    proj_out_moment,
    proj_out_square,
    ffn_in_moment,
    ffn_in_square,
    ffn_out_moment,
    ffn_out_square,
    norm_moment,
    norm_square,
):
    wide_count = lax.axis_size("wide")
    w = lax.axis_index("wide")
    n = lax.axis_index("narrow")
    rows_dev = tokens.shape[0] // PACK
    stride = wide_count // rows_dev
    share = proj_in.shape[1]
    blocks = ffn_in.shape[1] // HALF
    direct = share == CH

    places = jnp.arange(rows_dev, dtype=jnp.int32)
    slot_rows = lax.dynamic_index_in_dim(send_rows, w, 0, keepdims=False)[places * stride + w % stride]
    mine = lax.dynamic_slice_in_dim(slot_rows, n * SLOTS, SLOTS)
    theirs = lax.dynamic_slice_in_dim(slot_rows, (1 - n) * SLOTS, SLOTS)
    mine_global = w * rows_dev + mine
    lengths = target_lengths[mine_global]
    if direct:
        orders = jnp.array([[a for a in order for _ in range(4)] for order in ((0, 1, 2, 3), (0, 2, 1, 3))])
        in_plane = jnp.concatenate([orders[n], orders[1 - n]]) ^ (w % 4)
        piece_ids = in_plane + 4 * (jnp.arange(2 * PIECES, dtype=jnp.int32) % 4)
    else:
        piece_ids = jnp.tile(jnp.arange(PIECES, dtype=jnp.int32), 2)
    counts = call(
        count_body,
        (sds((8, source_segments.shape[0]), F32),),
        (),
        (source_segments,),
        scratch=[pltpu.VMEM(source_segments.shape, jnp.int32), sems(1)],
        mb=56,
    )[0]
    cut = counts[0][mine_global].astype(jnp.int32)
    meta = jnp.concatenate(
        [n[None], piece_ids, mine, theirs, lengths[:, 0], lengths[:, 0] + lengths[:, 1], cut]
    ).astype(jnp.int32)

    tok_rows = (tokens, swap(tokens))
    enc_rows = (encoded, swap(encoded))
    pout_t = proj_out.transpose(0, 2, 1)
    wout_t = ffn_out.T
    out_moment, out_square = proj_out_moment.transpose(0, 2, 1), proj_out_square.transpose(0, 2, 1)

    if direct:
        g0 = call(
            pack_attention_body,
            (sds((8, CH, HALF)),),
            (),
            (proj_in, pout_t, norm_par),
            scratch=[pltpu.VMEM(a, F32) for a in (proj_in.shape, (CH, HALF), norm_par.shape)] + [sems(3)],
            us=2,
        )[0]
        line = [peer(g0, 4 * k) for k in (1, 2, 3)]
        z0 = call(
            stack_body,
            (sds((4, 8, CH, HALF)),),
            ((w // 4)[None], g0, *line),
            deps=(meta, tok_rows[1], enc_rows[1]),
        )[0]
        first0 = peer(z0, 1, 2)
        second0 = peer(z0, 2, 1)
        g1 = call(
            pack_ffn_body,
            (sds((4, 1 + 2 * blocks, CH, HALF)),),
            (pout_t, ffn_in, wout_t),
            deps=(z0,),
            us=2,
        )[0]
        z1 = along_z(g1)
        third0 = peer(copy_after(first0, (z1, second0)), 2, 1)
        pieces0 = [z0, first0, second0, third0]
        first1 = peer(z1, 1, 2)
        second1 = peer(z1, 2, 1)
        pieces1 = [z1, first1, second1]
        pieces = [own + [swap(a) for a in own] for own in (pieces0, pieces1)]
        cotangent = copy_after(cotangent, (third0,))
    else:
        low_in = lax.all_gather(proj_in.astype(BF), "wide", axis=1, tiled=True)
        low_out = lax.all_gather(proj_out.astype(BF), "wide", axis=2, tiled=True).transpose(0, 2, 1)
        low_win = lax.all_gather(ffn_in.astype(BF), "wide", axis=0, tiled=True)
        low_wout = lax.all_gather(ffn_out.astype(BF), "wide", axis=1, tiled=True).T
        low_norm = lax.all_gather(norm_par.astype(BF), "wide", axis=1, tiled=True)

        def column_blocks(a):
            return a.reshape(D, blocks, HALF).transpose(1, 0, 2)

        tiled = jnp.tile(low_norm.reshape(6, PIECES, CH).transpose(1, 0, 2), (1, 1, HALF // CH))
        norm_mat = jnp.pad(tiled, ((0, 0), (0, CH - 6), (0, 0))).reshape(1, D, HALF)
        groups = (
            jnp.concatenate([low_in[:3], low_out[:1], low_in[3:], norm_mat]),
            jnp.concatenate([low_out[1:], column_blocks(low_win), column_blocks(low_wout)]),
        )
        pieces = []
        for group in groups:
            cut = group.reshape(-1, PIECES, CH, HALF).transpose(1, 0, 2, 3)
            own = [cut[4 * k : 4 * k + 4] for k in range(4)]
            pieces.append(own + [swap(a) for a in own])

    everyone = [[r + stride * j for j in range(rows_dev)] for r in range(stride)]

    def exchange(rows):
        return lax.all_to_all(
            rows.reshape(rows_dev, PACK, HALF), "wide", 0, 0, axis_index_groups=everyone
        ).reshape(rows_dev * PACK, HALF)

    cot_own = exchange(cotangent)
    cot_oth = swap(cot_own)
    m2, lse1, lse2, norm, q1, k1, v1, m1, n1, rstd1, q2, k2, v2 = attention_layers(
        meta, tok_rows + enc_rows, pieces[0]
    )
    if direct:
        third1 = peer(copy_after(first1, (lse2, second1)), 2, 1)
        pieces[1] = pieces[1][:3] + [third1] + pieces[1][3:] + [swap(third1)]
    out_own, out_oth, w_ffn, act, slope, n2, n3, rstd, m2_far, po2 = ffn_forward(meta, n1, m2, norm, pieces[1])
    joined = call(join_body, (sds(BOTH),), (meta, out_own, swap(out_oth)))[0]
    gf_own, gf_oth, ng, dr2 = ffn_backward(
        meta, norm, w_ffn, act, slope, n2, n3, rstd, cot_own, cot_oth, (joined,)
    )
    layer_out = copy_after(exchange(joined), ())
    early = ()
    if direct:
        sf = pair_sum(meta, gf_own, swap(gf_oth))
        early = (sf[2],)
    dr1, gc_own, gc_oth, ng, dr1_far, dk2, dv2 = cross_backward(
        meta, dr2, norm, ng, lse2, (q2, k2, v2, m2_far, n1, rstd1, po2) + enc_rows, pieces[0], early
    )
    if direct:
        kf, send_f = call(stage_sum_body, (sds(sf[0].shape),) * 2, (sf[0], sf[1], peer(sf[2], 2, 1)))
        sc = pair_sum(meta, gc_own, swap(gc_oth))
    gs_own, gs_oth, dq1, dk1, dv1 = self_backward(
        meta, dr1, lse1, (q1, k1, v1, m1) + tok_rows, pieces[0], (send_f,) if direct else ()
    )
    if direct:
        at_z = (w // 4)[None]
        zf = call(last_line_body, (sds(kf.shape[1:]),) * 4, (at_z, kf, peer(send_f, 1, 2)))
        ss = pair_sum(meta, gs_own, swap(copy_after(gs_oth, (zf[1],))))
        zf = jnp.stack([zf[0]] + [peer(zf[k], 4 * k) for k in (1, 2, 3)])
    dx_own, dx_oth, de_own, de_oth = inputs_backward(
        meta, (dr1_far, dq1, dk1, dv1, dk2, dv2), pieces[0], (layer_out,) if direct else ()
    )
    tokens_grad = call(place_body, (sds(BOTH),), (meta, dx_own, swap(dx_oth)))[0]
    encoded_grad = call(place_body, (sds(BOTH),), (meta, de_own, swap(de_oth)))[0]

    if direct:
        kc, send_c = call(
            stage_sum_body, (sds(sc[0].shape),) * 2, (sc[0], sc[1], peer(sc[2], 2, 1)), deps=(dx_own,)
        )
        ks, send_s = call(stage_sum_body, (sds(ss[0].shape),) * 2, (ss[0], ss[1], peer(ss[2], 2, 1)))
        line = call(
            tail_sum_body,
            (sds((kc.shape[1] + ks.shape[1], CH, HALF)),) * 4,
            (at_z, kc, peer(send_c, 1, 2), ks, peer(send_s, 1, 2)),
        )
        line = [line[0]] + [peer(line[k], 4 * k) for k in (1, 2, 3)]
        pairs = ((proj_in, proj_in_moment, proj_in_square), (pout_t, out_moment, out_square))
        wide_pairs = ((ffn_in, ffn_in_moment, ffn_in_square), (wout_t, ffn_out_moment.T, ffn_out_square.T))

        def news(group):
            return tuple(sds(a.shape, F32) for triple in group for a in triple)

        upd = call(adam_ffn_body, news(wide_pairs), (zf,) + wide_pairs[0] + wide_pairs[1], us=2)
        upd_expand, upd_reduce = upd[:3], tuple(u.T for u in upd[3:])
        upd = call(
            adam_attention_body,
            news(pairs) + (sds((8, HALF), F32),),
            tuple(line) + pairs[0] + pairs[1],
            deps=(tokens_grad, encoded_grad, upd[0]),
            us=2,
        )
        upd_in, upd_out = upd[:3], tuple(u.transpose(0, 2, 1) for u in upd[3:6])
        norm_half = upd[6][:6]
        norm_half = jnp.where(n == 0, norm_half, swap(norm_half))
        norm_grad = lax.dynamic_slice_in_dim(norm_half, (w % (HALF // CH)) * CH, CH, 1)
    else:

        def summed(own, oth):
            total = (own.astype(F32) + swap(oth).astype(F32)).astype(BF)
            total = total.transpose(1, 0, 2, 3).reshape(-1, D, HALF)
            return lax.psum_scatter(total, "wide", scatter_dimension=1, tiled=True).astype(F32)

        gf, gc, gs = summed(gf_own, gf_oth), summed(gc_own[:, :4], gc_oth[:, :4]), summed(gs_own, gs_oth)
        norm_all = lax.psum(ng, ("wide", "narrow"))[:6]
        norm_grad = lax.dynamic_slice_in_dim(norm_all, w * share, share, 1)

        grad_in = jnp.concatenate([gs[1:4], gc[1:4]])
        grad_out = jnp.stack([gs[0], gc[0]])
        grad_expand = gf[:blocks].transpose(1, 0, 2).reshape(share, blocks * HALF)
        grad_reduce = gf[blocks:].transpose(1, 0, 2).reshape(share, blocks * HALF)
        upd_in = adam(proj_in, proj_in_moment, proj_in_square, grad_in, rate_matrix, decay_matrix)
        upd_out = adam(pout_t, out_moment, out_square, grad_out, rate_matrix, decay_matrix)
        upd_out = tuple(u.transpose(0, 2, 1) for u in upd_out)
        upd_expand = adam(ffn_in, ffn_in_moment, ffn_in_square, grad_expand, rate_matrix, decay_matrix)
        upd_reduce = adam(
            wout_t, ffn_out_moment.T, ffn_out_square.T, grad_reduce, rate_matrix, decay_matrix
        )
        upd_reduce = tuple(u.T for u in upd_reduce)
    upd_norm = adam(norm_par, norm_moment, norm_square, norm_grad, rate_norm, 0.0)
    return (layer_out, tokens_grad, encoded_grad) + upd_in + upd_out + upd_expand + upd_reduce + upd_norm


def solution(mesh):
    rows = P("wide", "narrow")
    p_in = P(None, "wide", "narrow")
    p_out = P(None, "narrow", "wide")
    p_expand = P("wide", "narrow")
    p_reduce = P("narrow", "wide")
    p_norm = P(None, "wide")
    weights = (p_in, p_out, p_expand, p_reduce, p_norm)
    in_specs = (rows,) * 3 + (P(),) * 3 + weights + tuple(s for s in weights for _ in range(2))
    out_specs = (rows,) * 3 + tuple(s for s in weights for _ in range(3))
    return jax.shard_map(local, mesh=mesh, in_specs=in_specs, out_specs=out_specs, check_vma=False)
```

```python
import functools
import math

import jax
import jax.numpy as jnp
from jax import lax
from jax.experimental import pallas as pl
from jax.experimental.pallas import tpu as pltpu
from jax.sharding import PartitionSpec as P

D = 512
H = 8
HD = D // H
PACK = 128
STEP = 5
CH = 32
HALF = D // 2
PIECES = D // CH
SLOTS = 8
TOK = SLOTS * PACK
BLK = 1024

norm_epsilon = 1e-05
beta_first = 0.9
beta_second = 0.98
adam_epsilon = 1e-08
rate_matrix = 0.1
rate_norm = 0.5
decay_matrix = 0.01
masked_score = -1e30

CORE = 0
PIECE = 1
ROW = PIECE + 2 * PIECES
FIRST = ROW + 2 * SLOTS
SECOND = FIRST + SLOTS
CUT = SECOND + SLOTS

BF = jnp.bfloat16
F32 = jnp.float32


def dot(a, b):
    return jnp.dot(a, b, preferred_element_type=F32)


def dot_nt(a, b):
    return lax.dot_general(a, b, (((1,), (1,)), ((), ())), preferred_element_type=F32)


def dot_tn(a, b):
    return lax.dot_general(a, b, (((0,), (0,)), ((), ())), preferred_element_type=F32)


def sds(shape, dtype=BF):
    return jax.ShapeDtypeStruct(shape, dtype)


def cost(us):
    return pl.CostEstimate(flops=us * 10**9, bytes_accessed=us * 3 * 10**6, transcendentals=0)


def call(body, outs, operands, far=(), far_outs=(), deps=(), scratch=(), us=1, mb=16):
    count = len(operands) + len(far)

    def run(*refs):
        body(*refs[:count], *refs[count + len(deps) :])

    vmem = pl.BlockSpec(memory_space=pltpu.VMEM)
    hbm = pl.BlockSpec(memory_space=pltpu.HBM)
    smem = pl.BlockSpec(memory_space=pltpu.SMEM)
    specs = [smem if o.dtype == jnp.int32 and o.ndim == 1 else vmem for o in operands]
    return pl.pallas_call(
        run,
        in_specs=specs + [hbm] * len(far) + [ANY] * len(deps),
        out_specs=(vmem,) * len(outs) + (hbm,) * len(far_outs),
        out_shape=tuple(outs) + tuple(far_outs),
        scratch_shapes=list(scratch),
        cost_estimate=cost(us),
        compiler_params=pltpu.CompilerParams(vmem_limit_bytes=mb * 2**20),
    )(*operands, *far, *deps)


def sems(count):
    return pltpu.SemaphoreType.DMA((count,))


class Copies:
    def __init__(self, sem):
        self.sem, self.count = sem, 0

    def start(self, src, dst):
        c = pltpu.make_async_copy(src, dst, self.sem.at[self.count])
        self.count += 1
        c.start()
        return c


def wait(copies):
    for c in copies:
        c.wait()


ANY = pl.BlockSpec(memory_space=pl.ANY)


def block(i, size):
    return pl.ds(pl.multiple_of(i * size, size), size)


def loop(count, body, unroll=1):
    def step(i, carry):
        body(i)
        return carry

    lax.fori_loop(0, count, step, 0, unroll=unroll)


def eye_of(rows, columns):
    at = [lax.broadcasted_iota(jnp.int32, (rows, columns), d) for d in range(2)]
    return (at[0] == at[1] % CH).astype(BF)


def pack_attention_body(pin_far, pout_far, norm_far, g, pin, pout, norm, sem):
    loads = Copies(sem)
    wait([loads.start(pin_far, pin), loads.start(pout_far.at[0], pout), loads.start(norm_far, norm)])
    rows = dot(eye_of(CH, 6), norm[...].astype(BF)).astype(BF)
    rows = dot(rows, eye_of(CH, HALF)).astype(BF)
    g[0:3] = pin[0:3].astype(BF)
    g[3] = pout[...].astype(BF)
    g[4:7] = pin[3:6].astype(BF)
    g[7] = rows


def pack_ffn_body(pout, win, wout, g):
    blocks = win.shape[1] // HALF
    for to in range(4):
        g[to, 0] = pout[1].astype(BF)
        for b in range(blocks):
            g[to, 1 + b] = win[:, b * HALF : (b + 1) * HALF].astype(BF)
            g[to, 1 + blocks + b] = wout[:, b * HALF : (b + 1) * HALF].astype(BF)


def stack_body(at, *refs):
    for j in range(4):
        refs[4][at[0] ^ j] = refs[j][...]


def load_weights(meta, pieces, w_ref, sem, first=0, count=None, at=None):
    at = first if at is None else at
    count = w_ref.shape[0] - at if count is None else count
    copies = []
    for a, piece in enumerate(pieces):
        half, group = divmod(a, len(pieces) // 2)
        per = piece.shape[0]
        for j in range(per):
            row = pl.multiple_of(meta[PIECE + half * PIECES + group * per + j] * CH, CH)
            copies.append(
                pltpu.make_async_copy(
                    piece.at[j, pl.ds(first, count)],
                    w_ref.at[pl.ds(at, count), pl.ds(row, CH), pl.ds(half * HALF, HALF)],
                    sem.at[a],
                )
            )
    for c in copies:
        c.start()
    return copies


def load_rows(meta, own, oth, dst, sem):
    copies = []
    for side, src in enumerate((own, oth)):
        at = meta[CORE] if side == 0 else 1 - meta[CORE]
        for j in range(SLOTS):
            copies.append(
                pltpu.make_async_copy(
                    src.at[block(meta[ROW + j], PACK)],
                    dst.at[pl.ds(j * PACK, PACK), block(at, HALF)],
                    sem.at[side],
                )
            )
    for c in copies:
        c.start()
    return copies


def lane_masks():
    low = (lax.broadcasted_iota(jnp.int32, (1, PACK), 1) < HD).astype(F32)
    return low.astype(BF), (1.0 - low).astype(BF)


def low_lanes(rows=PACK):
    return lax.broadcasted_iota(jnp.int32, (rows, PACK), 1) < HD


def two_heads(rows, low, high):
    return jnp.concatenate([rows * low, rows * high], 0)


def norm_forward(r):
    center = r - jnp.mean(r, -1, keepdims=True)
    rstd = lax.rsqrt(jnp.mean(center * center, -1, keepdims=True) + norm_epsilon)
    return center * rstd, rstd


def norm_backward(dy, n, rstd, gain):
    dn = dy * gain
    dr = rstd * (dn - jnp.mean(dn, -1, keepdims=True) - n * jnp.mean(dn * n, -1, keepdims=True))
    return dr, jnp.sum(dy * n, 0, keepdims=True), jnp.sum(dy, 0, keepdims=True)


def target_segments(meta, slot, dim):
    at = lax.broadcasted_iota(jnp.int32, (PACK, PACK), dim)
    one = (at >= meta[FIRST + slot]).astype(jnp.int32)
    return one + (at >= meta[SECOND + slot]).astype(jnp.int32)


def source_segments_of(meta, slot, dim):
    return (lax.broadcasted_iota(jnp.int32, (PACK, PACK), dim) >= meta[CUT + slot]).astype(jnp.int32)


def halves(meta, full):
    first = meta[CORE] == 0
    lo, hi = full[:, :HALF], full[:, HALF:]
    return jnp.where(first, lo, hi), jnp.where(first, hi, lo)


def mask_of(meta, slot, key_segments):
    mask = key_segments(meta, slot, 0) == target_segments(meta, slot, 1)
    return jnp.concatenate([mask, mask], 1)


def pairs_of(meta, first, count, key_segments):
    pairs = []
    for slot in [first + j for j in range(count)]:
        mask = mask_of(meta, slot, key_segments)
        rows = block(slot, PACK)
        for h in range(H // 2):
            pairs.append((rows, slice(h * PACK, (h + 1) * PACK), mask, (slot, slice(h, h + 1))))
    return pairs


def attention_forward(meta, q, k, v, lse, m, key_segments):
    low, high = lane_masks()
    scale = HD**-0.5
    slots = 2

    def step(i):
        pairs = pairs_of(meta, i * slots, slots, key_segments)
        s = [
            jnp.where(mask, dot_nt(k[r, c], two_heads(q[r, c], low * scale, high * scale)), masked_score)
            for r, c, mask, _ in pairs
        ]
        peak = [jnp.max(one, 0, keepdims=True) for one in s]
        e = [jnp.exp(one - top) for one, top in zip(s, peak)]
        total = [jnp.sum(one, 0, keepdims=True) for one in e]
        p = [(one * (1.0 / all_keys)).astype(BF) for one, all_keys in zip(e, total)]
        for (_, _, _, (slot, h)), top, all_keys in zip(pairs, peak, total):
            lse[slot, h, :] = top + jnp.log(all_keys)
        for (r, c, _, _), one in zip(pairs, p):
            mixed = dot_tn(v[r, c], one).astype(BF)
            m[r, c] = jnp.concatenate([mixed[:HD, :PACK], mixed[HD:, PACK:]], 0).T

    loop(SLOTS // slots, step, 4)


def attention_backward(meta, q, k, v, lse, dm, dq, dk, dv, key_segments):
    low, high = lane_masks()
    pick = low_lanes()
    scale = HD**-0.5

    def step(i):
        pairs = pairs_of(meta, i, 1, key_segments)
        qs = [two_heads(q[r, c], low * scale, high * scale) for r, c, _, _ in pairs]
        s = [dot_nt(k[r, c], one) for (r, c, _, _), one in zip(pairs, qs)]
        dms = [two_heads(dm[r, c], low, high) for r, c, _, _ in pairs]
        dp = [dot_nt(v[r, c], one) for (r, c, _, _), one in zip(pairs, dms)]
        p = [
            jnp.exp(jnp.where(mask, one, masked_score) - lse[slot, h, :])
            for (_, _, mask, (slot, h)), one in zip(pairs, s)
        ]
        for (r, c, _, _), one, grad in zip(pairs, p, dms):
            dv[r, c] = dot(one.astype(BF), grad).astype(BF)
        ds = [
            (one * (grad - jnp.sum(one * grad, 0, keepdims=True))).astype(BF) for one, grad in zip(p, dp)
        ]
        for (r, c, _, _), one, two in zip(pairs, ds, qs):
            dk[r, c] = dot(one, two).astype(BF)
        for (r, c, _, _), one in zip(pairs, ds):
            both = dot_tn(one, k[r, c])
            dq[r, c] = (jnp.where(pick, both[:PACK], both[PACK:]) * scale).astype(BF)

    loop(SLOTS, step, 4)


ROWS_BF = (TOK, D)
TOTALS = (SLOTS, 8, 2 * PACK)


def full(dtype=BF):
    return sds((TOK, D), dtype)


def attention_layers_body(*refs):
    meta, tok_own, tok_oth, enc_own, enc_oth = refs[:5]
    pieces = refs[5:13]
    m2, lse1, lse2, norm = refs[13:17]
    q1_far, k1_far, v1_far, m1_far, n_far, r_far, q2_far, k2_far, v2_far = refs[17:26]
    w, x, enc, q1, k1, v1, m1, h, q2, k2, v2, n_ref, r_ref, x_sem, enc_sem, w_sem, out_sem = refs[26:]
    loads = load_rows(meta, tok_own, tok_oth, x, x_sem)
    loads += load_weights(meta, pieces, w, w_sem.at[0], 0, 3)
    rest = load_weights(meta, pieces, w, w_sem.at[1], 3)
    rest += load_rows(meta, enc_own, enc_oth, enc, enc_sem)
    wait(loads)
    outs = Copies(out_sem)
    q1[...] = dot(x[...], w[0]).astype(BF)
    k1[...] = dot(x[...], w[1]).astype(BF)
    v1[...] = dot(x[...], w[2]).astype(BF)
    flying = [outs.start(q1, q1_far), outs.start(k1, k1_far), outs.start(v1, v1_far)]
    attention_forward(meta, q1, k1, v1, lse1, m1, target_segments)
    flying.append(outs.start(m1, m1_far))
    wait(rest)
    lane = lax.broadcasted_iota(jnp.int32, (8, HALF), 1) // CH
    for half in range(2):
        total = jnp.zeros((8, HALF), F32)
        for j in range(PIECES // 2):
            at = (half * (PIECES // 2) + j) * CH
            part = w[7, at : at + 16, :HALF][:8].astype(F32)
            total = total + jnp.where(lane == j, part, 0.0)
        norm[:, half * HALF : (half + 1) * HALF] = total
    k2[...] = dot(enc[...], w[5]).astype(BF)
    v2[...] = dot(enc[...], w[6]).astype(BF)

    def step(i):
        rows = block(i, BLK)
        n, rstd = norm_forward(x[rows, :].astype(F32) + dot_nt(m1[rows, :], w[3]))
        n_ref[rows, :] = n
        r_ref[rows, :] = jnp.broadcast_to(rstd, (BLK, PACK))
        h[rows, :] = (n * norm[0:1, :] + norm[3:4, :]).astype(BF)

    loop(TOK // BLK, step)
    q2[...] = dot(h[...], w[4]).astype(BF)
    flying += [
        outs.start(src, dst)
        for src, dst in ((k2, k2_far), (v2, v2_far), (q2, q2_far), (n_ref, n_far), (r_ref, r_far))
    ]
    attention_forward(meta, q2, k2, v2, lse2, m2, source_segments_of)
    wait(flying)


def attention_layers(meta, rows, pieces, deps=()):
    one = pltpu.VMEM(ROWS_BF, BF)
    return call(
        attention_layers_body,
        (full(), sds(TOTALS, F32), sds(TOTALS, F32), sds((8, D), F32)),
        (meta,),
        rows + tuple(pieces),
        (full(),) * 4 + (full(F32), sds((TOK, PACK), F32)) + (full(),) * 3,
        deps=deps,
        scratch=[pltpu.VMEM((pieces[0].shape[1], D, D), BF)]
        + [one] * 10
        + [pltpu.VMEM((TOK, D), F32), pltpu.VMEM((TOK, PACK), F32), sems(2), sems(2), pltpu.SemaphoreType.DMA((2, 8)), sems(9)],
        us=15,
        mb=48,
    )


def gelu_both(v):
    c = math.sqrt(2.0 / math.pi)
    v2 = v * v
    t = jnp.tanh(c * (v + 0.044715 * (v * v2)))
    cdf = 0.5 + 0.5 * t
    return v * cdf, cdf + (0.5 * v) * (1.0 - t * t) * (c + (3.0 * 0.044715 * c) * v2)


def put_grad(g_own, g_oth, m, value):
    value = value.astype(BF)
    g_own[:, m] = value[:, :HALF].reshape(PIECES, CH, HALF)
    g_oth[:, m] = value[:, HALF:].reshape(PIECES, CH, HALF)


def ffn_forward_body(*refs):
    meta, m2, norm, n_far = refs[:4]
    pieces = refs[4:12]
    out_own, out_oth, w, act_ref, slope_ref, n2_ref, n3_ref, r_ref, m_far, po_far, n1, sem, out_sem, in_sem = refs[12:]
    blocks = (w.shape[0] - 1) // 2
    outs = Copies(out_sem)
    flying = [outs.start(m2, m_far)]
    loading = Copies(in_sem).start(n_far, n1)
    wait(load_weights(meta, pieces, w, sem))
    loading.wait()
    flying.append(outs.start(w.at[0], po_far))

    def step(i):
        rows = block(i, BLK)
        h1 = n1[rows, :] * norm[0:1, :] + norm[3:4, :]
        n2, rstd2 = norm_forward(h1 + dot_nt(m2[rows, :], w[0]))
        n2_ref[rows, :] = n2
        h2 = n2 * norm[1:2, :] + norm[4:5, :]
        h2b = h2.astype(BF)
        r3 = h2
        pre = dot(h2b, w[1])
        for b in range(blocks):
            now = pre
            if b + 1 < blocks:
                pre = dot(h2b, w[2 + b])
            act, slope = gelu_both(now)
            act = act.astype(BF)
            act_ref[b, rows, :] = act
            slope_ref[b, rows, :] = slope.astype(BF)
            r3 = r3 + dot_nt(act, w[1 + blocks + b])
        n3, rstd3 = norm_forward(r3)
        n3_ref[rows, :] = n3
        r_ref[rows, :] = jnp.where(low_lanes(BLK), rstd2, rstd3)
        result = n3 * norm[2:3, :] + norm[5:6, :]
        out_own[rows, :], out_oth[rows, :] = halves(meta, result.astype(BF))

    loop(TOK // BLK, step)
    wait(flying)


def ffn_forward(meta, n1_far, m2, norm, pieces):
    mats = pieces[0].shape[1]
    hidden = sds(((mats - 1) // 2, TOK, D))
    return call(
        ffn_forward_body,
        (sds((TOK, HALF)), sds((TOK, HALF)), sds((mats, D, D)), hidden, hidden)
        + (full(F32), full(F32), sds((TOK, PACK), F32)),
        (meta, m2, norm),
        (n1_far,) + tuple(pieces),
        (full(), sds((D, D))),
        scratch=[pltpu.VMEM((TOK, D), F32), sems(8), sems(2), sems(1)],
        us=9,
        mb=24,
    )


def ffn_backward_body(*refs):
    meta, norm, w, act_ref, slope_ref, n2_ref, n3_ref, r_ref, cot_own, cot_oth = refs[:10]
    g_own, g_oth, ng, dr_far = refs[10:14]
    cot, pre_ref, df_ref, h_ref, dr_ref, sem, out_sem = refs[14:]
    blocks = (w.shape[0] - 1) // 2
    mine = block(meta[CORE], TOK)
    loads = Copies(sem)
    wait(
        [
            loads.start(src.at[mine], cot.at[:, block(at, HALF)])
            for src, at in ((cot_own, meta[CORE]), (cot_oth, 1 - meta[CORE]))
        ]
    )
    ng[...] = jnp.zeros_like(ng)

    def step(i):
        rows = block(i, BLK)
        dy = cot[rows, :].astype(F32)
        dr3, gain3, bias3 = norm_backward(dy, n3_ref[rows, :], r_ref[rows, HD : HD + 1], norm[2:3, :])
        df = dr3.astype(BF)
        df_ref[rows, :] = df
        dh2 = dr3
        for b in range(blocks):
            dpre = (dot(df, w[1 + blocks + b]) * slope_ref[b, rows, :].astype(F32)).astype(BF)
            pre_ref[b, rows, :] = dpre
            dh2 = dh2 + dot_nt(dpre, w[1 + b])
        n2 = n2_ref[rows, :]
        h_ref[rows, :] = (n2 * norm[1:2, :] + norm[4:5, :]).astype(BF)
        dr2, gain2, bias2 = norm_backward(dh2, n2, r_ref[rows, 0:1], norm[1:2, :])
        dr_ref[rows, :] = dr2
        ng[1:2, :] += gain2
        ng[2:3, :] += gain3
        ng[4:5, :] += bias2
        ng[5:6, :] += bias3

    loop(TOK // BLK, step)
    flying = Copies(out_sem).start(dr_ref, dr_far)
    h_t = h_ref[...].T
    for b in range(blocks):
        put_grad(g_own, g_oth, b, dot(h_t, pre_ref[b]))
    df_t = df_ref[...].T
    for b in range(blocks):
        put_grad(g_own, g_oth, blocks + b, dot(df_t, act_ref[b]))
    flying.wait()


def ffn_backward(meta, norm, w, act, slope, n2, n3, rstd, cot_own, cot_oth, deps=()):
    blocks = act.shape[0]
    grad = sds((PIECES, 2 * blocks, CH, HALF))
    return call(
        ffn_backward_body,
        (grad, grad, sds((8, D), F32)),
        (meta, norm, w, act, slope, n2, n3, rstd),
        (cot_own, cot_oth),
        (full(F32),),
        deps=deps,
        scratch=[
            pltpu.VMEM(ROWS_BF, BF),
            pltpu.VMEM((blocks, TOK, D), BF),
            pltpu.VMEM(ROWS_BF, BF),
            pltpu.VMEM(ROWS_BF, BF),
            pltpu.VMEM((TOK, D), F32),
            sems(2),
            sems(1),
        ],
        us=14,
        mb=24,
    )


def fetch(sem, pairs):
    copies = Copies(sem)
    started = [copies.start(src, dst) for src, dst in pairs]
    return lambda *at: wait([started[k] for k in at])


def cross_backward_body(*refs):
    meta, norm, ng_in, lse = refs[:4]
    dr_in_far, q_far, k_far, v_far, m_far, n_far, r_far, po_far, enc_own, enc_oth = refs[4:14]
    pieces = refs[14:22]
    dr_ref, g_own, g_oth, ng, dr_far, dk_far, dv_far = refs[22:29]
    q, k, v, m, enc, n, r, w, po, da, dm, dq, dk, dv, h, dr_in, in_sem, out_sem, w_sem, enc_sem = refs[29:]
    ready = fetch(
        in_sem,
        ((po_far, po), (q_far, q), (k_far, k), (v_far, v), (n_far, n), (r_far, r), (m_far, m), (dr_in_far, dr_in)),
    )
    weights = load_weights(meta, pieces, w, w_sem, 4, 1, 0)
    rows_in = load_rows(meta, enc_own, enc_oth, enc, enc_sem)
    outs = Copies(out_sem)
    ready(7)
    da[...] = dr_in[...].astype(BF)
    ready(0)
    dm[...] = dot(da[...], po[...]).astype(BF)
    ready(1, 2, 3)
    attention_backward(meta, q, k, v, lse, dm, dq, dk, dv, source_segments_of)
    flying = [outs.start(dk, dk_far), outs.start(dv, dv_far)]
    ng[...] = ng_in[...]
    ready(4, 5)
    wait(weights)

    def step(i):
        rows = block(i, BLK)
        normed = n[rows, :]
        h[rows, :] = (normed * norm[0:1, :] + norm[3:4, :]).astype(BF)
        dh1 = dr_in[rows, :] + dot_nt(dq[rows, :], w[0])
        dr1, gain1, bias1 = norm_backward(dh1, normed, r[rows, 0:1], norm[0:1, :])
        dr_ref[rows, :] = dr1
        ng[0:1, :] += gain1
        ng[3:4, :] += bias1

    loop(TOK // BLK, step)
    flying.append(outs.start(dr_ref, dr_far))
    ready(6)
    wait(rows_in)
    put_grad(g_own, g_oth, 0, dot_tn(da[...], m[...]))
    put_grad(g_own, g_oth, 1, dot_tn(h[...], dq[...]))
    put_grad(g_own, g_oth, 2, dot_tn(enc[...], dk[...]))
    put_grad(g_own, g_oth, 3, dot_tn(enc[...], dv[...]))
    total = jnp.concatenate([ng[...], jnp.zeros((CH - 8, D), F32)], 0).astype(BF)
    for c in range(PIECES):
        part = total[:, :HALF] if c < PIECES // 2 else total[:, HALF:]
        g_own[c, 4] = part
        g_oth[c, 4] = part
    wait(flying)


def cross_backward(meta, dr2, norm, ng, lse, saved, pieces, deps=()):
    grad = sds((PIECES, 5, CH, HALF))
    rows = pltpu.VMEM(ROWS_BF, BF)
    return call(
        cross_backward_body,
        (full(F32), grad, grad, sds((8, D), F32)),
        (meta, norm, ng, lse),
        (dr2,) + saved + tuple(pieces),
        (full(F32), full(), full()),
        deps,
        [rows] * 5
        + [pltpu.VMEM((TOK, D), F32), pltpu.VMEM((TOK, PACK), F32), pltpu.VMEM((1, D, D), BF), pltpu.VMEM((D, D), BF)]
        + [rows] * 6
        + [pltpu.VMEM((TOK, D), F32), sems(8), sems(3), sems(8), sems(2)],
        us=12,
        mb=46,
    )


def self_backward_body(*refs):
    meta, dr_in, lse = refs[:3]
    q_far, k_far, v_far, m_far, tok_own, tok_oth = refs[3:9]
    pieces = refs[9:17]
    g_own, g_oth, dq_far, dk_far, dv_far, q, k, v, m, x, w, da, dm, dq, dk, dv, in_sem, w_sem, x_sem, out_sem = refs[17:]
    weights = load_weights(meta, pieces, w, w_sem, 3, 1, 0)
    ready = fetch(in_sem, ((q_far, q), (k_far, k), (v_far, v), (m_far, m)))
    rows_in = load_rows(meta, tok_own, tok_oth, x, x_sem)
    da[...] = dr_in[...].astype(BF)
    wait(weights)
    dm[...] = dot(da[...], w[0]).astype(BF)
    ready(0, 1, 2)
    attention_backward(meta, q, k, v, lse, dm, dq, dk, dv, target_segments)
    outs = Copies(out_sem)
    flying = [outs.start(dq, dq_far), outs.start(dk, dk_far), outs.start(dv, dv_far)]
    ready(3)
    wait(rows_in)
    put_grad(g_own, g_oth, 0, dot_tn(da[...], m[...]))
    put_grad(g_own, g_oth, 1, dot_tn(x[...], dq[...]))
    put_grad(g_own, g_oth, 2, dot_tn(x[...], dk[...]))
    put_grad(g_own, g_oth, 3, dot_tn(x[...], dv[...]))
    wait(flying)


def self_backward(meta, dr1, lse, saved, pieces, deps=()):
    grad = sds((PIECES, 4, CH, HALF))
    rows = pltpu.VMEM(ROWS_BF, BF)
    return call(
        self_backward_body,
        (grad, grad),
        (meta, dr1, lse),
        saved + tuple(pieces),
        (full(), full(), full()),
        deps,
        [rows] * 5 + [pltpu.VMEM((1, D, D), BF)] + [rows] * 5 + [sems(4), sems(8), sems(2), sems(3)],
        us=10,
        mb=46,
    )


def inputs_backward_body(*refs):
    meta = refs[0]
    pieces = refs[7:15]
    x_own, x_oth, e_own, e_oth, dr, dq, dk, dv, dk2, dv2, w, w2, in_sem, w_sem, w2_sem = refs[15:]
    ready = fetch(in_sem, tuple(zip(refs[1:7], (dr, dq, dk, dv, dk2, dv2))))
    weights = load_weights(meta, pieces, w, w_sem, 0, 3) + load_weights(meta, pieces, w2, w2_sem, 5, 2, 0)
    wait(weights)
    ready(*range(6))

    def step(i):
        rows = block(i, BLK)
        dx = dr[rows, :] + dot_nt(dq[rows, :], w[0]) + dot_nt(dk[rows, :], w[1]) + dot_nt(dv[rows, :], w[2])
        x_own[rows, :], x_oth[rows, :] = halves(meta, dx.astype(BF))
        de = dot_nt(dk2[rows, :], w2[0]) + dot_nt(dv2[rows, :], w2[1])
        e_own[rows, :], e_oth[rows, :] = halves(meta, de.astype(BF))

    loop(TOK // BLK, step)


def inputs_backward(meta, saved, pieces, deps=()):
    rows = pltpu.VMEM(ROWS_BF, BF)
    return call(
        inputs_backward_body,
        (sds((TOK, HALF)),) * 4,
        (meta,),
        saved + tuple(pieces),
        (),
        deps,
        [pltpu.VMEM((TOK, D), F32)] + [rows] * 5 + [pltpu.VMEM((3, D, D), BF), pltpu.VMEM((2, D, D), BF)]
        + [sems(6), sems(8), sems(8)],
        us=5,
        mb=46,
    )


def place_body(meta, own, oth, out):
    for side, src in enumerate((own, oth)):
        for j in range(SLOTS):
            out[block(meta[ROW + SLOTS * side + j], PACK), :] = src[j * PACK : (j + 1) * PACK, :]


def count_body(far, out, seg, sem):
    Copies(sem).start(far, seg).wait()
    first = jnp.where(seg[...] == 0, 1.0, 0.0).astype(BF)
    out[...] = dot_nt(jnp.ones((8, PACK), BF), first)


def join_body(meta, own, oth, out):
    out[block(meta[CORE], TOK), :] = own[...]
    out[block(1 - meta[CORE], TOK), :] = oth[...]


def copy_body(src, out):
    out[...] = src[...]


def copy_after(value, deps):
    return call(copy_body, (sds(value.shape),), (value,), deps=deps)[0]


BOTH = (2 * TOK, HALF)


def add(a, b):
    return (a.astype(F32) + b.astype(F32)).astype(BF)


def pair_sum_body(meta, own, rec, *outs):
    for k in range(4):
        for j in range(4):
            c = meta[PIECE + 4 * k + j]
            if k < 2:
                outs[k][j] = add(own[c], rec[c])
            else:
                outs[2][k - 2, j] = add(own[c], rec[c])


def pair_sum(meta, own, rec):
    shape = (4,) + own.shape[1:]
    return call(pair_sum_body, (sds(shape), sds(shape), sds((2,) + shape)), (meta, own, rec))


def stage_sum_body(a0, a1, b, keep, send):
    keep[...] = add(a0[...], b[0])
    send[...] = add(a1[...], b[1])


def last_line_body(at, a, b, *outs):
    for j in range(4):
        k = at[0] ^ j
        outs[j][...] = add(a[k], b[k])


def tail_sum_body(at, kc, rc, ks, rs, *outs):
    mats = kc.shape[1]
    for j in range(4):
        k = at[0] ^ j
        outs[j][:mats] = add(kc[k], rc[k])
        outs[j][mats:] = add(ks[k], rs[k])


def adam_attention_body(*refs):
    parts, state, outs = refs[:4], refs[4:10], refs[10:]
    total = [ref[...].astype(F32) for ref in parts]
    g = (total[0] + total[1]) + (total[2] + total[3])
    grads = (jnp.concatenate([g[6:9], g[1:4]], 0), jnp.concatenate([g[5:6], g[0:1]], 0))
    for k, grad in enumerate(grads):
        weight, first, second = (ref[...] for ref in state[3 * k : 3 * k + 3])
        outs[3 * k][...], outs[3 * k + 1][...], outs[3 * k + 2][...] = adam(
            weight, first, second, grad, rate_matrix, decay_matrix
        )
    outs[6][...] = g[4, :8]


def adam_ffn_body(z, *refs):
    state, outs = refs[:6], refs[6:]
    g = (z[0].astype(F32) + z[1].astype(F32)) + (z[2].astype(F32) + z[3].astype(F32))
    blocks = g.shape[0] // 2
    for k in range(2):
        for b in range(blocks):
            cols = slice(b * HALF, (b + 1) * HALF)
            weight, first, second = (ref[:, cols] for ref in state[3 * k : 3 * k + 3])
            outs[3 * k][:, cols], outs[3 * k + 1][:, cols], outs[3 * k + 2][:, cols] = adam(
                weight, first, second, g[k * blocks + b], rate_matrix, decay_matrix
            )


def adam(weight, first_old, second_old, grad, rate, decay):
    first_new = beta_first * first_old + (1.0 - beta_first) * grad
    second_new = beta_second * second_old + (1.0 - beta_second) * grad * grad
    first_hat = first_new / (1.0 - beta_first**STEP)
    second_hat = second_new / (1.0 - beta_second**STEP)
    updated = weight - rate * (first_hat / (jnp.sqrt(second_hat) + adam_epsilon) + decay * weight)
    return (first_new, second_new, updated)


def swap(value):
    return lax.ppermute(value, "narrow", [(0, 1), (1, 0)])


def peer(value, mask, mask_one=None):
    masks = (mask, mask if mask_one is None else mask_one)
    chips = lax.axis_size("wide")
    route = [(2 * i + c, 2 * (i ^ masks[c]) + c) for i in range(chips) for c in range(2)]
    return lax.ppermute(value, ("wide", "narrow"), route)


def along_z(parts):
    plane = lax.axis_size("wide") // 4
    lines = [[at + plane * j for j in range(4)] for at in range(plane)]
    return lax.all_to_all(parts, "wide", 0, 0, axis_index_groups=lines)


def local(
    tokens,
    encoded,
    cotangent,
    target_lengths,
    source_segments,
    send_rows,
    proj_in,
    proj_out,
    ffn_in,
    ffn_out,
    norm_par,
    proj_in_moment,
    proj_in_square,
    proj_out_moment,
    proj_out_square,
    ffn_in_moment,
    ffn_in_square,
    ffn_out_moment,
    ffn_out_square,
    norm_moment,
    norm_square,
):
    wide_count = lax.axis_size("wide")
    w = lax.axis_index("wide")
    n = lax.axis_index("narrow")
    rows_dev = tokens.shape[0] // PACK
    stride = wide_count // rows_dev
    share = proj_in.shape[1]
    blocks = ffn_in.shape[1] // HALF
    direct = share == CH

    places = jnp.arange(rows_dev, dtype=jnp.int32)
    slot_rows = lax.dynamic_index_in_dim(send_rows, w, 0, keepdims=False)[places * stride + w % stride]
    mine = lax.dynamic_slice_in_dim(slot_rows, n * SLOTS, SLOTS)
    theirs = lax.dynamic_slice_in_dim(slot_rows, (1 - n) * SLOTS, SLOTS)
    mine_global = w * rows_dev + mine
    lengths = target_lengths[mine_global]
    if direct:
        orders = jnp.array([[a for a in order for _ in range(4)] for order in ((0, 1, 2, 3), (0, 2, 1, 3))])
        in_plane = jnp.concatenate([orders[n], orders[1 - n]]) ^ (w % 4)
        piece_ids = in_plane + 4 * (jnp.arange(2 * PIECES, dtype=jnp.int32) % 4)
    else:
        piece_ids = jnp.tile(jnp.arange(PIECES, dtype=jnp.int32), 2)
    counts = call(
        count_body,
        (sds((8, source_segments.shape[0]), F32),),
        (),
        (source_segments,),
        scratch=[pltpu.VMEM(source_segments.shape, jnp.int32), sems(1)],
        mb=56,
    )[0]
    cut = counts[0][mine_global].astype(jnp.int32)
    meta = jnp.concatenate(
        [n[None], piece_ids, mine, theirs, lengths[:, 0], lengths[:, 0] + lengths[:, 1], cut]
    ).astype(jnp.int32)

    tok_rows = (tokens, swap(tokens))
    enc_rows = (encoded, swap(encoded))
    pout_t = proj_out.transpose(0, 2, 1)
    wout_t = ffn_out.T
    out_moment, out_square = proj_out_moment.transpose(0, 2, 1), proj_out_square.transpose(0, 2, 1)

    if direct:
        g0 = call(
            pack_attention_body,
            (sds((8, CH, HALF)),),
            (),
            (proj_in, pout_t, norm_par),
            scratch=[pltpu.VMEM(a, F32) for a in (proj_in.shape, (CH, HALF), norm_par.shape)] + [sems(3)],
            us=2,
        )[0]
        line = [peer(g0, 4 * k) for k in (1, 2, 3)]
        z0 = call(
            stack_body,
            (sds((4, 8, CH, HALF)),),
            ((w // 4)[None], g0, *line),
            deps=(meta, tok_rows[1], enc_rows[1]),
        )[0]
        first0 = peer(z0, 1, 2)
        second0 = peer(z0, 2, 1)
        g1 = call(
            pack_ffn_body,
            (sds((4, 1 + 2 * blocks, CH, HALF)),),
            (pout_t, ffn_in, wout_t),
            deps=(z0,),
            us=2,
        )[0]
        z1 = along_z(g1)
        third0 = peer(copy_after(first0, (z1, second0)), 2, 1)
        pieces0 = [z0, first0, second0, third0]
        first1 = peer(z1, 1, 2)
        second1 = peer(z1, 2, 1)
        pieces1 = [z1, first1, second1]
        pieces = [own + [swap(a) for a in own] for own in (pieces0, pieces1)]
        cotangent = copy_after(cotangent, (third0,))
    else:
        low_in = lax.all_gather(proj_in.astype(BF), "wide", axis=1, tiled=True)
        low_out = lax.all_gather(proj_out.astype(BF), "wide", axis=2, tiled=True).transpose(0, 2, 1)
        low_win = lax.all_gather(ffn_in.astype(BF), "wide", axis=0, tiled=True)
        low_wout = lax.all_gather(ffn_out.astype(BF), "wide", axis=1, tiled=True).T
        low_norm = lax.all_gather(norm_par.astype(BF), "wide", axis=1, tiled=True)

        def column_blocks(a):
            return a.reshape(D, blocks, HALF).transpose(1, 0, 2)

        tiled = jnp.tile(low_norm.reshape(6, PIECES, CH).transpose(1, 0, 2), (1, 1, HALF // CH))
        norm_mat = jnp.pad(tiled, ((0, 0), (0, CH - 6), (0, 0))).reshape(1, D, HALF)
        groups = (
            jnp.concatenate([low_in[:3], low_out[:1], low_in[3:], norm_mat]),
            jnp.concatenate([low_out[1:], column_blocks(low_win), column_blocks(low_wout)]),
        )
        pieces = []
        for group in groups:
            cut = group.reshape(-1, PIECES, CH, HALF).transpose(1, 0, 2, 3)
            own = [cut[4 * k : 4 * k + 4] for k in range(4)]
            pieces.append(own + [swap(a) for a in own])

    everyone = [[r + stride * j for j in range(rows_dev)] for r in range(stride)]

    def exchange(rows):
        return lax.all_to_all(
            rows.reshape(rows_dev, PACK, HALF), "wide", 0, 0, axis_index_groups=everyone
        ).reshape(rows_dev * PACK, HALF)

    cot_own = exchange(cotangent)
    cot_oth = swap(cot_own)
    m2, lse1, lse2, norm, q1, k1, v1, m1, n1, rstd1, q2, k2, v2 = attention_layers(
        meta, tok_rows + enc_rows, pieces[0]
    )
    if direct:
        third1 = peer(copy_after(first1, (lse2, second1)), 2, 1)
        pieces[1] = pieces[1][:3] + [third1] + pieces[1][3:] + [swap(third1)]
    out_own, out_oth, w_ffn, act, slope, n2, n3, rstd, m2_far, po2 = ffn_forward(meta, n1, m2, norm, pieces[1])
    joined = call(join_body, (sds(BOTH),), (meta, out_own, swap(out_oth)))[0]
    gf_own, gf_oth, ng, dr2 = ffn_backward(
        meta, norm, w_ffn, act, slope, n2, n3, rstd, cot_own, cot_oth, (joined,)
    )
    layer_out = copy_after(exchange(joined), ())
    early = ()
    if direct:
        sf = pair_sum(meta, gf_own, swap(gf_oth))
        early = (sf[2],)
    dr1, gc_own, gc_oth, ng, dr1_far, dk2, dv2 = cross_backward(
        meta, dr2, norm, ng, lse2, (q2, k2, v2, m2_far, n1, rstd1, po2) + enc_rows, pieces[0], early
    )
    if direct:
        kf, send_f = call(stage_sum_body, (sds(sf[0].shape),) * 2, (sf[0], sf[1], peer(sf[2], 2, 1)))
        sc = pair_sum(meta, gc_own, swap(gc_oth))
    gs_own, gs_oth, dq1, dk1, dv1 = self_backward(
        meta, dr1, lse1, (q1, k1, v1, m1) + tok_rows, pieces[0], (send_f,) if direct else ()
    )
    if direct:
        at_z = (w // 4)[None]
        zf = call(last_line_body, (sds(kf.shape[1:]),) * 4, (at_z, kf, peer(send_f, 1, 2)))
        ss = pair_sum(meta, gs_own, swap(copy_after(gs_oth, (zf[1],))))
        zf = jnp.stack([zf[0]] + [peer(zf[k], 4 * k) for k in (1, 2, 3)])
    dx_own, dx_oth, de_own, de_oth = inputs_backward(
        meta, (dr1_far, dq1, dk1, dv1, dk2, dv2), pieces[0], (layer_out,) if direct else ()
    )
    tokens_grad = call(place_body, (sds(BOTH),), (meta, dx_own, swap(dx_oth)))[0]
    encoded_grad = call(place_body, (sds(BOTH),), (meta, de_own, swap(de_oth)))[0]

    if direct:
        kc, send_c = call(
            stage_sum_body, (sds(sc[0].shape),) * 2, (sc[0], sc[1], peer(sc[2], 2, 1)), deps=(dx_own,)
        )
        ks, send_s = call(stage_sum_body, (sds(ss[0].shape),) * 2, (ss[0], ss[1], peer(ss[2], 2, 1)))
        line = call(
            tail_sum_body,
            (sds((kc.shape[1] + ks.shape[1], CH, HALF)),) * 4,
            (at_z, kc, peer(send_c, 1, 2), ks, peer(send_s, 1, 2)),
        )
        line = [line[0]] + [peer(line[k], 4 * k) for k in (1, 2, 3)]
        pairs = ((proj_in, proj_in_moment, proj_in_square), (pout_t, out_moment, out_square))
        wide_pairs = ((ffn_in, ffn_in_moment, ffn_in_square), (wout_t, ffn_out_moment.T, ffn_out_square.T))

        def news(group):
            return tuple(sds(a.shape, F32) for triple in group for a in triple)

        upd = call(adam_ffn_body, news(wide_pairs), (zf,) + wide_pairs[0] + wide_pairs[1], us=2)
        upd_expand, upd_reduce = upd[:3], tuple(u.T for u in upd[3:])
        upd = call(
            adam_attention_body,
            news(pairs) + (sds((8, HALF), F32),),
            tuple(line) + pairs[0] + pairs[1],
            deps=(tokens_grad, encoded_grad, upd[0]),
            us=2,
        )
        upd_in, upd_out = upd[:3], tuple(u.transpose(0, 2, 1) for u in upd[3:6])
        norm_half = upd[6][:6]
        norm_half = jnp.where(n == 0, norm_half, swap(norm_half))
        norm_grad = lax.dynamic_slice_in_dim(norm_half, (w % (HALF // CH)) * CH, CH, 1)
    else:

        def summed(own, oth):
            total = (own.astype(F32) + swap(oth).astype(F32)).astype(BF)
            total = total.transpose(1, 0, 2, 3).reshape(-1, D, HALF)
            return lax.psum_scatter(total, "wide", scatter_dimension=1, tiled=True).astype(F32)

        gf, gc, gs = summed(gf_own, gf_oth), summed(gc_own[:, :4], gc_oth[:, :4]), summed(gs_own, gs_oth)
        norm_all = lax.psum(ng, ("wide", "narrow"))[:6]
        norm_grad = lax.dynamic_slice_in_dim(norm_all, w * share, share, 1)

        grad_in = jnp.concatenate([gs[1:4], gc[1:4]])
        grad_out = jnp.stack([gs[0], gc[0]])
        grad_expand = gf[:blocks].transpose(1, 0, 2).reshape(share, blocks * HALF)
        grad_reduce = gf[blocks:].transpose(1, 0, 2).reshape(share, blocks * HALF)
        upd_in = adam(proj_in, proj_in_moment, proj_in_square, grad_in, rate_matrix, decay_matrix)
        upd_out = adam(pout_t, out_moment, out_square, grad_out, rate_matrix, decay_matrix)
        upd_out = tuple(u.transpose(0, 2, 1) for u in upd_out)
        upd_expand = adam(ffn_in, ffn_in_moment, ffn_in_square, grad_expand, rate_matrix, decay_matrix)
        upd_reduce = adam(
            wout_t, ffn_out_moment.T, ffn_out_square.T, grad_reduce, rate_matrix, decay_matrix
        )
        upd_reduce = tuple(u.T for u in upd_reduce)
    upd_norm = adam(norm_par, norm_moment, norm_square, norm_grad, rate_norm, 0.0)
    return (layer_out, tokens_grad, encoded_grad) + upd_in + upd_out + upd_expand + upd_reduce + upd_norm


def solution(mesh):
    rows = P("wide", "narrow")
    p_in = P(None, "wide", "narrow")
    p_out = P(None, "narrow", "wide")
    p_expand = P("wide", "narrow")
    p_reduce = P("narrow", "wide")
    p_norm = P(None, "wide")
    weights = (p_in, p_out, p_expand, p_reduce, p_norm)
    in_specs = (rows,) * 3 + (P(),) * 3 + weights + tuple(s for s in weights for _ in range(2))
    out_specs = (rows,) * 3 + tuple(s for s in weights for _ in range(3))
    return jax.shard_map(local, mesh=mesh, in_specs=in_specs, out_specs=out_specs, check_vma=False)
```
